32 devices in a mesh: groups: 2 (over y), wide: 4 (over z), narrow: 2 (over x), pair: 2 (over core).
Axes of the slice: x: 2, y: 2, z: 4, core: 2. Of those that a mesh axis runs over, the one named last changes fastest.
Arguments:
- row_codes: bfloat16 [256, 7168], P(('groups', 'wide', 'narrow', 'pair')), parts along dimension 0, may hold values from -448 to 448
- row_scales: bfloat16 [256, 56], P(('groups', 'wide', 'narrow', 'pair')), parts along dimension 0, may hold values from 0.0039978027 to 0.039794922
- expert_ids: int32 [256, 2], P(('groups', 'wide', 'narrow', 'pair')), parts along dimension 0, may hold values from 0 to 3, all different within a row; in each aligned block of 8 rows (0 to 7, 8 to 15, ...) at most 5 rows name the same one
- gate_weights: float32 [256, 2], P(('groups', 'wide', 'narrow', 'pair')), parts along dimension 0, may hold values from 0.1 to 0.5
- placement: int32 [4], replicated, may hold values from 0 to 3, as said below
- w_gate: bfloat16 [4, 7168, 1024], P('wide', None, ('narrow', 'pair')), may hold values from -0.0625 to 0.0625
- w_up: bfloat16 [4, 7168, 1024], P('wide', None, ('narrow', 'pair')), may hold values from -0.0625 to 0.0625
- w_down: bfloat16 [4, 1024, 7168], P('wide', ('narrow', 'pair')), may hold values from -0.1875 to 0.1875
- shared_gate: bfloat16 [7168, 1024], P(None, ('narrow', 'pair')), may hold values from -0.0625 to 0.0625
- shared_up: bfloat16 [7168, 1024], P(None, ('narrow', 'pair')), may hold values from -0.0625 to 0.0625
- shared_down: bfloat16 [1024, 7168], P(('narrow', 'pair')), may hold values from -0.1875 to 0.1875
Outputs:
- layer_out: bfloat16 [256, 7168], P(('groups', 'wide', 'narrow', 'pair')), parts along dimension 0
The draws below stay inside these ranges and needn't reach their ends.
There are 2 independent parts, one for each index of `groups`. The reference program is written for one: setup_inputs(seed, part) draws one part's arguments, and reference() takes and returns one part's arrays. A program takes and returns all parts, laid end to end along the dimension named above; an argument that names none is the same for every part. Nothing has to cross between parts.
Inputs may be any that keep to these rules, and one draw needn't show every extreme that they name: `expert_ids`: each row names 2 different experts. Among the rows of one device no expert is named by more than 5 rows, and in every draw some device names some expert exactly 5 times. `placement`: each storage index is used by exactly one expert.
All inputs are finite; a program needn't handle non-finite values.
Results may differ from the reference program's by a relative error of at most 0.012.
Values may be sent and summed in bfloat16 or wider, within the bound.
No kernel may reach another device: no remote copies, remote signals or barrier semaphores. Data moves between devices by JAX's collectives and lax.ppermute only.
A program may use at most 128 MiB of HBM per device.

```python
import math
import jax
import jax.numpy as jnp
import numpy as np
from jax import lax

D = 7168
FF_W = 1024
TOK_DEV = 8
CAP = 5
EXPERTS = 4
TOPK = 2
TOKENS = 128
N_WIDE = 4
N_NARROW = 2
N_PAIR = 2


def draw_placement(key, part):
    key = jax.random.fold_in(key, 7919)
    return jax.random.permutation(key, jnp.arange(EXPERTS, dtype=jnp.int32)).astype(jnp.int32)


def steps_of(stream_key, dims, shards, least, top_value):
    gain = 1.0
    for dim, parts in shards:
        heights = jax.random.uniform(jax.random.fold_in(jax.random.fold_in(stream_key, 6), dim), (parts,), jnp.float32, least / len(shards), top_value / len(shards))
        gain = gain * jnp.repeat(jnp.exp(heights), dims[dim] // parts).reshape((-1,) + (1,) * (len(dims) - 1 - dim))
    return gain


def assign_block(key, own, number, rows, number_of, top, most, lean):
    order = jax.random.permutation(key, number_of)
    crowded, common = load_shares(number_of, rows * top, most, lean, True), load_shares(number_of, rows * top, most, lean, False)
    places = jnp.arange(number_of)

    def named(sizes, rotation):
        used = int((sizes > 0).sum())
        fixed = max(1, used // 4)
        shifted = fixed + (places - fixed + rotation * (used - fixed)) % max(1, number_of - fixed)
        return jnp.zeros((number_of,), jnp.int32).at[order[jnp.where(places < fixed, places, shifted)]].set(jnp.asarray(sizes, jnp.int32))

    sizes = jnp.where(number % 4 == 0, named(crowded, number // 4), named(common, number - number // 4 - 1))
    mixed = jax.random.permutation(jax.random.fold_in(own, 3), number_of)
    source_of, taker = mixed[0:number_of // 2 * 2:2], mixed[1:number_of // 2 * 2:2]
    margin = jnp.minimum(sizes[source_of] - 1, most - sizes[taker]) // 2
    margin = jnp.where((source_of == order[0]) | (taker == order[0]) | (sizes[taker] == 0), 0, jnp.maximum(margin, 0))
    shifted = jax.random.randint(jax.random.fold_in(own, 4), (number_of // 2,), 0, 1 << 20) % (margin + 1)
    sizes = sizes.at[source_of].add(-shifted).at[taker].add(shifted)
    items = jnp.searchsorted(jnp.cumsum(sizes), jnp.arange(rows * top), side="right").astype(jnp.int32)
    listing = items.reshape(top, rows).T
    listing = listing[jax.random.permutation(jax.random.fold_in(own, 1), rows)]
    rotation = jax.random.randint(jax.random.fold_in(own, 2), (rows, 1), 0, top)
    return jnp.take_along_axis(listing, (jnp.arange(top)[None, :] + rotation) % top, axis=1)


def load_shares(count, total, most, lean, full):
    loads = [(1 << 20) // math.isqrt(rank ** lean) + 1 for rank in range(1, count + 1)]
    largest = most if full else min(most, max(-(-total // count), total * loads[0] // sum(loads)))
    least = 1 if total - largest >= count - 1 else 0
    holding, spare = [largest] + [least] * (count - 1), total - largest - least * (count - 1)
    while spare > 0:
        movable = [i for i in range(1, count) if holding[i] < largest] or [i for i in range(1, count) if holding[i] < most]
        whole, budget = sum([loads[i] for i in movable]), spare
        for i in movable:
            extra = min(most - holding[i], max(1, budget * loads[i] // whole), spare)
            holding[i] = holding[i] + extra
            spare = spare - extra
    return np.array(holding)


def centred(own_key, dims, width, limit, split=(), kind=jnp.bfloat16):
    level = steps_of(own_key, dims, split, -0.22, 0.18) if split else 1.0
    drawn = jax.random.normal(own_key, dims, jnp.float32) * width * level
    return jnp.minimum(jnp.maximum(drawn, -limit), limit).astype(kind)


def setup_inputs(seed: int = 0, part: int = 0) -> dict:
    keys = jax.random.split(jax.random.key(seed), 12)
    own_keys = jax.random.split(jax.random.fold_in(keys[11], part), 12)
    row_codes = centred(own_keys[0], (TOKENS, D), 64.0, 448.0, ((0, 16),))
    row_scales = jnp.clip(jnp.exp(math.log(0.039794922) - 2.2979944 * jax.random.uniform(own_keys[1], (TOKENS, D // 128), jnp.float32) ** steps_of(own_keys[1], (TOKENS, D // 128), ((0, 16),), -0.2, 0.2)), 0.0039978027, 0.039794922).astype(jnp.bfloat16)
    expert_ids_keys = jax.random.split(jax.random.fold_in(own_keys[2], 1), TOKENS // TOK_DEV)
    expert_ids_turns = jax.random.permutation(jax.random.fold_in(own_keys[2], 3), TOKENS // TOK_DEV)
    expert_ids = jax.vmap(lambda own, number: assign_block(jax.random.fold_in(own_keys[2], 2), own, number, TOK_DEV, EXPERTS, TOPK, CAP, 2))(expert_ids_keys, expert_ids_turns).reshape((TOKENS, TOPK))
    gate_weights = jnp.clip(0.1 + 0.4 * jax.random.uniform(own_keys[3], (TOKENS, TOPK), jnp.float32) ** steps_of(own_keys[3], (TOKENS, TOPK), ((0, 16),), -0.2, 0.2), 0.1, 0.5)
    placement = draw_placement(jax.random.fold_in(keys[11], 71), part)
    w_gate = centred(keys[5], (EXPERTS, D, FF_W), D ** -0.5, 0.0625, ((0, 4), (2, 4)))
    w_up = centred(keys[6], (EXPERTS, D, FF_W), D ** -0.5, 0.0625, ((0, 4), (2, 4)))
    w_down = centred(keys[7], (EXPERTS, FF_W, D), FF_W ** -0.5, 0.1875, ((0, 4), (1, 4)))
    shared_gate = centred(keys[8], (D, FF_W), D ** -0.5, 0.0625, ((1, 4),))
    shared_up = centred(keys[9], (D, FF_W), D ** -0.5, 0.0625, ((1, 4),))
    shared_down = centred(keys[10], (FF_W, D), FF_W ** -0.5, 0.1875, ((0, 4),))
    return {"row_codes": row_codes, "row_scales": row_scales, "expert_ids": expert_ids, "gate_weights": gate_weights, "placement": placement, "w_gate": w_gate, "w_up": w_up, "w_down": w_down, "shared_gate": shared_gate, "shared_up": shared_up, "shared_down": shared_down}


def dequantize(codes, scales):
    row_total, feature_width = codes.shape
    blocks = codes.astype(jnp.float32).reshape(row_total, feature_width // 128, 128) * scales.astype(jnp.float32)[:, :, None]
    return blocks.reshape(row_total, feature_width).astype(jnp.bfloat16)


def grouped_expert(inputs, gate_proj, up_proj, down_proj):
    gate_act = jnp.dot(inputs, gate_proj, preferred_element_type=jnp.float32)
    up_act = jnp.dot(inputs, up_proj, preferred_element_type=jnp.float32)
    hidden = (jax.nn.silu(gate_act) * up_act).astype(jnp.bfloat16)
    group_count = N_NARROW * N_PAIR
    group_width = gate_proj.shape[1] // group_count

    def one_group(running, group):
        first = (group * group_width).astype(jnp.int32)
        hidden_part = lax.dynamic_slice_in_dim(hidden, first, group_width, 1)
        down_part = lax.dynamic_slice_in_dim(down_proj, first, group_width, 0)
        partial_value = jnp.dot(hidden_part, down_part, preferred_element_type=jnp.float32).astype(jnp.bfloat16)
        partial_value = lax.optimization_barrier(partial_value)
        return running + partial_value.astype(jnp.float32), None

    start_sum = jnp.zeros((inputs.shape[0], down_proj.shape[1]), jnp.float32)
    total, _ = lax.scan(one_group, start_sum, jnp.arange(group_count, dtype=jnp.int32))
    return total


def reference(row_codes, row_scales, expert_ids, gate_weights, placement, w_gate, w_up, w_down, shared_gate, shared_up, shared_down):
    tokens = dequantize(row_codes, row_scales)
    shared_out = grouped_expert(tokens, shared_gate, shared_up, shared_down)
    rows_most = N_WIDE * N_NARROW * N_PAIR * CAP

    def per_expert(totals, expert):
        is_hit = expert_ids == expert
        chosen = jnp.any(is_hit, axis=1)
        weight = jnp.sum(jnp.where(is_hit, gate_weights, jnp.zeros_like(gate_weights)), axis=1)
        row_index = jnp.nonzero(chosen, size=rows_most, fill_value=0)[0].astype(jnp.int32)
        live_count = jnp.sum(chosen.astype(jnp.int32))
        is_valid = jnp.arange(rows_most, dtype=jnp.int32) < live_count
        home_slot = placement[expert]
        expert_out = grouped_expert(tokens[row_index], w_gate[home_slot], w_up[home_slot], w_down[home_slot]).astype(jnp.bfloat16)
        expert_out = lax.optimization_barrier(expert_out)
        contribution = weight[row_index][:, None] * expert_out.astype(jnp.float32)
        contribution = jnp.where(is_valid[:, None], contribution, jnp.zeros_like(contribution))
        return totals.at[row_index].add(contribution), None

    start_totals = jnp.zeros((row_codes.shape[0], row_codes.shape[1]), jnp.float32)
    routed, _ = lax.scan(per_expert, start_totals, jnp.arange(EXPERTS, dtype=jnp.int32))
    return (shared_out + routed).astype(jnp.bfloat16)
```

```python
import functools

import jax
import jax.numpy as jnp
from jax import lax
from jax.experimental import pallas as pl
from jax.experimental.pallas import tpu as pltpu
from jax.sharding import PartitionSpec as P

CAP = 5
LANES = 128
SPAN = 7
MAX_ROWS = 128

VMEM = pltpu.VMEM
VSPEC = pl.BlockSpec(memory_space=pltpu.VMEM)
SSPEC = pl.BlockSpec(memory_space=pltpu.SMEM)
ASPEC = pl.BlockSpec(memory_space=pl.ANY)
F32 = jnp.float32
BF16 = jnp.bfloat16


def put(flat, at, value, rows):
    tall = flat.shape[0] // rows
    for b in range(value.shape[1] // LANES):
        flat[pl.ds(at // LANES + b, rows, stride=tall), :] = value[
            :, b * LANES : (b + 1) * LANES
        ]


def dispatch_kernel(ids, place, weights, here, codes, scales, near, *rest):
    far, (tok, stage, count) = rest[:-3], rest[-3:]
    rows, features = codes.shape
    topk = ids.shape[1]
    tall = features // LANES
    for e in range(place.shape[0]):
        count[e] = 0
    for b in range(tall):
        block = codes[:, b * LANES : (b + 1) * LANES].astype(F32)
        tok[pl.ds(b, rows, stride=tall), :] = block * scales[:, b : b + 1].astype(F32)
    near[:rows] = tok[...].reshape(rows, tall, LANES).astype(BF16)
    stage[...] = jnp.zeros_like(stage)
    sub = lax.broadcasted_iota(jnp.int32, (rows, LANES), 0)
    lane = lax.broadcasted_iota(jnp.int32, (rows, LANES), 1)
    weight = jnp.zeros((rows, LANES), F32)
    for t in range(rows):
        for k in range(topk):
            e = ids[t, k]
            node = place[e]
            slot = count[e]
            count[e] = slot + 1
            weight = jnp.where((sub == t) & (lane == node), weights[t, k], weight)
            stage[(node ^ here[0]) * CAP + slot] = tok[t * tall : (t + 1) * tall, :]
    high = weight.astype(BF16).astype(F32)
    middle = (weight - high).astype(BF16).astype(F32)
    low = weight - high - middle
    near[rows] = jnp.concatenate(
        [high, middle, low, jnp.zeros((tall - 3 * rows, LANES), F32)], axis=0
    ).astype(BF16)
    for k, ref in enumerate(far):
        ref[...] = stage[(k + 1) * CAP : (k + 2) * CAP].astype(BF16)


def unpack(refs, blocks, rows, flat, inputs):
    tall = inputs.shape[1] // LANES
    at = 0
    for ref, count in zip(refs, blocks):
        flat[at * tall : (at + count) * tall, :] = (
            ref[:count].astype(F32).reshape(count * tall, LANES)
        )
        at += count
    if at < rows:
        flat[at * tall : rows * tall, :] = jnp.zeros(((rows - at) * tall, LANES), F32)
    for b in range(tall):
        inputs[:rows, b * LANES : (b + 1) * LANES] = flat[
            pl.ds(b, rows, stride=tall), :
        ].astype(BF16)


def silu_mul(gate, up):
    return (gate / (1.0 + jnp.exp(-gate)) * up).astype(BF16)


def near_kernel(n_narrow, n_pair, here, *refs):
    count = n_narrow * n_pair
    arrived = refs[:count]
    hbm = refs[count : count + 6]
    outs = refs[count + 6 : count + 6 + n_pair]
    kept = refs[count + 6 + n_pair : count + 9 + n_pair]
    s_gate, s_up, s_down, flat, inputs, sems = refs[count + 9 + n_pair :]
    held = (s_gate, s_up, s_down) + tuple(kept)
    copies = [
        pltpu.make_async_copy(src, dst, sems.at[i])
        for i, (src, dst) in enumerate(zip(hbm, held))
    ]
    for copy in copies:
        copy.start()
    tokens, tall = arrived[0].shape[0] - 1, arrived[0].shape[1]
    rows = count * tokens
    unpack(arrived, [tokens] * count, rows, flat, inputs)
    weight = []
    for ref in arrived:
        parts = ref[tokens].astype(F32)
        whole = (
            parts[:tokens] + parts[tokens : 2 * tokens] + parts[2 * tokens : 3 * tokens]
        )
        lane = lax.broadcasted_iota(jnp.int32, whole.shape, 1)
        weight.append(
            jnp.sum(jnp.where(lane == here[0], whole, 0.0), axis=1, keepdims=True)
        )
    weight = jnp.concatenate(weight, axis=0)
    x = inputs[:rows]
    hidden = []
    for i in (0, 3):
        copies[i].wait()
        gate = jnp.dot(x, held[i][...], preferred_element_type=F32)
        copies[i + 1].wait()
        up = jnp.dot(x, held[i + 1][...], preferred_element_type=F32)
        hidden.append(silu_mul(gate, up))
    copies[2].wait()
    copies[5].wait()
    for first in range(0, tall * LANES, SPAN * LANES):
        at = slice(first, first + SPAN * LANES)
        shared = jnp.dot(hidden[0], held[2][:, at], preferred_element_type=F32)
        routed = jnp.dot(hidden[1], held[5][:, at], preferred_element_type=F32)
        put(flat, first, shared + weight * routed, rows)
    each = n_narrow * tokens
    for c in range(n_pair):
        part = flat[c * each * tall : (c + 1) * each * tall, :]
        outs[c][...] = part.reshape(n_narrow, tokens, tall, LANES).astype(BF16)


def far_kernel(n_narrow, n_pair, per, *refs):
    count = n_narrow * n_pair * per
    arrived, rest = refs[:count], refs[count:]
    gate_w, up_w, down_w = rest[:3]
    outs = rest[3 : 3 + n_pair]
    flat, inputs = rest[3 + n_pair :]
    tall = arrived[0].shape[1]
    blocks = [ref.shape[0] for ref in arrived]
    slots = sum(blocks[:per])
    step = count if sum(blocks) <= MAX_ROWS else per
    for first in range(0, count, step):
        total = sum(blocks[first : first + step])
        rows = -(-total // 16) * 16
        unpack(arrived[first : first + step], blocks[first : first + step], rows, flat, inputs)
        x = inputs[:rows]
        gate = jnp.dot(x, gate_w[...], preferred_element_type=F32)
        up = jnp.dot(x, up_w[...], preferred_element_type=F32)
        hidden = silu_mul(gate, up)
        for at in range(0, tall * LANES, SPAN * LANES):
            value = jnp.dot(
                hidden, down_w[:, at : at + SPAN * LANES], preferred_element_type=F32
            )
            put(flat, at, value, rows)
        for i in range(step // per):
            c, j = divmod(first // per + i, n_narrow)
            part = flat[i * slots * tall : (i + 1) * slots * tall, :]
            outs[c][j] = part.reshape(slots, tall, LANES).astype(BF16)


def pair_sum_kernel(n_pair, *refs):
    parts, outs = refs[:n_pair], refs[n_pair:]
    for j, out in enumerate(outs):
        total = parts[0][j].astype(F32)
        for ref in parts[1:]:
            total = total + ref[j].astype(F32)
        out[...] = total.astype(BF16)


def narrow_sum_kernel(n_narrow, *refs):
    parts, outs = refs[:n_narrow], refs[n_narrow:]
    for k, out in enumerate(outs):
        at = slice(k * CAP, (k + 1) * CAP)
        total = parts[0][at].astype(F32)
        for ref in parts[1:]:
            total = total + ref[at].astype(F32)
        out[...] = total.astype(BF16)


def combine_kernel(n_narrow, ids, place, weights, here, *refs):
    near, rest = refs[:n_narrow], refs[n_narrow:]
    far, (out, total, stage, count) = rest[:-4], rest[-4:]
    rows, features = out.shape
    tall = features // LANES
    topk = ids.shape[1]
    for e in range(place.shape[0]):
        count[e] = 0
    stage[:CAP] = jnp.zeros((CAP, tall, LANES), F32)
    for k, ref in enumerate(far):
        stage[(k + 1) * CAP : (k + 2) * CAP] = ref[...].astype(F32)
    for t in range(rows):
        value = near[0][t].astype(F32)
        for ref in near[1:]:
            value = value + ref[t].astype(F32)
        for k in range(topk):
            e = ids[t, k]
            slot = count[e]
            count[e] = slot + 1
            value = value + weights[t, k] * stage[(place[e] ^ here[0]) * CAP + slot]
        total[t * tall : (t + 1) * tall, :] = value
    for b in range(tall):
        out[:, b * LANES : (b + 1) * LANES] = total[
            pl.ds(b, rows, stride=tall), :
        ].astype(BF16)


def swap(value, axis, offset):
    size = lax.axis_size(axis)
    return lax.ppermute(value, axis, [(i, i ^ offset) for i in range(size)])


def call(kernel, name, ins, specs, outs, scratch, flops=0, moved=0, limit=48):
    return pl.pallas_call(
        kernel,
        out_shape=outs,
        in_specs=specs,
        out_specs=jax.tree.map(lambda _: VSPEC, outs),
        scratch_shapes=scratch,
        compiler_params=pltpu.CompilerParams(vmem_limit_bytes=limit << 20),
        cost_estimate=pl.CostEstimate(flops=flops, bytes_accessed=moved, transcendentals=0),
        name=name,
    )(*ins)


def shards(
    row_codes,
    row_scales,
    expert_ids,
    gate_weights,
    placement,
    w_gate,
    w_up,
    w_down,
    shared_gate,
    shared_up,
    shared_down,
):
    n_wide = lax.axis_size("wide")
    n_narrow = lax.axis_size("narrow")
    n_pair = lax.axis_size("pair")
    tokens, features = row_codes.shape
    hidden = w_gate.shape[2]
    tall = features // LANES
    slots = (n_wide - 1) * CAP
    here = lax.axis_index("wide").astype(jnp.int32).reshape(1)
    routing = (expert_ids, placement, gate_weights, here)

    def block(*lead):
        return jax.ShapeDtypeStruct(lead + (tall, LANES), BF16)

    near, *far = call(
        dispatch_kernel,
        "dispatch",
        routing + (row_codes, row_scales),
        [SSPEC] * 4 + [VSPEC] * 2,
        [block(tokens + 1)] + [block(CAP)] * (n_wide - 1),
        [
            VMEM((tokens * tall, LANES), F32),
            VMEM((n_wide * CAP, tall, LANES), F32),
            pltpu.SMEM((placement.shape[0],), jnp.int32),
        ],
    )
    order = [k for k in range(1, n_wide)]
    far = [swap(value, "wide", k) for k, value in zip(order, far)]
    near_line = [near] + [swap(near, "narrow", j) for j in range(1, n_narrow)]
    near_all = list(near_line)
    for c in range(1, n_pair):
        near_all += [swap(value, "pair", c) for value in near_line]
    if n_wide > 4:
        far = [jnp.concatenate(far, axis=0)]
    per = len(far)
    far_line = list(far)
    for j in range(1, n_narrow):
        far_line += [swap(value, "narrow", j) for value in far]
    far_all = list(far_line)
    for c in range(1, n_pair):
        far_all += [swap(value, "pair", c) for value in far_line]

    near_rows = n_narrow * n_pair * tokens
    outs = call(
        functools.partial(near_kernel, n_narrow, n_pair),
        "near",
        [here] + near_all
        + [shared_gate, shared_up, shared_down, w_gate.reshape(features, hidden),
           w_up.reshape(features, hidden), w_down.reshape(hidden, features)],
        [SSPEC] + [VSPEC] * (n_narrow * n_pair) + [ASPEC] * 6,
        [block(n_narrow, tokens)] * n_pair
        + [VMEM((features, hidden), BF16)] * 2 + [VMEM((hidden, features), BF16)],
        [
            VMEM((features, hidden), BF16),
            VMEM((features, hidden), BF16),
            VMEM((hidden, features), BF16),
            VMEM((near_rows * tall, LANES), F32),
            VMEM((near_rows, features), BF16),
            pltpu.SemaphoreType.DMA((6,)),
        ],
        flops=12 * near_rows * features * hidden,
        moved=12 * features * hidden,
    )
    near_out, kept = outs[:n_pair], outs[n_pair:]

    far_rows = n_narrow * n_pair * slots
    pass_rows = far_rows if far_rows <= MAX_ROWS else slots
    pass_rows = -(-pass_rows // 16) * 16
    far_out = call(
        functools.partial(far_kernel, n_narrow, n_pair, per),
        "far",
        far_all + list(kept),
        [VSPEC] * (n_narrow * n_pair * per + 3),
        [block(n_narrow, slots)] * n_pair,
        [VMEM((pass_rows * tall, LANES), F32), VMEM((pass_rows, features), BF16)],
        flops=6 * far_rows * features * hidden,
        moved=6 * features * hidden,
    )

    def reduce_pair(parts, rows):
        parts = [parts[0]] + [swap(parts[c], "pair", c) for c in range(1, n_pair)]
        parts = call(
            functools.partial(pair_sum_kernel, n_pair),
            "pair_sum",
            parts,
            [VSPEC] * n_pair,
            [block(rows)] * n_narrow,
            [],
        )
        return [parts[0]] + [swap(parts[j], "narrow", j) for j in range(1, n_narrow)]

    far_back = call(
        functools.partial(narrow_sum_kernel, n_narrow),
        "narrow_sum",
        reduce_pair(far_out, slots),
        [VSPEC] * n_narrow,
        [block(CAP)] * (n_wide - 1),
        [],
    )
    far_back = [swap(value, "wide", k) for k, value in zip(order, far_back)]
    near_back = reduce_pair(near_out, tokens)
    return call(
        functools.partial(combine_kernel, n_narrow),
        "combine",
        list(routing) + near_back + far_back,
        [SSPEC] * 4 + [VSPEC] * (n_narrow + n_wide - 1),
        jax.ShapeDtypeStruct((tokens, features), BF16),
        [
            VMEM((tokens * tall, LANES), F32),
            VMEM((n_wide * CAP, tall, LANES), F32),
            pltpu.SMEM((placement.shape[0],), jnp.int32),
        ],
    )


def solution(mesh):
    rows = P(("groups", "wide", "narrow", "pair"), None)
    return jax.shard_map(
        shards,
        mesh=mesh,
        in_specs=(
            rows,
            rows,
            rows,
            rows,
            P(),
            P("wide", None, ("narrow", "pair")),
            P("wide", None, ("narrow", "pair")),
            P("wide", ("narrow", "pair"), None),
            P(None, ("narrow", "pair")),
            P(None, ("narrow", "pair")),
            P(("narrow", "pair"), None),
        ),
        out_specs=rows,
        check_vma=False,
    )
```

```python
import functools

import jax
import jax.numpy as jnp
from jax import lax
from jax.experimental import pallas as pl
from jax.experimental.pallas import tpu as pltpu
from jax.sharding import PartitionSpec as P

CAP = 5
LANES = 128
SPAN = 7
MAX_ROWS = 128

VMEM = pltpu.VMEM
VSPEC = pl.BlockSpec(memory_space=pltpu.VMEM)
SSPEC = pl.BlockSpec(memory_space=pltpu.SMEM)
ASPEC = pl.BlockSpec(memory_space=pl.ANY)
F32 = jnp.float32
BF16 = jnp.bfloat16


def put(flat, at, value, rows):
    tall = flat.shape[0] // rows
    for b in range(value.shape[1] // LANES):
        flat[pl.ds(at // LANES + b, rows, stride=tall), :] = value[
            :, b * LANES : (b + 1) * LANES
        ]


def dispatch_kernel(ids_in, place_in, weights_in, codes_in, scales_in, *refs):
    near, far = refs[0], refs[1:-10]
    route, gains = refs[-10:-8]
    ids, place, weights, codes, scales, tok, stage, sems = refs[-8:]
    copies = [
        pltpu.make_async_copy(src, dst, sems.at[i])
        for i, (src, dst) in enumerate(
            (
                (codes_in, codes),
                (scales_in, scales),
                (ids_in, ids),
                (place_in, place),
                (weights_in, weights),
            )
        )
    ]
    for copy in copies:
        copy.start()
    here = lax.axis_index("wide")
    rows, features = codes.shape
    topk = ids.shape[0]
    tall = features // LANES
    stage[...] = jnp.zeros_like(stage)
    for copy in copies:
        copy.wait()
    for b in range(tall):
        block = codes[:, b * LANES : (b + 1) * LANES].astype(F32)
        tok[pl.ds(b, rows, stride=tall), :] = block * scales[:, b : b + 1].astype(F32)
    near[:rows] = tok[...].reshape(rows, tall, LANES).astype(BF16)
    sub = lax.broadcasted_iota(jnp.int32, (rows, LANES), 0)
    lane = lax.broadcasted_iota(jnp.int32, (rows, LANES), 1)
    weight = jnp.zeros((rows, LANES), F32)
    named = []
    for t in range(rows):
        for k in range(topk):
            e = ids[k, t]
            node = place[e]
            slot = jnp.int32(0)
            for other in named[: t * topk]:
                slot = slot + jnp.where(other == e, 1, 0)
            named.append(e)
            at = (node ^ here) * CAP + slot
            route[k, t] = at
            gains[k, t] = weights[k, t]
            weight = jnp.where((sub == t) & (lane == node), weights[k, t], weight)
            stage[at] = tok[t * tall : (t + 1) * tall, :]
    high = weight.astype(BF16).astype(F32)
    middle = (weight - high).astype(BF16).astype(F32)
    low = weight - high - middle
    near[rows] = jnp.concatenate(
        [high, middle, low, jnp.zeros((tall - 3 * rows, LANES), F32)], axis=0
    ).astype(BF16)
    for k, ref in enumerate(far):
        ref[...] = stage[(k + 1) * CAP : (k + 2) * CAP].astype(BF16)


def load_kernel(count, *refs):
    srcs, outs, sems = refs[:count], refs[-count - 1 : -1], refs[-1]
    copies = [
        pltpu.make_async_copy(src, dst, sems.at[i])
        for i, (src, dst) in enumerate(zip(srcs, outs))
    ]
    for copy in copies:
        copy.start()
    for copy in copies:
        copy.wait()


def unpack(refs, blocks, rows, flat, inputs):
    tall = inputs.shape[1] // LANES
    at = 0
    for ref, count in zip(refs, blocks):
        flat[at * tall : (at + count) * tall, :] = (
            ref[:count].astype(F32).reshape(count * tall, LANES)
        )
        at += count
    if at < rows:
        flat[at * tall : rows * tall, :] = jnp.zeros(((rows - at) * tall, LANES), F32)
    for b in range(tall):
        inputs[:rows, b * LANES : (b + 1) * LANES] = flat[
            pl.ds(b, rows, stride=tall), :
        ].astype(BF16)


def silu_mul(gate, up):
    return (gate / (1.0 + jnp.exp(-gate)) * up).astype(BF16)


def near_kernel(n_narrow, n_pair, *refs):
    count = n_narrow * n_pair
    arrived = refs[:count]
    held = refs[count : count + 6]
    outs = refs[count + 6 : count + 6 + n_pair]
    flat, inputs = refs[count + 6 + n_pair :]
    here = lax.axis_index("wide")
    tokens, tall = arrived[0].shape[0] - 1, arrived[0].shape[1]
    rows = count * tokens
    unpack(arrived, [tokens] * count, rows, flat, inputs)
    weight = []
    for ref in arrived:
        parts = ref[tokens].astype(F32)
        whole = (
            parts[:tokens] + parts[tokens : 2 * tokens] + parts[2 * tokens : 3 * tokens]
        )
        lane = lax.broadcasted_iota(jnp.int32, whole.shape, 1)
        weight.append(
            jnp.sum(jnp.where(lane == here, whole, 0.0), axis=1, keepdims=True)
        )
    weight = jnp.concatenate(weight, axis=0)
    x = inputs[:rows]
    hidden = []
    for i in (0, 3):
        gate = jnp.dot(x, held[i][...], preferred_element_type=F32)
        up = jnp.dot(x, held[i + 1][...], preferred_element_type=F32)
        hidden.append(silu_mul(gate, up))
    for first in range(0, tall * LANES, SPAN * LANES):
        at = slice(first, first + SPAN * LANES)
        shared = jnp.dot(hidden[0], held[2][:, at], preferred_element_type=F32)
        routed = jnp.dot(hidden[1], held[5][:, at], preferred_element_type=F32)
        put(flat, first, shared + weight * routed, rows)
    each = n_narrow * tokens
    for c in range(n_pair):
        part = flat[c * each * tall : (c + 1) * each * tall, :]
        outs[c][...] = part.reshape(n_narrow, tokens, tall, LANES).astype(BF16)


def far_kernel(n_narrow, n_pair, per, *refs):
    count = n_narrow * n_pair * per
    arrived, rest = refs[:count], refs[count:]
    gate_w, up_w, down_w = rest[:3]
    outs = rest[3 : 3 + n_pair * per]
    flat, inputs = rest[3 + n_pair * per :]
    tall = arrived[0].shape[1]
    blocks = [ref.shape[0] for ref in arrived]
    step = count if sum(blocks) <= MAX_ROWS else per
    for first in range(0, count, step):
        group = blocks[first : first + step]
        rows = -(-sum(group) // 16) * 16
        unpack(arrived[first : first + step], group, rows, flat, inputs)
        x = inputs[:rows]
        gate = jnp.dot(x, gate_w[...], preferred_element_type=F32)
        up = jnp.dot(x, up_w[...], preferred_element_type=F32)
        hidden = silu_mul(gate, up)
        for at in range(0, tall * LANES, SPAN * LANES):
            value = jnp.dot(
                hidden, down_w[:, at : at + SPAN * LANES], preferred_element_type=F32
            )
            put(flat, at, value, rows)
        at = 0
        for i, slots in enumerate(group):
            line, k = divmod(first + i, per)
            c, j = divmod(line, n_narrow)
            part = flat[at * tall : (at + slots) * tall, :]
            outs[c * per + k][j] = part.reshape(slots, tall, LANES).astype(BF16)
            at += slots


def pair_sum_kernel(n_pair, *refs):
    parts, outs = refs[:n_pair], refs[n_pair:]
    for j, out in enumerate(outs):
        total = parts[0][j].astype(F32)
        for ref in parts[1:]:
            total = total + ref[j].astype(F32)
        out[...] = total.astype(BF16)


def narrow_sum_kernel(n_narrow, *refs):
    parts, outs = refs[:n_narrow], refs[n_narrow:]
    at = 0
    for out in outs:
        rows = slice(at, at + out.shape[0])
        total = parts[0][rows].astype(F32)
        for ref in parts[1:]:
            total = total + ref[rows].astype(F32)
        out[...] = total.astype(BF16)
        at += out.shape[0]


def combine_kernel(n_narrow, order, route, gains, *refs):
    near, rest = refs[:n_narrow], refs[n_narrow:]
    far, (out, total, stage) = rest[:-3], rest[-3:]
    rows, features = out.shape
    tall = features // LANES
    topk = route.shape[0]
    stage[:CAP] = jnp.zeros((CAP, tall, LANES), F32)
    for k, ref in zip(order, far):
        stage[k * CAP : (k + 1) * CAP] = ref[...].astype(F32)
    for t in range(rows):
        value = near[0][t].astype(F32)
        for ref in near[1:]:
            value = value + ref[t].astype(F32)
        for k in range(topk):
            value = value + gains[k, t] * stage[route[k, t]]
        total[t * tall : (t + 1) * tall, :] = value
    for b in range(tall):
        out[:, b * LANES : (b + 1) * LANES] = total[
            pl.ds(b, rows, stride=tall), :
        ].astype(BF16)


def swap(value, axis, offset):
    size = lax.axis_size(axis)
    return lax.ppermute(value, axis, [(i, i ^ offset) for i in range(size)])


def call(kernel, name, ins, specs, outs, scratch, flops=0, moved=0, limit=16):
    return pl.pallas_call(
        kernel,
        out_shape=outs,
        in_specs=specs,
        out_specs=jax.tree.map(
            lambda out: SSPEC if getattr(out, "memory_space", None) == pltpu.SMEM else VSPEC,
            outs,
        ),
        scratch_shapes=scratch,
        compiler_params=pltpu.CompilerParams(vmem_limit_bytes=limit << 20),
        cost_estimate=pl.CostEstimate(flops=flops, bytes_accessed=moved, transcendentals=0),
        name=name,
    )(*ins)


def shards(
    row_codes,
    row_scales,
    expert_ids,
    gate_weights,
    placement,
    w_gate,
    w_up,
    w_down,
    shared_gate,
    shared_up,
    shared_down,
):
    n_wide = lax.axis_size("wide")
    n_narrow = lax.axis_size("narrow")
    n_pair = lax.axis_size("pair")
    tokens, features = row_codes.shape
    hidden = w_gate.shape[2]
    tall = features // LANES
    topk = expert_ids.shape[1]
    limit = 16 if n_wide <= 4 else 48

    def block(*lead):
        return jax.ShapeDtypeStruct(lead + (tall, LANES), BF16)

    near, *far = call(
        dispatch_kernel,
        "dispatch",
        (expert_ids.T, placement, gate_weights.T, row_codes, row_scales),
        [ASPEC] * 5,
        [block(tokens + 1)]
        + [block(CAP)] * (n_wide - 1)
        + [pltpu.SMEM((topk, tokens), jnp.int32), pltpu.SMEM((topk, tokens), F32)],
        [
            pltpu.SMEM((topk, tokens), jnp.int32),
            pltpu.SMEM(placement.shape, jnp.int32),
            pltpu.SMEM((topk, tokens), F32),
            VMEM((tokens, features), BF16),
            VMEM(row_scales.shape, BF16),
            VMEM((tokens * tall, LANES), F32),
            VMEM((n_wide * CAP, tall, LANES), F32),
            pltpu.SemaphoreType.DMA((5,)),
        ],
    )
    far, (route, gains) = far[:-2], far[-2:]
    order = list(range(n_wide - 1, 0, -1))
    far = [swap(far[k - 1], "wide", k) for k in order]
    near_line = [near] + [swap(near, "narrow", j) for j in range(1, n_narrow)]

    def load(name, after, *weights):
        return call(
            functools.partial(load_kernel, len(weights)),
            name,
            list(weights) + [after],
            [ASPEC] * (len(weights) + 1),
            [VMEM(value.shape, BF16) for value in weights],
            [pltpu.SemaphoreType.DMA((len(weights),))],
            moved=2 * sum(value.size for value in weights),
        )

    shared = load("load_shared", near, shared_gate, shared_up, shared_down)
    routed = load(
        "load_routed",
        near,
        w_gate.reshape(features, hidden),
        w_up.reshape(features, hidden),
        w_down.reshape(hidden, features),
    )
    near_all = list(near_line)
    for c in range(1, n_pair):
        near_all += [swap(value, "pair", c) for value in near_line]
    if n_wide > 4:
        far = [jnp.concatenate(far, axis=0)]
    per = len(far)
    slots = far[0].shape[0]
    far_line = list(far)
    for j in range(1, n_narrow):
        far_line += [swap(value, "narrow", j) for value in far]
    far_all = list(far_line)
    for c in range(1, n_pair):
        far_all += [swap(value, "pair", c) for value in far_line]

    near_rows = n_narrow * n_pair * tokens
    near_out = call(
        functools.partial(near_kernel, n_narrow, n_pair),
        "near",
        near_all + list(shared) + list(routed),
        [VSPEC] * (n_narrow * n_pair + 6),
        [block(n_narrow, tokens)] * n_pair,
        [VMEM((near_rows * tall, LANES), F32), VMEM((near_rows, features), BF16)],
        flops=12 * near_rows * features * hidden,
        moved=12 * features * hidden,
        limit=limit,
    )

    far_rows = n_narrow * n_pair * per * slots
    pass_rows = far_rows if far_rows <= MAX_ROWS else per * slots
    pass_rows = -(-pass_rows // 16) * 16
    far_out = call(
        functools.partial(far_kernel, n_narrow, n_pair, per),
        "far",
        far_all + list(routed),
        [VSPEC] * (n_narrow * n_pair * per + 3),
        [block(n_narrow, slots)] * (n_pair * per),
        [VMEM((pass_rows * tall, LANES), F32), VMEM((pass_rows, features), BF16)],
        flops=6 * far_rows * features * hidden,
        moved=6 * features * hidden,
        limit=limit,
    )

    def reduce_pair(parts, rows):
        parts = [parts[0]] + [swap(parts[c], "pair", c) for c in range(1, n_pair)]
        parts = call(
            functools.partial(pair_sum_kernel, n_pair),
            "pair_sum",
            parts,
            [VSPEC] * n_pair,
            [block(rows)] * n_narrow,
            [],
            limit=limit,
        )
        return [parts[0]] + [swap(parts[j], "narrow", j) for j in range(1, n_narrow)]

    near_back = reduce_pair(near_out, tokens)
    far_back = []
    for k in range(per):
        far_back += call(
            functools.partial(narrow_sum_kernel, n_narrow),
            "narrow_sum",
            reduce_pair(far_out[k::per], slots),
            [VSPEC] * n_narrow,
            [block(CAP)] * (slots // CAP),
            [],
            limit=limit,
        )
    far_back = [swap(value, "wide", k) for k, value in zip(order, far_back)]
    return call(
        functools.partial(combine_kernel, n_narrow, order),
        "combine",
        [route, gains] + near_back + far_back,
        [SSPEC] * 2 + [VSPEC] * (n_narrow + n_wide - 1),
        jax.ShapeDtypeStruct((tokens, features), BF16),
        [
            VMEM((tokens * tall, LANES), F32),
            VMEM((n_wide * CAP, tall, LANES), F32),
        ],
    )


def solution(mesh):
    rows = P(("groups", "wide", "narrow", "pair"), None)
    return jax.shard_map(
        shards,
        mesh=mesh,
        in_specs=(
            rows,
            rows,
            rows,
            rows,
            P(),
            P("wide", None, ("narrow", "pair")),
            P("wide", None, ("narrow", "pair")),
            P("wide", ("narrow", "pair"), None),
            P(None, ("narrow", "pair")),
            P(None, ("narrow", "pair")),
            P(("narrow", "pair"), None),
        ),
        out_specs=rows,
        check_vma=False,
    )
```

```python
import functools

import jax
import jax.numpy as jnp
from jax import lax
from jax.experimental import pallas as pl
from jax.experimental.pallas import tpu as pltpu
from jax.sharding import PartitionSpec as P

CAP = 5
LANES = 128
SPAN = 7
MAX_ROWS = 128

VMEM = pltpu.VMEM
VSPEC = pl.BlockSpec(memory_space=pltpu.VMEM)
SSPEC = pl.BlockSpec(memory_space=pltpu.SMEM)
ASPEC = pl.BlockSpec(memory_space=pl.ANY)
F32 = jnp.float32
BF16 = jnp.bfloat16


def put(flat, at, value, rows):
    tall = flat.shape[0] // rows
    for b in range(value.shape[1] // LANES):
        flat[pl.ds(at // LANES + b, rows, stride=tall), :] = value[
            :, b * LANES : (b + 1) * LANES
        ]


def dispatch_kernel(ids_in, place_in, weights_in, codes_in, scales_in, *refs):
    near, far = refs[0], refs[1:-10]
    route, gains = refs[-10:-8]
    ids, place, weights, codes, scales, tok, stage, sems = refs[-8:]
    copies = [
        pltpu.make_async_copy(src, dst, sems.at[i])
        for i, (src, dst) in enumerate(
            (
                (codes_in, codes),
                (scales_in, scales),
                (ids_in, ids),
                (place_in, place),
                (weights_in, weights),
            )
        )
    ]
    for copy in copies:
        copy.start()
    here = lax.axis_index("wide")
    rows, features = codes.shape
    topk = ids.shape[0]
    tall = features // LANES
    stage[...] = jnp.zeros_like(stage)
    for copy in copies:
        copy.wait()
    for b in range(tall):
        block = codes[:, b * LANES : (b + 1) * LANES].astype(F32)
        tok[pl.ds(b, rows, stride=tall), :] = block * scales[:, b : b + 1].astype(F32)
    near[:rows] = tok[...].reshape(rows, tall, LANES).astype(BF16)
    sub = lax.broadcasted_iota(jnp.int32, (rows, LANES), 0)
    lane = lax.broadcasted_iota(jnp.int32, (rows, LANES), 1)
    weight = jnp.zeros((rows, LANES), F32)
    named = []
    for t in range(rows):
        for k in range(topk):
            e = ids[k, t]
            node = place[e]
            slot = jnp.int32(0)
            for other in named[: t * topk]:
                slot = slot + jnp.where(other == e, 1, 0)
            named.append(e)
            at = (node ^ here) * CAP + slot
            route[k, t] = at
            gains[k, t] = weights[k, t]
            weight = jnp.where((sub == t) & (lane == node), weights[k, t], weight)
            stage[at] = tok[t * tall : (t + 1) * tall, :]
    high = weight.astype(BF16).astype(F32)
    middle = (weight - high).astype(BF16).astype(F32)
    low = weight - high - middle
    near[rows] = jnp.concatenate(
        [high, middle, low, jnp.zeros((tall - 3 * rows, LANES), F32)], axis=0
    ).astype(BF16)
    for k, ref in enumerate(far):
        ref[...] = stage[(k + 1) * CAP : (k + 2) * CAP].astype(BF16)


def load_kernel(count, *refs):
    srcs, outs, sems = refs[:count], refs[-count - 1 : -1], refs[-1]
    copies = [
        pltpu.make_async_copy(src, dst, sems.at[i])
        for i, (src, dst) in enumerate(zip(srcs, outs))
    ]
    for copy in copies:
        copy.start()
    for copy in copies:
        copy.wait()


def unpack(refs, blocks, rows, flat, inputs):
    tall = inputs.shape[1] // LANES
    at = 0
    for ref, count in zip(refs, blocks):
        flat[at * tall : (at + count) * tall, :] = (
            ref[:count].astype(F32).reshape(count * tall, LANES)
        )
        at += count
    if at < rows:
        flat[at * tall : rows * tall, :] = jnp.zeros(((rows - at) * tall, LANES), F32)
    for b in range(tall):
        inputs[:rows, b * LANES : (b + 1) * LANES] = flat[
            pl.ds(b, rows, stride=tall), :
        ].astype(BF16)


def silu_mul(gate, up):
    return (gate / (1.0 + jnp.exp(-gate)) * up).astype(BF16)


def near_kernel(n_narrow, n_pair, *refs):
    count = n_narrow * n_pair
    arrived = refs[:count]
    held = refs[count : count + 6]
    outs = refs[count + 6 : count + 6 + n_pair]
    flat, inputs = refs[count + 6 + n_pair :]
    here = lax.axis_index("wide")
    tokens, tall = arrived[0].shape[0] - 1, arrived[0].shape[1]
    rows = count * tokens
    unpack(arrived, [tokens] * count, rows, flat, inputs)
    weight = []
    for ref in arrived:
        parts = ref[tokens].astype(F32)
        whole = (
            parts[:tokens] + parts[tokens : 2 * tokens] + parts[2 * tokens : 3 * tokens]
        )
        lane = lax.broadcasted_iota(jnp.int32, whole.shape, 1)
        weight.append(
            jnp.sum(jnp.where(lane == here, whole, 0.0), axis=1, keepdims=True)
        )
    weight = jnp.concatenate(weight, axis=0)
    x = inputs[:rows]
    hidden = []
    for i in (0, 3):
        gate = jnp.dot(x, held[i][...], preferred_element_type=F32)
        up = jnp.dot(x, held[i + 1][...], preferred_element_type=F32)
        hidden.append(silu_mul(gate, up))
    for first in range(0, tall * LANES, SPAN * LANES):
        at = slice(first, first + SPAN * LANES)
        shared = jnp.dot(hidden[0], held[2][:, at], preferred_element_type=F32)
        routed = jnp.dot(hidden[1], held[5][:, at], preferred_element_type=F32)
        put(flat, first, shared + weight * routed, rows)
    each = n_narrow * tokens
    for c in range(n_pair):
        part = flat[c * each * tall : (c + 1) * each * tall, :]
        outs[c][...] = part.reshape(n_narrow, tokens, tall, LANES).astype(BF16)


def far_kernel(n_narrow, n_pair, per, *refs):
    count = n_narrow * n_pair * per
    arrived, rest = refs[:count], refs[count:]
    gate_w, up_w, down_w = rest[:3]
    outs = rest[3 : 3 + n_pair * per]
    flat, inputs = rest[3 + n_pair * per :]
    tall = arrived[0].shape[1]
    blocks = [ref.shape[0] for ref in arrived]
    step = count if sum(blocks) <= MAX_ROWS else per
    for first in range(0, count, step):
        group = blocks[first : first + step]
        rows = -(-sum(group) // 16) * 16
        unpack(arrived[first : first + step], group, rows, flat, inputs)
        x = inputs[:rows]
        gate = jnp.dot(x, gate_w[...], preferred_element_type=F32)
        up = jnp.dot(x, up_w[...], preferred_element_type=F32)
        hidden = silu_mul(gate, up)
        for at in range(0, tall * LANES, SPAN * LANES):
            value = jnp.dot(
                hidden, down_w[:, at : at + SPAN * LANES], preferred_element_type=F32
            )
            put(flat, at, value, rows)
        at = 0
        for i, slots in enumerate(group):
            line, k = divmod(first + i, per)
            c, j = divmod(line, n_narrow)
            part = flat[at * tall : (at + slots) * tall, :]
            outs[c * per + k][j] = part.reshape(slots, tall, LANES).astype(BF16)
            at += slots


def pair_sum_kernel(n_pair, *refs):
    parts, outs = refs[:n_pair], refs[n_pair:]
    for j, out in enumerate(outs):
        total = parts[0][j].astype(F32)
        for ref in parts[1:]:
            total = total + ref[j].astype(F32)
        out[...] = total.astype(BF16)


def narrow_sum_kernel(n_narrow, *refs):
    parts, outs = refs[:n_narrow], refs[n_narrow:]
    at = 0
    for out in outs:
        rows = slice(at, at + out.shape[0])
        total = parts[0][rows].astype(F32)
        for ref in parts[1:]:
            total = total + ref[rows].astype(F32)
        out[...] = total.astype(BF16)
        at += out.shape[0]


def combine_kernel(n_narrow, order, route, gains, *refs):
    near, rest = refs[:n_narrow], refs[n_narrow:]
    far, (out, total, stage) = rest[:-3], rest[-3:]
    rows, features = out.shape
    tall = features // LANES
    topk = route.shape[0]
    stage[:CAP] = jnp.zeros((CAP, tall, LANES), F32)
    for k, ref in zip(order, far):
        stage[k * CAP : (k + 1) * CAP] = ref[...].astype(F32)
    for t in range(rows):
        value = near[0][t].astype(F32)
        for ref in near[1:]:
            value = value + ref[t].astype(F32)
        for k in range(topk):
            value = value + gains[k, t] * stage[route[k, t]]
        total[t * tall : (t + 1) * tall, :] = value
    for b in range(tall):
        out[:, b * LANES : (b + 1) * LANES] = total[
            pl.ds(b, rows, stride=tall), :
        ].astype(BF16)


def swap(value, axis, offset):
    size = lax.axis_size(axis)
    return lax.ppermute(value, axis, [(i, i ^ offset) for i in range(size)])


def in_hbm(*values):
    return [pltpu.with_memory_space_constraint(value, pltpu.HBM) for value in values]


def after(values, *others):
    return list(lax.optimization_barrier((tuple(values), others))[0])


def call(kernel, name, ins, specs, outs, scratch, flops=0, moved=0, limit=16):
    return pl.pallas_call(
        kernel,
        out_shape=outs,
        in_specs=specs,
        out_specs=jax.tree.map(
            lambda out: SSPEC if getattr(out, "memory_space", None) == pltpu.SMEM else VSPEC,
            outs,
        ),
        scratch_shapes=scratch,
        compiler_params=pltpu.CompilerParams(vmem_limit_bytes=limit << 20),
        cost_estimate=pl.CostEstimate(flops=flops, bytes_accessed=moved, transcendentals=0),
        name=name,
    )(*ins)


def shards(
    row_codes,
    row_scales,
    expert_ids,
    gate_weights,
    placement,
    w_gate,
    w_up,
    w_down,
    shared_gate,
    shared_up,
    shared_down,
):
    n_wide = lax.axis_size("wide")
    n_narrow = lax.axis_size("narrow")
    n_pair = lax.axis_size("pair")
    tokens, features = row_codes.shape
    hidden = w_gate.shape[2]
    tall = features // LANES
    topk = expert_ids.shape[1]
    limit = 16 if n_wide <= 4 else 48

    def block(*lead):
        return jax.ShapeDtypeStruct(lead + (tall, LANES), BF16)

    near, *far = call(
        dispatch_kernel,
        "dispatch",
        in_hbm(expert_ids.T, placement, gate_weights.T, row_codes, row_scales),
        [ASPEC] * 5,
        [block(tokens + 1)]
        + [block(CAP)] * (n_wide - 1)
        + [pltpu.SMEM((topk, tokens), jnp.int32), pltpu.SMEM((topk, tokens), F32)],
        [
            pltpu.SMEM((topk, tokens), jnp.int32),
            pltpu.SMEM(placement.shape, jnp.int32),
            pltpu.SMEM((topk, tokens), F32),
            VMEM((tokens, features), BF16),
            VMEM(row_scales.shape, BF16),
            VMEM((tokens * tall, LANES), F32),
            VMEM((n_wide * CAP, tall, LANES), F32),
            pltpu.SemaphoreType.DMA((5,)),
        ],
    )
    far, (route, gains) = far[:-2], far[-2:]
    order = list(range(n_wide - 1, 0, -1))
    far = [swap(far[k - 1], "wide", k) for k in order]
    near_line = [near] + [swap(near, "narrow", j) for j in range(1, n_narrow)]

    def load(name, first, *weights):
        return call(
            functools.partial(load_kernel, len(weights)),
            name,
            in_hbm(*weights) + [first],
            [ASPEC] * (len(weights) + 1),
            [VMEM(value.shape, BF16) for value in weights],
            [pltpu.SemaphoreType.DMA((len(weights),))],
            moved=2 * sum(value.size for value in weights),
        )

    shared = load("load_shared", near, shared_gate, shared_up, shared_down)
    routed = load(
        "load_routed",
        near,
        w_gate.reshape(features, hidden),
        w_up.reshape(features, hidden),
        w_down.reshape(hidden, features),
    )
    if n_wide > 4:
        far = [jnp.concatenate(far, axis=0)]
    per = len(far)
    slots = far[0].shape[0]
    far = after(far, shared[0])
    far_side = []
    for j in range(1, n_narrow):
        far_side += [swap(value, "narrow", j) for value in far]
    far_side = after(far_side, routed[0])
    near_line = after(near_line, *far)
    near_all = list(near_line)
    for c in range(1, n_pair):
        near_all += [swap(value, "pair", c) for value in near_line]
    near_all = after(near_all, *far_side)

    near_rows = n_narrow * n_pair * tokens
    near_out = call(
        functools.partial(near_kernel, n_narrow, n_pair),
        "near",
        near_all + list(shared) + list(routed),
        [VSPEC] * (n_narrow * n_pair + 6),
        [block(n_narrow, tokens)] * n_pair,
        [VMEM((near_rows * tall, LANES), F32), VMEM((near_rows, features), BF16)],
        flops=12 * near_rows * features * hidden,
        moved=12 * features * hidden,
        limit=limit,
    )

    def reduce_pair(parts, rows):
        parts = [parts[0]] + [swap(parts[c], "pair", c) for c in range(1, n_pair)]
        parts = call(
            functools.partial(pair_sum_kernel, n_pair),
            "pair_sum",
            parts,
            [VSPEC] * n_pair,
            [block(rows)] * n_narrow,
            [],
            limit=limit,
        )
        return [parts[0]] + [swap(parts[j], "narrow", j) for j in range(1, n_narrow)]

    near_back = reduce_pair(near_out, tokens)
    far_line = list(far) + far_side
    far_all = list(far_line)
    for c in range(1, n_pair):
        far_all += [swap(value, "pair", c) for value in far_line]

    far_rows = n_narrow * n_pair * per * slots
    pass_rows = far_rows if far_rows <= MAX_ROWS else per * slots
    pass_rows = -(-pass_rows // 16) * 16
    far_out = call(
        functools.partial(far_kernel, n_narrow, n_pair, per),
        "far",
        far_all + list(routed),
        [VSPEC] * (n_narrow * n_pair * per + 3),
        [block(n_narrow, slots)] * (n_pair * per),
        [VMEM((pass_rows * tall, LANES), F32), VMEM((pass_rows, features), BF16)],
        flops=6 * far_rows * features * hidden,
        moved=6 * features * hidden,
        limit=limit,
    )

    far_back = []
    for k in range(per):
        far_back += call(
            functools.partial(narrow_sum_kernel, n_narrow),
            "narrow_sum",
            reduce_pair(far_out[k::per], slots),
            [VSPEC] * n_narrow,
            [block(CAP)] * (slots // CAP),
            [],
            limit=limit,
        )
    far_back = [swap(value, "wide", k) for k, value in zip(order, far_back)]
    return call(
        functools.partial(combine_kernel, n_narrow, order),
        "combine",
        [route, gains] + near_back + far_back,
        [SSPEC] * 2 + [VSPEC] * (n_narrow + n_wide - 1),
        jax.ShapeDtypeStruct((tokens, features), BF16),
        [
            VMEM((tokens * tall, LANES), F32),
            VMEM((n_wide * CAP, tall, LANES), F32),
        ],
    )


def solution(mesh):
    rows = P(("groups", "wide", "narrow", "pair"), None)
    return jax.shard_map(
        shards,
        mesh=mesh,
        in_specs=(
            rows,
            rows,
            rows,
            rows,
            P(),
            P("wide", None, ("narrow", "pair")),
            P("wide", None, ("narrow", "pair")),
            P("wide", ("narrow", "pair"), None),
            P(None, ("narrow", "pair")),
            P(None, ("narrow", "pair")),
            P(("narrow", "pair"), None),
        ),
        out_specs=rows,
        check_vma=False,
    )
```

```python
import functools

import jax
import jax.numpy as jnp
from jax import lax
from jax.experimental import pallas as pl
from jax.experimental.pallas import tpu as pltpu
from jax.sharding import PartitionSpec as P

CAP = 5
LANES = 128
SPAN = 7
MAX_ROWS = 128

VMEM = pltpu.VMEM
VSPEC = pl.BlockSpec(memory_space=pltpu.VMEM)
SSPEC = pl.BlockSpec(memory_space=pltpu.SMEM)
ASPEC = pl.BlockSpec(memory_space=pl.ANY)
F32 = jnp.float32
BF16 = jnp.bfloat16


def put(flat, at, value, rows):
    tall = flat.shape[0] // rows
    for b in range(value.shape[1] // LANES):
        flat[pl.ds(at // LANES + b, rows, stride=tall), :] = value[
            :, b * LANES : (b + 1) * LANES
        ]


def dispatch_kernel(ids_in, place_in, weights_in, codes_in, scales_in, *refs):
    refs = refs[6:]
    near, far = refs[0], refs[1:-10]
    route, gains = refs[-10:-8]
    ids, place, weights, codes, scales, tok, stage, sems = refs[-8:]
    copies = [
        pltpu.make_async_copy(src, dst, sems.at[i])
        for i, (src, dst) in enumerate(
            (
                (codes_in, codes),
                (scales_in, scales),
                (ids_in, ids),
                (place_in, place),
                (weights_in, weights),
            )
        )
    ]
    for copy in copies:
        copy.start()
    here = lax.axis_index("wide")
    rows, features = codes.shape
    topk = ids.shape[0]
    tall = features // LANES
    stage[...] = jnp.zeros_like(stage)
    for copy in copies:
        copy.wait()
    for b in range(tall):
        block = codes[:, b * LANES : (b + 1) * LANES].astype(F32)
        tok[pl.ds(b, rows, stride=tall), :] = block * scales[:, b : b + 1].astype(F32)
    near[:rows] = tok[...].reshape(rows, tall, LANES).astype(BF16)
    sub = lax.broadcasted_iota(jnp.int32, (rows, LANES), 0)
    lane = lax.broadcasted_iota(jnp.int32, (rows, LANES), 1)
    weight = jnp.zeros((rows, LANES), F32)
    named = []
    for t in range(rows):
        for k in range(topk):
            e = ids[k, t]
            node = place[e]
            slot = jnp.int32(0)
            for other in named[: t * topk]:
                slot = slot + jnp.where(other == e, 1, 0)
            named.append(e)
            at = (node ^ here) * CAP + slot
            route[k, t] = at
            gains[k, t] = weights[k, t]
            weight = jnp.where((sub == t) & (lane == node), weights[k, t], weight)
            stage[at] = tok[t * tall : (t + 1) * tall, :]
    high = weight.astype(BF16).astype(F32)
    middle = (weight - high).astype(BF16).astype(F32)
    low = weight - high - middle
    near[rows] = jnp.concatenate(
        [high, middle, low, jnp.zeros((tall - 3 * rows, LANES), F32)], axis=0
    ).astype(BF16)
    for k, ref in enumerate(far):
        ref[...] = stage[(k + 1) * CAP : (k + 2) * CAP].astype(BF16)


def unpack(refs, blocks, rows, flat, inputs):
    tall = inputs.shape[1] // LANES
    at = 0
    for ref, count in zip(refs, blocks):
        flat[at * tall : (at + count) * tall, :] = (
            ref[:count].astype(F32).reshape(count * tall, LANES)
        )
        at += count
    if at < rows:
        flat[at * tall : rows * tall, :] = jnp.zeros(((rows - at) * tall, LANES), F32)
    for b in range(tall):
        inputs[:rows, b * LANES : (b + 1) * LANES] = flat[
            pl.ds(b, rows, stride=tall), :
        ].astype(BF16)


def silu_mul(gate, up):
    return (gate / (1.0 + jnp.exp(-gate)) * up).astype(BF16)


def near_kernel(n_narrow, n_pair, *refs):
    count = n_narrow * n_pair
    arrived = refs[:count]
    held = refs[count : count + 6]
    outs = refs[count + 6 : count + 6 + n_pair]
    flat, inputs = refs[count + 6 + n_pair :]
    here = lax.axis_index("wide")
    tokens, tall = arrived[0].shape[0] - 1, arrived[0].shape[1]
    rows = count * tokens
    unpack(arrived, [tokens] * count, rows, flat, inputs)
    weight = []
    for ref in arrived:
        parts = ref[tokens].astype(F32)
        whole = (
            parts[:tokens] + parts[tokens : 2 * tokens] + parts[2 * tokens : 3 * tokens]
        )
        lane = lax.broadcasted_iota(jnp.int32, whole.shape, 1)
        weight.append(
            jnp.sum(jnp.where(lane == here, whole, 0.0), axis=1, keepdims=True)
        )
    weight = jnp.concatenate(weight, axis=0)
    x = inputs[:rows]
    hidden = []
    for i in (0, 3):
        gate = jnp.dot(x, held[i][...], preferred_element_type=F32)
        up = jnp.dot(x, held[i + 1][...], preferred_element_type=F32)
        hidden.append(silu_mul(gate, up))
    for first in range(0, tall * LANES, SPAN * LANES):
        at = slice(first, first + SPAN * LANES)
        shared = jnp.dot(hidden[0], held[2][:, at], preferred_element_type=F32)
        routed = jnp.dot(hidden[1], held[5][:, at], preferred_element_type=F32)
        put(flat, first, shared + weight * routed, rows)
    each = n_narrow * tokens
    for c in range(n_pair):
        part = flat[c * each * tall : (c + 1) * each * tall, :]
        outs[c][...] = part.reshape(n_narrow, tokens, tall, LANES).astype(BF16)


def far_kernel(n_narrow, n_pair, per, *refs):
    count = n_narrow * n_pair * per
    arrived, rest = refs[:count], refs[count:]
    gate_w, up_w, down_w = rest[:3]
    outs = rest[3 : 3 + n_pair * per]
    flat, inputs = rest[3 + n_pair * per :]
    tall = arrived[0].shape[1]
    blocks = [ref.shape[0] for ref in arrived]
    step = count if sum(blocks) <= MAX_ROWS else per
    for first in range(0, count, step):
        group = blocks[first : first + step]
        rows = -(-sum(group) // 16) * 16
        unpack(arrived[first : first + step], group, rows, flat, inputs)
        x = inputs[:rows]
        gate = jnp.dot(x, gate_w[...], preferred_element_type=F32)
        up = jnp.dot(x, up_w[...], preferred_element_type=F32)
        hidden = silu_mul(gate, up)
        for at in range(0, tall * LANES, SPAN * LANES):
            value = jnp.dot(
                hidden, down_w[:, at : at + SPAN * LANES], preferred_element_type=F32
            )
            put(flat, at, value, rows)
        at = 0
        for i, slots in enumerate(group):
            line, k = divmod(first + i, per)
            c, j = divmod(line, n_narrow)
            part = flat[at * tall : (at + slots) * tall, :]
            outs[c * per + k][j] = part.reshape(slots, tall, LANES).astype(BF16)
            at += slots


def pair_sum_kernel(n_pair, *refs):
    parts, outs = refs[:n_pair], refs[n_pair:]
    for j, out in enumerate(outs):
        total = parts[0][j].astype(F32)
        for ref in parts[1:]:
            total = total + ref[j].astype(F32)
        out[...] = total.astype(BF16)


def narrow_sum_kernel(n_narrow, *refs):
    parts, outs = refs[:n_narrow], refs[n_narrow:]
    at = 0
    for out in outs:
        rows = slice(at, at + out.shape[0])
        total = parts[0][rows].astype(F32)
        for ref in parts[1:]:
            total = total + ref[rows].astype(F32)
        out[...] = total.astype(BF16)
        at += out.shape[0]


def combine_kernel(n_narrow, order, route, gains, *refs):
    near, rest = refs[:n_narrow], refs[n_narrow:]
    far, (out, total, stage) = rest[:-3], rest[-3:]
    rows, features = out.shape
    tall = features // LANES
    topk = route.shape[0]
    stage[:CAP] = jnp.zeros((CAP, tall, LANES), F32)
    for k, ref in zip(order, far):
        stage[k * CAP : (k + 1) * CAP] = ref[...].astype(F32)
    for t in range(rows):
        value = near[0][t].astype(F32)
        for ref in near[1:]:
            value = value + ref[t].astype(F32)
        for k in range(topk):
            value = value + gains[k, t] * stage[route[k, t]]
        total[t * tall : (t + 1) * tall, :] = value
    for b in range(tall):
        out[:, b * LANES : (b + 1) * LANES] = total[
            pl.ds(b, rows, stride=tall), :
        ].astype(BF16)


def swap(value, axis, offset):
    size = lax.axis_size(axis)
    return lax.ppermute(value, axis, [(i, i ^ offset) for i in range(size)])


def in_hbm(*values):
    return [pltpu.with_memory_space_constraint(value, pltpu.HBM) for value in values]


def after(values, *others):
    return list(lax.optimization_barrier((tuple(values), others))[0])


def call(kernel, name, ins, specs, outs, scratch, flops=0, moved=0, limit=16):
    return pl.pallas_call(
        kernel,
        out_shape=outs,
        in_specs=specs,
        out_specs=jax.tree.map(
            lambda out: SSPEC if getattr(out, "memory_space", None) == pltpu.SMEM else VSPEC,
            outs,
        ),
        scratch_shapes=scratch,
        compiler_params=pltpu.CompilerParams(vmem_limit_bytes=limit << 20),
        cost_estimate=pl.CostEstimate(flops=flops, bytes_accessed=moved, transcendentals=0),
        name=name,
    )(*ins)


def shards(
    row_codes,
    row_scales,
    expert_ids,
    gate_weights,
    placement,
    w_gate,
    w_up,
    w_down,
    shared_gate,
    shared_up,
    shared_down,
):
    n_wide = lax.axis_size("wide")
    n_narrow = lax.axis_size("narrow")
    n_pair = lax.axis_size("pair")
    tokens, features = row_codes.shape
    hidden = w_gate.shape[2]
    tall = features // LANES
    topk = expert_ids.shape[1]
    limit = 16 if n_wide <= 4 else 48

    def block(*lead):
        return jax.ShapeDtypeStruct(lead + (tall, LANES), BF16)

    shared = [shared_gate, shared_up, shared_down]
    routed = [
        w_gate.reshape(features, hidden),
        w_up.reshape(features, hidden),
        w_down.reshape(hidden, features),
    ]
    near, *far = call(
        dispatch_kernel,
        "dispatch",
        in_hbm(expert_ids.T, placement, gate_weights.T, row_codes, row_scales)
        + in_hbm(*shared, *routed),
        [ASPEC] * 11,
        [block(tokens + 1)]
        + [block(CAP)] * (n_wide - 1)
        + [pltpu.SMEM((topk, tokens), jnp.int32), pltpu.SMEM((topk, tokens), F32)],
        [
            pltpu.SMEM((topk, tokens), jnp.int32),
            pltpu.SMEM(placement.shape, jnp.int32),
            pltpu.SMEM((topk, tokens), F32),
            VMEM((tokens, features), BF16),
            VMEM(row_scales.shape, BF16),
            VMEM((tokens * tall, LANES), F32),
            VMEM((n_wide * CAP, tall, LANES), F32),
            pltpu.SemaphoreType.DMA((5,)),
        ],
    )
    far, (route, gains) = far[:-2], far[-2:]
    order = list(range(n_wide - 1, 0, -1))
    far = [swap(far[k - 1], "wide", k) for k in order]
    near_line = [near] + [swap(near, "narrow", j) for j in range(1, n_narrow)]

    if n_wide > 4:
        far = [jnp.concatenate(far, axis=0)]
    per = len(far)
    slots = far[0].shape[0]
    far_side = []
    for j in range(1, n_narrow):
        far_side += [swap(value, "narrow", j) for value in far]
    near_line = after(near_line, *far)
    near_all = list(near_line)
    for c in range(1, n_pair):
        near_all += [swap(value, "pair", c) for value in near_line]

    near_rows = n_narrow * n_pair * tokens
    near_out = call(
        functools.partial(near_kernel, n_narrow, n_pair),
        "near",
        near_all + list(shared) + list(routed),
        [VSPEC] * (n_narrow * n_pair + 6),
        [block(n_narrow, tokens)] * n_pair,
        [VMEM((near_rows * tall, LANES), F32), VMEM((near_rows, features), BF16)],
        flops=12 * near_rows * features * hidden,
        moved=12 * features * hidden,
        limit=limit,
    )

    def reduce_pair(parts, rows):
        parts = [parts[0]] + [swap(parts[c], "pair", c) for c in range(1, n_pair)]
        parts = call(
            functools.partial(pair_sum_kernel, n_pair),
            "pair_sum",
            parts,
            [VSPEC] * n_pair,
            [block(rows)] * n_narrow,
            [],
            limit=limit,
        )
        return [parts[0]] + [swap(parts[j], "narrow", j) for j in range(1, n_narrow)]

    near_back = reduce_pair(near_out, tokens)
    far_line = list(far) + after(far_side, near_out[0])
    far_all = list(far_line)
    for c in range(1, n_pair):
        far_all += [swap(value, "pair", c) for value in far_line]

    far_rows = n_narrow * n_pair * per * slots
    pass_rows = far_rows if far_rows <= MAX_ROWS else per * slots
    pass_rows = -(-pass_rows // 16) * 16
    far_out = call(
        functools.partial(far_kernel, n_narrow, n_pair, per),
        "far",
        far_all + list(routed),
        [VSPEC] * (n_narrow * n_pair * per + 3),
        [block(n_narrow, slots)] * (n_pair * per),
        [VMEM((pass_rows * tall, LANES), F32), VMEM((pass_rows, features), BF16)],
        flops=6 * far_rows * features * hidden,
        moved=6 * features * hidden,
        limit=limit,
    )

    far_back = []
    for k in range(per):
        far_back += call(
            functools.partial(narrow_sum_kernel, n_narrow),
            "narrow_sum",
            reduce_pair(far_out[k::per], slots),
            [VSPEC] * n_narrow,
            [block(CAP)] * (slots // CAP),
            [],
            limit=limit,
        )
    far_back = [swap(value, "wide", k) for k, value in zip(order, far_back)]
    return call(
        functools.partial(combine_kernel, n_narrow, order),
        "combine",
        [route, gains] + near_back + far_back,
        [SSPEC] * 2 + [VSPEC] * (n_narrow + n_wide - 1),
        jax.ShapeDtypeStruct((tokens, features), BF16),
        [
            VMEM((tokens * tall, LANES), F32),
            VMEM((n_wide * CAP, tall, LANES), F32),
        ],
    )


def solution(mesh):
    rows = P(("groups", "wide", "narrow", "pair"), None)
    return jax.shard_map(
        shards,
        mesh=mesh,
        in_specs=(
            rows,
            rows,
            rows,
            rows,
            P(),
            P("wide", None, ("narrow", "pair")),
            P("wide", None, ("narrow", "pair")),
            P("wide", ("narrow", "pair"), None),
            P(None, ("narrow", "pair")),
            P(None, ("narrow", "pair")),
            P(("narrow", "pair"), None),
        ),
        out_specs=rows,
        check_vma=False,
    )
```

```python
import functools

import jax
import jax.numpy as jnp
from jax import lax
from jax.experimental import pallas as pl
from jax.experimental.pallas import tpu as pltpu
from jax.sharding import PartitionSpec as P

CAP = 5
LANES = 128
SPAN = 7
MAX_ROWS = 128

VMEM = pltpu.VMEM
VSPEC = pl.BlockSpec(memory_space=pltpu.VMEM)
SSPEC = pl.BlockSpec(memory_space=pltpu.SMEM)
ASPEC = pl.BlockSpec(memory_space=pl.ANY)
F32 = jnp.float32
BF16 = jnp.bfloat16


def put(flat, at, value, rows):
    tall = flat.shape[0] // rows
    for b in range(value.shape[1] // LANES):
        flat[pl.ds(at // LANES + b, rows, stride=tall), :] = value[
            :, b * LANES : (b + 1) * LANES
        ]


def dispatch_kernel(ids_in, place_in, weights_in, codes_in, scales_in, *refs):
    refs = refs[6:]
    near, far = refs[0], refs[1:-10]
    route, gains = refs[-10:-8]
    ids, place, weights, codes, scales, tok, stage, sems = refs[-8:]
    copies = [
        pltpu.make_async_copy(src, dst, sems.at[i])
        for i, (src, dst) in enumerate(
            (
                (codes_in, codes),
                (scales_in, scales),
                (ids_in, ids),
                (place_in, place),
                (weights_in, weights),
            )
        )
    ]
    for copy in copies:
        copy.start()
    here = lax.axis_index("wide")
    rows, features = codes.shape
    topk = ids.shape[0]
    tall = features // LANES
    stage[...] = jnp.zeros_like(stage)
    for copy in copies:
        copy.wait()
    for b in range(tall):
        block = codes[:, b * LANES : (b + 1) * LANES].astype(F32)
        tok[pl.ds(b, rows, stride=tall), :] = block * scales[:, b : b + 1].astype(F32)
    near[:rows] = tok[...].reshape(rows, tall, LANES).astype(BF16)
    sub = lax.broadcasted_iota(jnp.int32, (rows, LANES), 0)
    lane = lax.broadcasted_iota(jnp.int32, (rows, LANES), 1)
    weight = jnp.zeros((rows, LANES), F32)
    named = []
    for t in range(rows):
        for k in range(topk):
            e = ids[k, t]
            node = place[e]
            slot = jnp.int32(0)
            for other in named[: t * topk]:
                slot = slot + jnp.where(other == e, 1, 0)
            named.append(e)
            at = (node ^ here) * CAP + slot
            route[k, t] = at
            gains[k, t] = weights[k, t]
            weight = jnp.where((sub == t) & (lane == node), weights[k, t], weight)
            stage[at] = tok[t * tall : (t + 1) * tall, :]
    high = weight.astype(BF16).astype(F32)
    middle = (weight - high).astype(BF16).astype(F32)
    low = weight - high - middle
    near[rows] = jnp.concatenate(
        [high, middle, low, jnp.zeros((tall - 3 * rows, LANES), F32)], axis=0
    ).astype(BF16)
    for k, ref in enumerate(far):
        ref[...] = stage[(k + 1) * CAP : (k + 2) * CAP].astype(BF16)


def unpack(refs, blocks, rows, flat, inputs):
    tall = inputs.shape[1] // LANES
    at = 0
    for ref, count in zip(refs, blocks):
        flat[at * tall : (at + count) * tall, :] = (
            ref[:count].astype(F32).reshape(count * tall, LANES)
        )
        at += count
    if at < rows:
        flat[at * tall : rows * tall, :] = jnp.zeros(((rows - at) * tall, LANES), F32)
    for b in range(tall):
        inputs[:rows, b * LANES : (b + 1) * LANES] = flat[
            pl.ds(b, rows, stride=tall), :
        ].astype(BF16)


def silu_mul(gate, up):
    return (gate / (1.0 + jnp.exp(-gate)) * up).astype(BF16)


def near_shared_kernel(*refs):
    count = len(refs) - 7
    arrived, (gate_w, up_w, down_w), outs = refs[:count], refs[count : count + 3], refs[-4:]
    inputs, weight, value, flat = outs
    here = lax.axis_index("wide")
    tokens, tall = arrived[0].shape[0] - 1, arrived[0].shape[1]
    rows = count * tokens
    unpack(arrived, [tokens] * count, rows, flat, inputs)
    for i, ref in enumerate(arrived):
        parts = ref[tokens].astype(F32)
        whole = (
            parts[:tokens] + parts[tokens : 2 * tokens] + parts[2 * tokens : 3 * tokens]
        )
        lane = lax.broadcasted_iota(jnp.int32, whole.shape, 1)
        gain = jnp.sum(jnp.where(lane == here, whole, 0.0), axis=1, keepdims=True)
        weight[i * tokens : (i + 1) * tokens, :] = jnp.broadcast_to(gain, whole.shape)
    x = inputs[...]
    gate = jnp.dot(x, gate_w[...], preferred_element_type=F32)
    up = jnp.dot(x, up_w[...], preferred_element_type=F32)
    hidden = silu_mul(gate, up)
    for first in range(0, tall * LANES, SPAN * LANES):
        at = slice(first, first + SPAN * LANES)
        value[:, at] = jnp.dot(hidden, down_w[:, at], preferred_element_type=F32)


def near_routed_kernel(n_narrow, n_pair, inputs, weight, value, gate_w, up_w, down_w, *refs):
    outs, flat = refs[:n_pair], refs[n_pair]
    rows, features = inputs.shape
    tall = features // LANES
    tokens = rows // (n_narrow * n_pair)
    x = inputs[...]
    gate = jnp.dot(x, gate_w[...], preferred_element_type=F32)
    up = jnp.dot(x, up_w[...], preferred_element_type=F32)
    hidden = silu_mul(gate, up)
    gain = weight[:, :1]
    for first in range(0, features, SPAN * LANES):
        at = slice(first, first + SPAN * LANES)
        routed = jnp.dot(hidden, down_w[:, at], preferred_element_type=F32)
        put(flat, first, value[:, at] + gain * routed, rows)
    each = n_narrow * tokens
    for c in range(n_pair):
        part = flat[c * each * tall : (c + 1) * each * tall, :]
        outs[c][...] = part.reshape(n_narrow, tokens, tall, LANES).astype(BF16)


def far_kernel(n_narrow, n_pair, per, *refs):
    count = n_narrow * n_pair * per
    arrived, rest = refs[:count], refs[count:]
    gate_w, up_w, down_w = rest[:3]
    outs = rest[3 : 3 + n_pair * per]
    flat, inputs = rest[3 + n_pair * per :]
    tall = arrived[0].shape[1]
    blocks = [ref.shape[0] for ref in arrived]
    step = count if sum(blocks) <= MAX_ROWS else per
    for first in range(0, count, step):
        group = blocks[first : first + step]
        rows = -(-sum(group) // 16) * 16
        unpack(arrived[first : first + step], group, rows, flat, inputs)
        x = inputs[:rows]
        gate = jnp.dot(x, gate_w[...], preferred_element_type=F32)
        up = jnp.dot(x, up_w[...], preferred_element_type=F32)
        hidden = silu_mul(gate, up)
        for at in range(0, tall * LANES, SPAN * LANES):
            value = jnp.dot(
                hidden, down_w[:, at : at + SPAN * LANES], preferred_element_type=F32
            )
            put(flat, at, value, rows)
        at = 0
        for i, slots in enumerate(group):
            line, k = divmod(first + i, per)
            c, j = divmod(line, n_narrow)
            part = flat[at * tall : (at + slots) * tall, :]
            outs[c * per + k][j] = part.reshape(slots, tall, LANES).astype(BF16)
            at += slots


def pair_sum_kernel(n_pair, *refs):
    parts, outs = refs[:n_pair], refs[n_pair:]
    for j, out in enumerate(outs):
        total = parts[0][j].astype(F32)
        for ref in parts[1:]:
            total = total + ref[j].astype(F32)
        out[...] = total.astype(BF16)


def narrow_sum_kernel(n_narrow, *refs):
    parts, outs = refs[:n_narrow], refs[n_narrow:]
    at = 0
    for out in outs:
        rows = slice(at, at + out.shape[0])
        total = parts[0][rows].astype(F32)
        for ref in parts[1:]:
            total = total + ref[rows].astype(F32)
        out[...] = total.astype(BF16)
        at += out.shape[0]


def combine_kernel(n_narrow, order, route, gains, *refs):
    near, rest = refs[:n_narrow], refs[n_narrow:]
    far, (out, total, stage) = rest[:-3], rest[-3:]
    rows, features = out.shape
    tall = features // LANES
    topk = route.shape[0]
    stage[:CAP] = jnp.zeros((CAP, tall, LANES), F32)
    for k, ref in zip(order, far):
        stage[k * CAP : (k + 1) * CAP] = ref[...].astype(F32)
    for t in range(rows):
        value = near[0][t].astype(F32)
        for ref in near[1:]:
            value = value + ref[t].astype(F32)
        for k in range(topk):
            value = value + gains[k, t] * stage[route[k, t]]
        total[t * tall : (t + 1) * tall, :] = value
    for b in range(tall):
        out[:, b * LANES : (b + 1) * LANES] = total[
            pl.ds(b, rows, stride=tall), :
        ].astype(BF16)


def swap(value, axis, offset):
    size = lax.axis_size(axis)
    return lax.ppermute(value, axis, [(i, i ^ offset) for i in range(size)])


def in_hbm(*values):
    return [pltpu.with_memory_space_constraint(value, pltpu.HBM) for value in values]


def after(values, *others):
    return list(lax.optimization_barrier((tuple(values), others))[0])


def call(kernel, name, ins, specs, outs, scratch, flops=0, moved=0, limit=16):
    return pl.pallas_call(
        kernel,
        out_shape=outs,
        in_specs=specs,
        out_specs=jax.tree.map(
            lambda out: SSPEC if getattr(out, "memory_space", None) == pltpu.SMEM else VSPEC,
            outs,
        ),
        scratch_shapes=scratch,
        compiler_params=pltpu.CompilerParams(vmem_limit_bytes=limit << 20),
        cost_estimate=pl.CostEstimate(flops=flops, bytes_accessed=moved, transcendentals=0),
        name=name,
    )(*ins)


def shards(
    row_codes,
    row_scales,
    expert_ids,
    gate_weights,
    placement,
    w_gate,
    w_up,
    w_down,
    shared_gate,
    shared_up,
    shared_down,
):
    n_wide = lax.axis_size("wide")
    n_narrow = lax.axis_size("narrow")
    n_pair = lax.axis_size("pair")
    tokens, features = row_codes.shape
    hidden = w_gate.shape[2]
    tall = features // LANES
    topk = expert_ids.shape[1]
    limit = 16 if n_wide <= 4 else 48

    def block(*lead):
        return jax.ShapeDtypeStruct(lead + (tall, LANES), BF16)

    shared = [shared_gate, shared_up, shared_down]
    routed = [
        w_gate.reshape(features, hidden),
        w_up.reshape(features, hidden),
        w_down.reshape(hidden, features),
    ]
    near, *far = call(
        dispatch_kernel,
        "dispatch",
        in_hbm(expert_ids.T, placement, gate_weights.T, row_codes, row_scales)
        + in_hbm(*shared, *routed),
        [ASPEC] * 11,
        [block(tokens + 1)]
        + [block(CAP)] * (n_wide - 1)
        + [pltpu.SMEM((topk, tokens), jnp.int32), pltpu.SMEM((topk, tokens), F32)],
        [
            pltpu.SMEM((topk, tokens), jnp.int32),
            pltpu.SMEM(placement.shape, jnp.int32),
            pltpu.SMEM((topk, tokens), F32),
            VMEM((tokens, features), BF16),
            VMEM(row_scales.shape, BF16),
            VMEM((tokens * tall, LANES), F32),
            VMEM((n_wide * CAP, tall, LANES), F32),
            pltpu.SemaphoreType.DMA((5,)),
        ],
    )
    far, (route, gains) = far[:-2], far[-2:]
    order = list(range(n_wide - 1, 0, -1))
    far = [swap(far[k - 1], "wide", k) for k in order]
    beside = ("narrow", "pair")
    near_all = [
        swap(near, beside, j * n_pair + c) if j + c else near
        for c in range(n_pair)
        for j in range(n_narrow)
    ]
    if n_wide > 4:
        far = [jnp.concatenate(far, axis=0)]
    per = len(far)
    slots = far[0].shape[0]

    near_rows = n_narrow * n_pair * tokens
    near_mid = call(
        near_shared_kernel,
        "near_shared",
        near_all + shared,
        [VSPEC] * (n_narrow * n_pair + 3),
        [
            jax.ShapeDtypeStruct((near_rows, features), BF16),
            jax.ShapeDtypeStruct((near_rows, LANES), F32),
            jax.ShapeDtypeStruct((near_rows, features), F32),
        ],
        [VMEM((near_rows * tall, LANES), F32)],
        flops=6 * near_rows * features * hidden,
        moved=6 * features * hidden,
        limit=limit,
    )
    far = after(far, near_mid[1])
    far_side = []
    for j in range(1, n_narrow):
        far_side += [swap(value, "narrow", j) for value in far]
    near_out = call(
        functools.partial(near_routed_kernel, n_narrow, n_pair),
        "near_routed",
        after(near_mid, *far) + routed,
        [VSPEC] * 6,
        [block(n_narrow, tokens)] * n_pair,
        [VMEM((near_rows * tall, LANES), F32)],
        flops=6 * near_rows * features * hidden,
        moved=6 * features * hidden,
        limit=limit,
    )
    far_line = list(far) + after(far_side, near_out[0])
    far_all = list(far_line)
    for c in range(1, n_pair):
        far_all += [swap(value, "pair", c) for value in far_line]

    far_rows = n_narrow * n_pair * per * slots
    pass_rows = far_rows if far_rows <= MAX_ROWS else per * slots
    pass_rows = -(-pass_rows // 16) * 16
    far_out = call(
        functools.partial(far_kernel, n_narrow, n_pair, per),
        "far",
        far_all + list(routed),
        [VSPEC] * (n_narrow * n_pair * per + 3),
        [block(n_narrow, slots)] * (n_pair * per),
        [VMEM((pass_rows * tall, LANES), F32), VMEM((pass_rows, features), BF16)],
        flops=6 * far_rows * features * hidden,
        moved=6 * features * hidden,
        limit=limit,
    )

    def reduce_pair(parts, rows):
        parts = [parts[0]] + [swap(parts[c], "pair", c) for c in range(1, n_pair)]
        parts = call(
            functools.partial(pair_sum_kernel, n_pair),
            "pair_sum",
            parts,
            [VSPEC] * n_pair,
            [block(rows)] * n_narrow,
            [],
            limit=limit,
        )
        return [parts[0]] + [swap(parts[j], "narrow", j) for j in range(1, n_narrow)]

    far_back = []
    for k in range(per):
        far_back += call(
            functools.partial(narrow_sum_kernel, n_narrow),
            "narrow_sum",
            reduce_pair(far_out[k::per], slots),
            [VSPEC] * n_narrow,
            [block(CAP)] * (slots // CAP),
            [],
            limit=limit,
        )
    near_back = reduce_pair(near_out, tokens)
    far_back = [swap(value, "wide", k) for k, value in zip(order, far_back)]
    return call(
        functools.partial(combine_kernel, n_narrow, order),
        "combine",
        [route, gains] + near_back + far_back,
        [SSPEC] * 2 + [VSPEC] * (n_narrow + n_wide - 1),
        jax.ShapeDtypeStruct((tokens, features), BF16),
        [
            VMEM((tokens * tall, LANES), F32),
            VMEM((n_wide * CAP, tall, LANES), F32),
        ],
    )


def solution(mesh):
    rows = P(("groups", "wide", "narrow", "pair"), None)
    return jax.shard_map(
        shards,
        mesh=mesh,
        in_specs=(
            rows,
            rows,
            rows,
            rows,
            P(),
            P("wide", None, ("narrow", "pair")),
            P("wide", None, ("narrow", "pair")),
            P("wide", ("narrow", "pair"), None),
            P(None, ("narrow", "pair")),
            P(None, ("narrow", "pair")),
            P(("narrow", "pair"), None),
        ),
        out_specs=rows,
        check_vma=False,
    )
```

```python
import functools

import jax
import jax.numpy as jnp
from jax import lax
from jax.experimental import pallas as pl
from jax.experimental.pallas import tpu as pltpu
from jax.sharding import PartitionSpec as P

CAP = 5
LANES = 128
SPAN = 7
MAX_ROWS = 128

VMEM = pltpu.VMEM
VSPEC = pl.BlockSpec(memory_space=pltpu.VMEM)
SSPEC = pl.BlockSpec(memory_space=pltpu.SMEM)
ASPEC = pl.BlockSpec(memory_space=pl.ANY)
F32 = jnp.float32
BF16 = jnp.bfloat16


def put(flat, at, value, tall):
    rows = value.shape[0]
    for b in range(value.shape[1] // LANES):
        flat[pl.ds(at // LANES + b, rows, stride=tall), :] = value[
            :, b * LANES : (b + 1) * LANES
        ]


def dispatch_kernel(ids_in, place_in, weights_in, codes_in, scales_in, *refs):
    refs = refs[6:]
    near, far = refs[0], refs[1:-10]
    route, gains = refs[-10:-8]
    ids, place, weights, codes, scales, tok, stage, sems = refs[-8:]
    copies = [
        pltpu.make_async_copy(src, dst, sems.at[i])
        for i, (src, dst) in enumerate(
            (
                (codes_in, codes),
                (scales_in, scales),
                (ids_in, ids),
                (place_in, place),
                (weights_in, weights),
            )
        )
    ]
    for copy in copies:
        copy.start()
    here = lax.axis_index("wide")
    rows, features = codes.shape
    topk = ids.shape[0]
    tall = features // LANES
    stage[...] = jnp.zeros_like(stage)
    for copy in copies:
        copy.wait()
    for b in range(tall):
        block = codes[:, b * LANES : (b + 1) * LANES].astype(F32)
        tok[pl.ds(b, rows, stride=tall), :] = block * scales[:, b : b + 1].astype(F32)
    near[:rows] = tok[...].reshape(rows, tall, LANES).astype(BF16)
    sub = lax.broadcasted_iota(jnp.int32, (rows, LANES), 0)
    lane = lax.broadcasted_iota(jnp.int32, (rows, LANES), 1)
    weight = jnp.zeros((rows, LANES), F32)
    named = []
    for t in range(rows):
        for k in range(topk):
            e = ids[k, t]
            node = place[e]
            slot = jnp.int32(0)
            for other in named[: t * topk]:
                slot = slot + jnp.where(other == e, 1, 0)
            named.append(e)
            at = (node ^ here) * CAP + slot
            route[k, t] = at
            gains[k, t] = weights[k, t]
            weight = jnp.where((sub == t) & (lane == node), weights[k, t], weight)
            stage[at] = tok[t * tall : (t + 1) * tall, :]
    high = weight.astype(BF16).astype(F32)
    middle = (weight - high).astype(BF16).astype(F32)
    low = weight - high - middle
    near[rows] = jnp.concatenate(
        [high, middle, low, jnp.zeros((tall - 3 * rows, LANES), F32)], axis=0
    ).astype(BF16)
    for k, ref in enumerate(far):
        ref[...] = stage[(k + 1) * CAP : (k + 2) * CAP].astype(BF16)


def unpack(refs, blocks, rows, flat, inputs, first=0):
    tall = inputs.shape[1] // LANES
    at = 0
    for ref, count in zip(refs, blocks):
        flat[at * tall : (at + count) * tall, :] = (
            ref[:count].astype(F32).reshape(count * tall, LANES)
        )
        at += count
    if at < rows:
        flat[at * tall : rows * tall, :] = jnp.zeros(((rows - at) * tall, LANES), F32)
    for b in range(tall):
        inputs[first : first + rows, b * LANES : (b + 1) * LANES] = flat[
            pl.ds(b, rows, stride=tall), :
        ].astype(BF16)


def silu_mul(gate, up):
    return (gate / (1.0 + jnp.exp(-gate)) * up).astype(BF16)


def near_shared_kernel(*refs):
    count = len(refs) - 7
    arrived, (gate_w, up_w, down_w), outs = refs[:count], refs[count : count + 3], refs[-4:]
    inputs, weight, value, flat = outs
    here = lax.axis_index("wide")
    tokens, tall = arrived[0].shape[0] - 1, arrived[0].shape[1]
    rows = count * tokens
    unpack(arrived, [tokens] * count, rows, flat, inputs)
    for i, ref in enumerate(arrived):
        parts = ref[tokens].astype(F32)
        whole = (
            parts[:tokens] + parts[tokens : 2 * tokens] + parts[2 * tokens : 3 * tokens]
        )
        lane = lax.broadcasted_iota(jnp.int32, whole.shape, 1)
        gain = jnp.sum(jnp.where(lane == here, whole, 0.0), axis=1, keepdims=True)
        weight[i * tokens : (i + 1) * tokens, :] = jnp.broadcast_to(gain, whole.shape)
    x = inputs[...]
    gate = jnp.dot(x, gate_w[...], preferred_element_type=F32)
    up = jnp.dot(x, up_w[...], preferred_element_type=F32)
    hidden = silu_mul(gate, up)
    for first in range(0, tall * LANES, SPAN * LANES):
        at = slice(first, first + SPAN * LANES)
        value[:, at] = jnp.dot(hidden, down_w[:, at], preferred_element_type=F32)


def routed_kernel(n_narrow, n_pair, per, *refs):
    count = n_narrow * n_pair * per
    arrived, rest = refs[:count], refs[count:]
    near, weight, value, gate_w, up_w, down_w = rest[:6]
    near_outs, outs = rest[6 : 6 + n_pair], rest[6 + n_pair : -2]
    flat, inputs = rest[-2:]
    tall = arrived[0].shape[1]
    near_rows = near.shape[0]
    each = near_rows // n_pair
    blocks = [ref.shape[0] for ref in arrived]
    step = count if sum(blocks) <= MAX_ROWS else per
    for first in range(0, count, step):
        group = blocks[first : first + step]
        head = 0 if first else near_rows
        rows = -(-sum(group) // 16) * 16
        unpack(arrived[first : first + step], group, rows, flat, inputs, head)
        if head:
            inputs[:head] = near[...]
        x = inputs[: head + rows]
        gate = jnp.dot(x, gate_w[...], preferred_element_type=F32)
        up = jnp.dot(x, up_w[...], preferred_element_type=F32)
        hidden = silu_mul(gate, up)
        for at in range(0, tall * LANES, SPAN * LANES):
            part = jnp.dot(
                hidden, down_w[:, at : at + SPAN * LANES], preferred_element_type=F32
            )
            if head:
                part = jnp.concatenate(
                    [
                        value[:, at : at + SPAN * LANES] + weight[:, :1] * part[:head],
                        part[head:],
                    ],
                    axis=0,
                )
            put(flat, at, part, tall)
        if head:
            for c in range(n_pair):
                part = flat[c * each * tall : (c + 1) * each * tall, :]
                near_outs[c][...] = part.reshape(near_outs[c].shape).astype(BF16)
        at = head
        for i, slots in enumerate(group):
            line, k = divmod(first + i, per)
            c, j = divmod(line, n_narrow)
            part = flat[at * tall : (at + slots) * tall, :]
            outs[c * per + k][j] = part.reshape(slots, tall, LANES).astype(BF16)
            at += slots


def pair_sum_kernel(n_pair, *refs):
    parts, outs = refs[:n_pair], refs[n_pair:]
    for j, out in enumerate(outs):
        total = parts[0][j].astype(F32)
        for ref in parts[1:]:
            total = total + ref[j].astype(F32)
        out[...] = total.astype(BF16)


def narrow_sum_kernel(n_narrow, *refs):
    parts, outs = refs[:n_narrow], refs[n_narrow:]
    at = 0
    for out in outs:
        rows = slice(at, at + out.shape[0])
        total = parts[0][rows].astype(F32)
        for ref in parts[1:]:
            total = total + ref[rows].astype(F32)
        out[...] = total.astype(BF16)
        at += out.shape[0]


def combine_kernel(n_narrow, order, route, gains, *refs):
    near, rest = refs[:n_narrow], refs[n_narrow:]
    far, direct = rest[: len(order)], rest[len(order) : -3]
    out, total, stage = rest[-3:]
    rows, features = out.shape
    tall = features // LANES
    topk = route.shape[0]
    stage[:CAP] = jnp.zeros((CAP, tall, LANES), F32)
    for k, ref in zip(order, far):
        stage[k * CAP : (k + 1) * CAP] = ref[...].astype(F32)
    arrived = direct[0][...].astype(F32)
    for ref in direct[1:]:
        arrived = arrived + ref[...].astype(F32)
    stage[CAP : 2 * CAP] = arrived
    for t in range(rows):
        value = near[0][t].astype(F32)
        for ref in near[1:]:
            value = value + ref[t].astype(F32)
        for k in range(topk):
            value = value + gains[k, t] * stage[route[k, t]]
        total[t * tall : (t + 1) * tall, :] = value
    for b in range(tall):
        out[:, b * LANES : (b + 1) * LANES] = total[
            pl.ds(b, rows, stride=tall), :
        ].astype(BF16)


def swap(value, axis, offset):
    size = lax.axis_size(axis)
    return lax.ppermute(value, axis, [(i, i ^ offset) for i in range(size)])


def in_hbm(*values):
    return [pltpu.with_memory_space_constraint(value, pltpu.HBM) for value in values]


def after(values, *others):
    return list(lax.optimization_barrier((tuple(values), others))[0])


def call(kernel, name, ins, specs, outs, scratch, flops=0, moved=0, limit=16):
    return pl.pallas_call(
        kernel,
        out_shape=outs,
        in_specs=specs,
        out_specs=jax.tree.map(
            lambda out: SSPEC if getattr(out, "memory_space", None) == pltpu.SMEM else VSPEC,
            outs,
        ),
        scratch_shapes=scratch,
        compiler_params=pltpu.CompilerParams(vmem_limit_bytes=limit << 20),
        cost_estimate=pl.CostEstimate(flops=flops, bytes_accessed=moved, transcendentals=0),
        name=name,
    )(*ins)


def shards(
    row_codes,
    row_scales,
    expert_ids,
    gate_weights,
    placement,
    w_gate,
    w_up,
    w_down,
    shared_gate,
    shared_up,
    shared_down,
):
    n_wide = lax.axis_size("wide")
    n_narrow = lax.axis_size("narrow")
    n_pair = lax.axis_size("pair")
    tokens, features = row_codes.shape
    hidden = w_gate.shape[2]
    tall = features // LANES
    topk = expert_ids.shape[1]
    limit = 16 if n_wide <= 4 else 48

    def block(*lead):
        return jax.ShapeDtypeStruct(lead + (tall, LANES), BF16)

    shared = [shared_gate, shared_up, shared_down]
    routed = [
        w_gate.reshape(features, hidden),
        w_up.reshape(features, hidden),
        w_down.reshape(hidden, features),
    ]
    near, *far = call(
        dispatch_kernel,
        "dispatch",
        in_hbm(expert_ids.T, placement, gate_weights.T, row_codes, row_scales)
        + in_hbm(*shared, *routed),
        [ASPEC] * 11,
        [block(tokens + 1)]
        + [block(CAP)] * (n_wide - 1)
        + [pltpu.SMEM((topk, tokens), jnp.int32), pltpu.SMEM((topk, tokens), F32)],
        [
            pltpu.SMEM((topk, tokens), jnp.int32),
            pltpu.SMEM(placement.shape, jnp.int32),
            pltpu.SMEM((topk, tokens), F32),
            VMEM((tokens, features), BF16),
            VMEM(row_scales.shape, BF16),
            VMEM((tokens * tall, LANES), F32),
            VMEM((n_wide * CAP, tall, LANES), F32),
            pltpu.SemaphoreType.DMA((5,)),
        ],
    )
    far, (route, gains) = far[:-2], far[-2:]
    order = list(range(n_wide - 1, 1, -1))
    across = ("wide", "narrow")
    bundles = [swap(far[k - 1], "wide", k) for k in order]
    direct = [swap(far[0], across, n_narrow + j) for j in range(n_narrow)]
    near_line = [near] + [swap(near, "narrow", j) for j in range(1, n_narrow)]
    bundles = after(bundles, *direct)
    if n_wide > 4:
        bundles = [jnp.concatenate(bundles, axis=0)]
    lines = [list(bundles)]
    for j in range(1, n_narrow):
        lines.append([swap(value, "narrow", j) for value in bundles])
    per = len(bundles) + 1
    slots = [value.shape[0] for value in bundles] + [CAP]
    near_line = after(near_line, *bundles)
    near_all = list(near_line)
    for c in range(1, n_pair):
        near_all += [swap(value, "pair", c) for value in near_line]

    near_rows = n_narrow * n_pair * tokens
    near_mid = call(
        near_shared_kernel,
        "near_shared",
        near_all + shared,
        [VSPEC] * (n_narrow * n_pair + 3),
        [
            jax.ShapeDtypeStruct((near_rows, features), BF16),
            jax.ShapeDtypeStruct((near_rows, LANES), F32),
            jax.ShapeDtypeStruct((near_rows, features), F32),
        ],
        [VMEM((near_rows * tall, LANES), F32)],
        flops=6 * near_rows * features * hidden,
        moved=6 * features * hidden,
        limit=limit,
    )
    side = after([value for line in lines[1:] for value in line], near_mid[1])
    far_line = []
    for j in range(n_narrow):
        far_line += lines[0] if j == 0 else side[(j - 1) * (per - 1) : j * (per - 1)]
        far_line.append(direct[j])
    far_all = list(far_line)
    for c in range(1, n_pair):
        far_all += [swap(value, "pair", c) for value in far_line]

    far_rows = n_narrow * n_pair * sum(slots)
    pass_rows = far_rows if far_rows <= MAX_ROWS else sum(slots)
    pass_rows = near_rows + -(-pass_rows // 16) * 16
    outs = call(
        functools.partial(routed_kernel, n_narrow, n_pair, per),
        "routed",
        far_all + list(near_mid) + routed,
        [VSPEC] * (n_narrow * n_pair * per + 6),
        [block(n_narrow, tokens)] * n_pair
        + [block(n_narrow, count) for count in slots] * n_pair,
        [VMEM((pass_rows * tall, LANES), F32), VMEM((pass_rows, features), BF16)],
        flops=6 * (near_rows + far_rows) * features * hidden,
        moved=6 * features * hidden,
        limit=limit,
    )
    near_out, far_out = outs[:n_pair], outs[n_pair:]

    def reduce_pair(parts, *first):
        rows = parts[0].shape[1]
        return call(
            functools.partial(pair_sum_kernel, n_pair),
            "pair_sum",
            after([parts[0]] + [swap(parts[c], "pair", c) for c in range(1, n_pair)], *first),
            [VSPEC] * n_pair,
            [block(rows)] * n_narrow,
            [],
            limit=limit,
        )

    def send_narrow(parts):
        return [parts[0]] + [swap(parts[j], "narrow", j) for j in range(1, n_narrow)]

    far_back = []
    for k in range(per - 1):
        far_back += call(
            functools.partial(narrow_sum_kernel, n_narrow),
            "narrow_sum",
            send_narrow(reduce_pair(far_out[k::per])),
            [VSPEC] * n_narrow,
            [block(CAP)] * (slots[k] // CAP),
            [],
            limit=limit,
        )
    sums = far_back
    far_back = [swap(value, "wide", k) for k, value in zip(order, far_back)]
    direct_back = reduce_pair(far_out[per - 1 :: per], sums[0])
    near_back = send_narrow(reduce_pair(near_out))
    direct_back = [
        swap(value, across, n_narrow + j) for j, value in enumerate(direct_back)
    ]
    return call(
        functools.partial(combine_kernel, n_narrow, order),
        "combine",
        [route, gains] + near_back + far_back + direct_back,
        [SSPEC] * 2 + [VSPEC] * (2 * n_narrow + len(order)),
        jax.ShapeDtypeStruct((tokens, features), BF16),
        [
            VMEM((tokens * tall, LANES), F32),
            VMEM((n_wide * CAP, tall, LANES), F32),
        ],
    )


def solution(mesh):
    rows = P(("groups", "wide", "narrow", "pair"), None)
    return jax.shard_map(
        shards,
        mesh=mesh,
        in_specs=(
            rows,
            rows,
            rows,
            rows,
            P(),
            P("wide", None, ("narrow", "pair")),
            P("wide", None, ("narrow", "pair")),
            P("wide", ("narrow", "pair"), None),
            P(None, ("narrow", "pair")),
            P(None, ("narrow", "pair")),
            P(("narrow", "pair"), None),
        ),
        out_specs=rows,
        check_vma=False,
    )
```

```python
import functools

import jax
import jax.numpy as jnp
from jax import lax
from jax.experimental import pallas as pl
from jax.experimental.pallas import tpu as pltpu
from jax.sharding import PartitionSpec as P

CAP = 5
LANES = 128
SPAN = 7
HALVES = 2
MAX_ROWS = 128

VMEM = pltpu.VMEM
VSPEC = pl.BlockSpec(memory_space=pltpu.VMEM)
SSPEC = pl.BlockSpec(memory_space=pltpu.SMEM)
ASPEC = pl.BlockSpec(memory_space=pl.ANY)
F32 = jnp.float32
BF16 = jnp.bfloat16


def put(flat, at, value, tall):
    rows = value.shape[0]
    for b in range(value.shape[1] // LANES):
        flat[pl.ds(at // LANES + b, rows, stride=tall), :] = value[
            :, b * LANES : (b + 1) * LANES
        ]


def dispatch_kernel(ids_in, place_in, weights_in, codes_in, scales_in, *refs):
    refs = refs[6:]
    near, far = refs[0], refs[1:-10]
    route, gains = refs[-10:-8]
    ids, place, weights, codes, scales, tok, stage, sems = refs[-8:]
    copies = [
        pltpu.make_async_copy(src, dst, sems.at[i])
        for i, (src, dst) in enumerate(
            (
                (codes_in, codes),
                (scales_in, scales),
                (ids_in, ids),
                (place_in, place),
                (weights_in, weights),
            )
        )
    ]
    for copy in copies:
        copy.start()
    here = lax.axis_index("wide")
    rows, features = codes.shape
    topk = ids.shape[0]
    tall = features // LANES
    stage[...] = jnp.zeros_like(stage)
    for copy in copies:
        copy.wait()
    for b in range(tall):
        block = codes[:, b * LANES : (b + 1) * LANES].astype(F32)
        tok[pl.ds(b, rows, stride=tall), :] = block * scales[:, b : b + 1].astype(F32)
    near[:rows] = tok[...].reshape(rows, tall, LANES).astype(BF16)
    sub = lax.broadcasted_iota(jnp.int32, (rows, LANES), 0)
    lane = lax.broadcasted_iota(jnp.int32, (rows, LANES), 1)
    weight = jnp.zeros((rows, LANES), F32)
    named = []
    for t in range(rows):
        for k in range(topk):
            e = ids[k, t]
            node = place[e]
            slot = jnp.int32(0)
            for other in named[: t * topk]:
                slot = slot + jnp.where(other == e, 1, 0)
            named.append(e)
            at = (node ^ here) * CAP + slot
            route[k, t] = at
            gains[k, t] = weights[k, t]
            weight = jnp.where((sub == t) & (lane == node), weights[k, t], weight)
            stage[at] = tok[t * tall : (t + 1) * tall, :]
    high = weight.astype(BF16).astype(F32)
    middle = (weight - high).astype(BF16).astype(F32)
    low = weight - high - middle
    near[rows] = jnp.concatenate(
        [high, middle, low, jnp.zeros((tall - 3 * rows, LANES), F32)], axis=0
    ).astype(BF16)
    for k, ref in enumerate(far):
        ref[...] = stage[(k + 1) * CAP : (k + 2) * CAP].astype(BF16)


def unpack(refs, blocks, rows, flat, inputs, first=0):
    tall = inputs.shape[1] // LANES
    at = 0
    for ref, count in zip(refs, blocks):
        flat[at * tall : (at + count) * tall, :] = (
            ref[:count].astype(F32).reshape(count * tall, LANES)
        )
        at += count
    if at < rows:
        flat[at * tall : rows * tall, :] = jnp.zeros(((rows - at) * tall, LANES), F32)
    for b in range(tall):
        inputs[first : first + rows, b * LANES : (b + 1) * LANES] = flat[
            pl.ds(b, rows, stride=tall), :
        ].astype(BF16)


def silu_mul(gate, up):
    return (gate / (1.0 + jnp.exp(-gate)) * up).astype(BF16)


def near_shared_kernel(*refs):
    count = len(refs) - 7
    arrived, (gate_w, up_w, down_w), outs = refs[:count], refs[count : count + 3], refs[-4:]
    inputs, weight, value, flat = outs
    here = lax.axis_index("wide")
    tokens, tall = arrived[0].shape[0] - 1, arrived[0].shape[1]
    rows = count * tokens
    unpack(arrived, [tokens] * count, rows, flat, inputs)
    for i, ref in enumerate(arrived):
        parts = ref[tokens].astype(F32)
        whole = (
            parts[:tokens] + parts[tokens : 2 * tokens] + parts[2 * tokens : 3 * tokens]
        )
        lane = lax.broadcasted_iota(jnp.int32, whole.shape, 1)
        gain = jnp.sum(jnp.where(lane == here, whole, 0.0), axis=1, keepdims=True)
        weight[i * tokens : (i + 1) * tokens, :] = jnp.broadcast_to(gain, whole.shape)
    x = inputs[...]
    gate = jnp.dot(x, gate_w[...], preferred_element_type=F32)
    up = jnp.dot(x, up_w[...], preferred_element_type=F32)
    hidden = silu_mul(gate, up)
    for first in range(0, tall * LANES, SPAN * LANES):
        at = slice(first, first + SPAN * LANES)
        value[:, at] = jnp.dot(hidden, down_w[:, at], preferred_element_type=F32)


def routed_kernel(n_narrow, n_pair, per, *refs):
    count = n_narrow * n_pair * per
    arrived, rest = refs[:count], refs[count:]
    near, weight, value, gate_w, up_w, down_w = rest[:6]
    near_outs, outs = rest[6 : 6 + n_pair], rest[6 + n_pair : -2]
    flat, inputs = rest[-2:]
    tall = arrived[0].shape[1]
    near_rows = near.shape[0]
    each = near_rows // n_pair
    blocks = [ref.shape[0] for ref in arrived]
    step = count if sum(blocks) <= MAX_ROWS else per
    for first in range(0, count, step):
        group = blocks[first : first + step]
        head = 0 if first else near_rows
        rows = -(-sum(group) // 16) * 16
        unpack(arrived[first : first + step], group, rows, flat, inputs, head)
        if head:
            inputs[:head] = near[...]
        x = inputs[: head + rows]
        gate = jnp.dot(x, gate_w[...], preferred_element_type=F32)
        up = jnp.dot(x, up_w[...], preferred_element_type=F32)
        hidden = silu_mul(gate, up)
        for at in range(0, tall * LANES, SPAN * LANES):
            part = jnp.dot(
                hidden, down_w[:, at : at + SPAN * LANES], preferred_element_type=F32
            )
            if head:
                part = jnp.concatenate(
                    [
                        value[:, at : at + SPAN * LANES] + weight[:, :1] * part[:head],
                        part[head:],
                    ],
                    axis=0,
                )
            put(flat, at, part, tall)
        if head:
            for c in range(n_pair):
                part = flat[c * each * tall : (c + 1) * each * tall, :]
                near_outs[c][...] = part.reshape(near_outs[c].shape).astype(BF16)
        at = head
        for i, slots in enumerate(group):
            line, k = divmod(first + i, per)
            c, j = divmod(line, n_narrow)
            part = flat[at * tall : (at + slots) * tall, :]
            outs[c * per + k][j] = part.reshape(slots, tall, LANES).astype(BF16)
            at += slots


def pair_sum_kernel(n_pair, cuts, *refs):
    parts, outs = refs[:n_pair], refs[n_pair:]
    for i, out in enumerate(outs):
        j, cut = divmod(i, cuts)
        rows = slice(cut * out.shape[0], (cut + 1) * out.shape[0])
        total = parts[0][j, rows].astype(F32)
        for ref in parts[1:]:
            total = total + ref[j, rows].astype(F32)
        out[...] = total.astype(BF16)


def narrow_sum_kernel(n_narrow, *refs):
    parts, outs = refs[:n_narrow], refs[n_narrow:]
    at = 0
    for out in outs:
        rows = slice(at, at + out.shape[0])
        total = parts[0][rows].astype(F32)
        for ref in parts[1:]:
            total = total + ref[rows].astype(F32)
        out[...] = total.astype(BF16)
        at += out.shape[0]


def far_combine_kernel(order, route, gains, *refs):
    far, (total, stage) = refs[: len(order)], refs[-2:]
    topk, rows = route.shape
    tall = stage.shape[1]
    stage[: 2 * CAP] = jnp.zeros((2 * CAP, tall, LANES), F32)
    for k, ref in zip(order, far):
        stage[k * CAP : (k + 1) * CAP] = ref[...].astype(F32)
    for t in range(rows):
        value = gains[0, t] * stage[route[0, t]]
        for k in range(1, topk):
            value = value + gains[k, t] * stage[route[k, t]]
        total[t] = value


def combine_kernel(n_narrow, route, gains, far, *refs):
    near, direct = refs[: HALVES * n_narrow], refs[HALVES * n_narrow : -3]
    out, total, stage = refs[-3:]
    rows, features = out.shape
    tall = features // LANES
    topk = route.shape[0]
    stage[0] = jnp.zeros((tall, LANES), F32)
    arrived = direct[0][...].astype(F32)
    for ref in direct[1:]:
        arrived = arrived + ref[...].astype(F32)
    stage[1:] = arrived
    for t in range(rows):
        value = far[t]
        cut, row = divmod(t, rows // HALVES)
        for ref in near[cut * n_narrow : (cut + 1) * n_narrow]:
            value = value + ref[row].astype(F32)
        for k in range(topk):
            slot = route[k, t] - CAP
            slot = jnp.where((slot >= 0) & (slot < CAP), slot + 1, 0)
            value = value + gains[k, t] * stage[slot]
        total[t * tall : (t + 1) * tall, :] = value
    for b in range(tall):
        out[:, b * LANES : (b + 1) * LANES] = total[
            pl.ds(b, rows, stride=tall), :
        ].astype(BF16)


def swap(value, axis, offset):
    size = lax.axis_size(axis)
    return lax.ppermute(value, axis, [(i, i ^ offset) for i in range(size)])


def in_hbm(*values):
    return [pltpu.with_memory_space_constraint(value, pltpu.HBM) for value in values]


def after(values, *others):
    return list(lax.optimization_barrier((tuple(values), others))[0])


def call(kernel, name, ins, specs, outs, scratch, flops=0, moved=0, limit=16):
    return pl.pallas_call(
        kernel,
        out_shape=outs,
        in_specs=specs,
        out_specs=jax.tree.map(
            lambda out: SSPEC if getattr(out, "memory_space", None) == pltpu.SMEM else VSPEC,
            outs,
        ),
        scratch_shapes=scratch,
        compiler_params=pltpu.CompilerParams(vmem_limit_bytes=limit << 20),
        cost_estimate=pl.CostEstimate(flops=flops, bytes_accessed=moved, transcendentals=0),
        name=name,
    )(*ins)


def shards(
    row_codes,
    row_scales,
    expert_ids,
    gate_weights,
    placement,
    w_gate,
    w_up,
    w_down,
    shared_gate,
    shared_up,
    shared_down,
):
    n_wide = lax.axis_size("wide")
    n_narrow = lax.axis_size("narrow")
    n_pair = lax.axis_size("pair")
    tokens, features = row_codes.shape
    hidden = w_gate.shape[2]
    tall = features // LANES
    topk = expert_ids.shape[1]
    limit = 16 if n_wide <= 4 else 48

    def block(*lead):
        return jax.ShapeDtypeStruct(lead + (tall, LANES), BF16)

    shared = [shared_gate, shared_up, shared_down]
    routed = [
        w_gate.reshape(features, hidden),
        w_up.reshape(features, hidden),
        w_down.reshape(hidden, features),
    ]
    near, *far = call(
        dispatch_kernel,
        "dispatch",
        in_hbm(expert_ids.T, placement, gate_weights.T, row_codes, row_scales)
        + in_hbm(*shared, *routed),
        [ASPEC] * 11,
        [block(tokens + 1)]
        + [block(CAP)] * (n_wide - 1)
        + [pltpu.SMEM((topk, tokens), jnp.int32), pltpu.SMEM((topk, tokens), F32)],
        [
            pltpu.SMEM((topk, tokens), jnp.int32),
            pltpu.SMEM(placement.shape, jnp.int32),
            pltpu.SMEM((topk, tokens), F32),
            VMEM((tokens, features), BF16),
            VMEM(row_scales.shape, BF16),
            VMEM((tokens * tall, LANES), F32),
            VMEM((n_wide * CAP, tall, LANES), F32),
            pltpu.SemaphoreType.DMA((5,)),
        ],
    )
    far, (route, gains) = far[:-2], far[-2:]
    order = list(range(n_wide - 1, 1, -1))
    across = ("wide", "narrow")
    bundles = [swap(far[k - 1], "wide", k) for k in order]
    direct = [swap(far[0], across, n_narrow + j) for j in range(n_narrow)]
    near_line = [near] + [swap(near, "narrow", j) for j in range(1, n_narrow)]
    bundles = after(bundles, *direct)
    if n_wide > 4:
        bundles = [jnp.concatenate(bundles, axis=0)]
    lines = [list(bundles)]
    for j in range(1, n_narrow):
        lines.append([swap(value, "narrow", j) for value in bundles])
    per = len(bundles) + 1
    slots = [value.shape[0] for value in bundles] + [CAP]
    near_line = after(near_line, *bundles)
    near_all = list(near_line)
    for c in range(1, n_pair):
        near_all += [swap(value, "pair", c) for value in near_line]

    near_rows = n_narrow * n_pair * tokens
    near_mid = call(
        near_shared_kernel,
        "near_shared",
        near_all + shared,
        [VSPEC] * (n_narrow * n_pair + 3),
        [
            jax.ShapeDtypeStruct((near_rows, features), BF16),
            jax.ShapeDtypeStruct((near_rows, LANES), F32),
            jax.ShapeDtypeStruct((near_rows, features), F32),
        ],
        [VMEM((near_rows * tall, LANES), F32)],
        flops=6 * near_rows * features * hidden,
        moved=6 * features * hidden,
        limit=limit,
    )
    side = after([value for line in lines[1:] for value in line], near_mid[1])
    far_line = []
    for j in range(n_narrow):
        far_line += lines[0] if j == 0 else side[(j - 1) * (per - 1) : j * (per - 1)]
        far_line.append(direct[j])
    far_all = list(far_line)
    for c in range(1, n_pair):
        far_all += [swap(value, "pair", c) for value in far_line]

    far_rows = n_narrow * n_pair * sum(slots)
    pass_rows = far_rows if far_rows <= MAX_ROWS else sum(slots)
    pass_rows = near_rows + -(-pass_rows // 16) * 16
    outs = call(
        functools.partial(routed_kernel, n_narrow, n_pair, per),
        "routed",
        far_all + list(near_mid) + routed,
        [VSPEC] * (n_narrow * n_pair * per + 6),
        [block(n_narrow, tokens)] * n_pair
        + [block(n_narrow, count) for count in slots] * n_pair,
        [VMEM((pass_rows * tall, LANES), F32), VMEM((pass_rows, features), BF16)],
        flops=6 * (near_rows + far_rows) * features * hidden,
        moved=6 * features * hidden,
        limit=limit,
    )
    near_out, far_out = outs[:n_pair], outs[n_pair:]

    def reduce_pair(parts, *first, cuts=1):
        rows = parts[0].shape[1]
        return call(
            functools.partial(pair_sum_kernel, n_pair, cuts),
            "pair_sum",
            after([parts[0]] + [swap(parts[c], "pair", c) for c in range(1, n_pair)], *first),
            [VSPEC] * n_pair,
            [block(rows // cuts)] * (n_narrow * cuts),
            [],
            limit=limit,
        )

    def send_narrow(parts):
        return [parts[0]] + [swap(parts[j], "narrow", j) for j in range(1, n_narrow)]

    far_back = []
    for k in range(per - 1):
        far_back += call(
            functools.partial(narrow_sum_kernel, n_narrow),
            "narrow_sum",
            send_narrow(reduce_pair(far_out[k::per])),
            [VSPEC] * n_narrow,
            [block(CAP)] * (slots[k] // CAP),
            [],
            limit=limit,
        )
    sums = far_back
    far_back = [swap(value, "wide", k) for k, value in zip(order, far_back)]
    direct_back = reduce_pair(far_out[per - 1 :: per])
    near_parts = reduce_pair(near_out, cuts=HALVES)
    near_back = []
    for cut in range(HALVES):
        near_back += send_narrow(near_parts[cut::HALVES])
    direct_back = [
        swap(value, across, n_narrow + j) for j, value in enumerate(direct_back)
    ]
    far_sum = call(
        functools.partial(far_combine_kernel, order),
        "far_combine",
        [route, gains] + far_back + in_hbm(*shared, *routed),
        [SSPEC] * 2 + [VSPEC] * len(order) + [ASPEC] * 6,
        jax.ShapeDtypeStruct((tokens, tall, LANES), F32),
        [VMEM((n_wide * CAP, tall, LANES), F32)],
    )
    return call(
        functools.partial(combine_kernel, n_narrow),
        "combine",
        [route, gains, far_sum] + near_back + direct_back,
        [SSPEC] * 2 + [VSPEC] * (1 + (HALVES + 1) * n_narrow),
        jax.ShapeDtypeStruct((tokens, features), BF16),
        [VMEM((tokens * tall, LANES), F32), VMEM((CAP + 1, tall, LANES), F32)],
    )


def solution(mesh):
    rows = P(("groups", "wide", "narrow", "pair"), None)
    return jax.shard_map(
        shards,
        mesh=mesh,
        in_specs=(
            rows,
            rows,
            rows,
            rows,
            P(),
            P("wide", None, ("narrow", "pair")),
            P("wide", None, ("narrow", "pair")),
            P("wide", ("narrow", "pair"), None),
            P(None, ("narrow", "pair")),
            P(None, ("narrow", "pair")),
            P(("narrow", "pair"), None),
        ),
        out_specs=rows,
        check_vma=False,
    )
```

```python
import functools

import jax
import jax.numpy as jnp
from jax import lax
from jax.experimental import pallas as pl
from jax.experimental.pallas import tpu as pltpu
from jax.sharding import PartitionSpec as P

CAP = 5
LANES = 128
SPAN = 7
HALVES = 2
MAX_ROWS = 128

VMEM = pltpu.VMEM
VSPEC = pl.BlockSpec(memory_space=pltpu.VMEM)
SSPEC = pl.BlockSpec(memory_space=pltpu.SMEM)
ASPEC = pl.BlockSpec(memory_space=pl.ANY)
F32 = jnp.float32
BF16 = jnp.bfloat16


def put(flat, at, value, tall):
    rows = value.shape[0]
    for b in range(value.shape[1] // LANES):
        flat[pl.ds(at // LANES + b, rows, stride=tall), :] = value[
            :, b * LANES : (b + 1) * LANES
        ]


def dispatch_kernel(ids_in, place_in, weights_in, codes_in, scales_in, *refs):
    refs = refs[6:]
    near, far = refs[0], refs[1:-10]
    route, gains = refs[-10:-8]
    ids, place, weights, codes, scales, tok, stage, sems = refs[-8:]
    copies = [
        pltpu.make_async_copy(src, dst, sems.at[i])
        for i, (src, dst) in enumerate(
            (
                (codes_in, codes),
                (scales_in, scales),
                (ids_in, ids),
                (place_in, place),
                (weights_in, weights),
            )
        )
    ]
    for copy in copies:
        copy.start()
    here = lax.axis_index("wide")
    rows, features = codes.shape
    topk = ids.shape[0]
    tall = features // LANES
    stage[...] = jnp.zeros_like(stage)
    for copy in copies:
        copy.wait()
    for b in range(tall):
        block = codes[:, b * LANES : (b + 1) * LANES].astype(F32)
        tok[pl.ds(b, rows, stride=tall), :] = block * scales[:, b : b + 1].astype(F32)
    near[:rows] = tok[...].reshape(rows, tall, LANES).astype(BF16)
    sub = lax.broadcasted_iota(jnp.int32, (rows, LANES), 0)
    lane = lax.broadcasted_iota(jnp.int32, (rows, LANES), 1)
    weight = jnp.zeros((rows, LANES), F32)
    named = []
    for t in range(rows):
        for k in range(topk):
            e = ids[k, t]
            node = place[e]
            slot = jnp.int32(0)
            for other in named[: t * topk]:
                slot = slot + jnp.where(other == e, 1, 0)
            named.append(e)
            at = (node ^ here) * CAP + slot
            route[k, t] = at
            gains[k, t] = weights[k, t]
            weight = jnp.where((sub == t) & (lane == node), weights[k, t], weight)
            stage[at] = tok[t * tall : (t + 1) * tall, :]
    high = weight.astype(BF16).astype(F32)
    middle = (weight - high).astype(BF16).astype(F32)
    low = weight - high - middle
    near[rows] = jnp.concatenate(
        [high, middle, low, jnp.zeros((tall - 3 * rows, LANES), F32)], axis=0
    ).astype(BF16)
    for k, ref in enumerate(far):
        ref[...] = stage[(k + 1) * CAP : (k + 2) * CAP].astype(BF16)


def unpack(refs, blocks, rows, flat, inputs, first=0):
    tall = inputs.shape[1] // LANES
    at = 0
    for ref, count in zip(refs, blocks):
        flat[at * tall : (at + count) * tall, :] = (
            ref[:count].astype(F32).reshape(count * tall, LANES)
        )
        at += count
    if at < rows:
        flat[at * tall : rows * tall, :] = jnp.zeros(((rows - at) * tall, LANES), F32)
    for b in range(tall):
        inputs[first : first + rows, b * LANES : (b + 1) * LANES] = flat[
            pl.ds(b, rows, stride=tall), :
        ].astype(BF16)


def silu_mul(gate, up):
    return (gate / (1.0 + jnp.exp(-gate)) * up).astype(BF16)


def near_shared_kernel(*refs):
    count = len(refs) - 7
    arrived, (gate_w, up_w, down_w), outs = refs[:count], refs[count : count + 3], refs[-4:]
    inputs, weight, value, flat = outs
    here = lax.axis_index("wide")
    tokens, tall = arrived[0].shape[0] - 1, arrived[0].shape[1]
    rows = count * tokens
    unpack(arrived, [tokens] * count, rows, flat, inputs)
    for i, ref in enumerate(arrived):
        parts = ref[tokens].astype(F32)
        whole = (
            parts[:tokens] + parts[tokens : 2 * tokens] + parts[2 * tokens : 3 * tokens]
        )
        lane = lax.broadcasted_iota(jnp.int32, whole.shape, 1)
        gain = jnp.sum(jnp.where(lane == here, whole, 0.0), axis=1, keepdims=True)
        weight[i * tokens : (i + 1) * tokens, :] = jnp.broadcast_to(gain, whole.shape)
    x = inputs[...]
    gate = jnp.dot(x, gate_w[...], preferred_element_type=F32)
    up = jnp.dot(x, up_w[...], preferred_element_type=F32)
    hidden = silu_mul(gate, up)
    for first in range(0, tall * LANES, SPAN * LANES):
        at = slice(first, first + SPAN * LANES)
        value[:, at] = jnp.dot(hidden, down_w[:, at], preferred_element_type=F32)


def routed_kernel(n_narrow, n_pair, per, *refs):
    count = n_narrow * n_pair * per
    arrived, rest = refs[:count], refs[count:]
    near, weight, value, gate_w, up_w, down_w = rest[:6]
    near_outs, outs = rest[6 : 6 + n_pair], rest[6 + n_pair : -2]
    flat, inputs = rest[-2:]
    tall = arrived[0].shape[1]
    near_rows = near.shape[0]
    each = near_rows // n_pair
    blocks = [ref.shape[0] for ref in arrived]
    step = count if sum(blocks) <= MAX_ROWS else per
    for first in range(0, count, step):
        group = blocks[first : first + step]
        head = 0 if first else near_rows
        rows = -(-sum(group) // 16) * 16
        unpack(arrived[first : first + step], group, rows, flat, inputs, head)
        if head:
            inputs[:head] = near[...]
        x = inputs[: head + rows]
        gate = jnp.dot(x, gate_w[...], preferred_element_type=F32)
        up = jnp.dot(x, up_w[...], preferred_element_type=F32)
        hidden = silu_mul(gate, up)
        for at in range(0, tall * LANES, SPAN * LANES):
            part = jnp.dot(
                hidden, down_w[:, at : at + SPAN * LANES], preferred_element_type=F32
            )
            if head:
                part = jnp.concatenate(
                    [
                        value[:, at : at + SPAN * LANES] + weight[:, :1] * part[:head],
                        part[head:],
                    ],
                    axis=0,
                )
            put(flat, at, part, tall)
        if head:
            for c in range(n_pair):
                part = flat[c * each * tall : (c + 1) * each * tall, :]
                near_outs[c][...] = part.reshape(near_outs[c].shape).astype(BF16)
        at = head
        for i, slots in enumerate(group):
            line, k = divmod(first + i, per)
            c, j = divmod(line, n_narrow)
            part = flat[at * tall : (at + slots) * tall, :]
            outs[c * per + k][j] = part.reshape(slots, tall, LANES).astype(BF16)
            at += slots


def pair_sum_kernel(n_pair, cuts, *refs):
    parts, outs = refs[:n_pair], refs[n_pair:]
    for i, out in enumerate(outs):
        j, cut = divmod(i, cuts)
        rows = slice(cut * out.shape[0], (cut + 1) * out.shape[0])
        total = parts[0][j, rows].astype(F32)
        for ref in parts[1:]:
            total = total + ref[j, rows].astype(F32)
        out[...] = total.astype(BF16)


def narrow_sum_kernel(n_narrow, *refs):
    parts, outs = refs[:n_narrow], refs[n_narrow:]
    at = 0
    for out in outs:
        rows = slice(at, at + out.shape[0])
        total = parts[0][rows].astype(F32)
        for ref in parts[1:]:
            total = total + ref[rows].astype(F32)
        out[...] = total.astype(BF16)
        at += out.shape[0]


def far_combine_kernel(order, route, gains, *refs):
    far, (total, stage) = refs[: len(order)], refs[-2:]
    topk, rows = route.shape
    tall = stage.shape[1]
    stage[:CAP] = jnp.zeros((CAP, tall, LANES), F32)
    for k, ref in zip(order, far):
        stage[k * CAP : (k + 1) * CAP] = ref[...].astype(F32)
    for t in range(rows):
        value = gains[0, t] * stage[route[0, t]]
        for k in range(1, topk):
            value = value + gains[k, t] * stage[route[k, t]]
        total[t] = value


def combine_kernel(n_narrow, far, *refs):
    near, (out, total) = refs[:-2], refs[-2:]
    rows, features = out.shape
    tall = features // LANES
    for t in range(rows):
        value = far[t]
        cut, row = divmod(t, rows // HALVES)
        for ref in near[cut * n_narrow : (cut + 1) * n_narrow]:
            value = value + ref[row].astype(F32)
        total[t * tall : (t + 1) * tall, :] = value
    for b in range(tall):
        out[:, b * LANES : (b + 1) * LANES] = total[
            pl.ds(b, rows, stride=tall), :
        ].astype(BF16)


def swap(value, axis, offset):
    size = lax.axis_size(axis)
    return lax.ppermute(value, axis, [(i, i ^ offset) for i in range(size)])


def in_hbm(*values):
    return [pltpu.with_memory_space_constraint(value, pltpu.HBM) for value in values]


def after(values, *others):
    return list(lax.optimization_barrier((tuple(values), others))[0])


def call(kernel, name, ins, specs, outs, scratch, flops=0, moved=0, limit=16):
    return pl.pallas_call(
        kernel,
        out_shape=outs,
        in_specs=specs,
        out_specs=jax.tree.map(
            lambda out: SSPEC if getattr(out, "memory_space", None) == pltpu.SMEM else VSPEC,
            outs,
        ),
        scratch_shapes=scratch,
        compiler_params=pltpu.CompilerParams(vmem_limit_bytes=limit << 20),
        cost_estimate=pl.CostEstimate(flops=flops, bytes_accessed=moved, transcendentals=0),
        name=name,
    )(*ins)


def shards(
    row_codes,
    row_scales,
    expert_ids,
    gate_weights,
    placement,
    w_gate,
    w_up,
    w_down,
    shared_gate,
    shared_up,
    shared_down,
):
    n_wide = lax.axis_size("wide")
    n_narrow = lax.axis_size("narrow")
    n_pair = lax.axis_size("pair")
    tokens, features = row_codes.shape
    hidden = w_gate.shape[2]
    tall = features // LANES
    topk = expert_ids.shape[1]
    limit = 16 if n_wide <= 4 else 48

    def block(*lead):
        return jax.ShapeDtypeStruct(lead + (tall, LANES), BF16)

    shared = [shared_gate, shared_up, shared_down]
    routed = [
        w_gate.reshape(features, hidden),
        w_up.reshape(features, hidden),
        w_down.reshape(hidden, features),
    ]
    near, *far = call(
        dispatch_kernel,
        "dispatch",
        in_hbm(expert_ids.T, placement, gate_weights.T, row_codes, row_scales)
        + in_hbm(*shared, *routed),
        [ASPEC] * 11,
        [block(tokens + 1)]
        + [block(CAP)] * (n_wide - 1)
        + [pltpu.SMEM((topk, tokens), jnp.int32), pltpu.SMEM((topk, tokens), F32)],
        [
            pltpu.SMEM((topk, tokens), jnp.int32),
            pltpu.SMEM(placement.shape, jnp.int32),
            pltpu.SMEM((topk, tokens), F32),
            VMEM((tokens, features), BF16),
            VMEM(row_scales.shape, BF16),
            VMEM((tokens * tall, LANES), F32),
            VMEM((n_wide * CAP, tall, LANES), F32),
            pltpu.SemaphoreType.DMA((5,)),
        ],
    )
    far, (route, gains) = far[:-2], far[-2:]
    order = list(range(n_wide - 1, 1, -1))
    across = ("wide", "narrow")
    bundles = [swap(far[k - 1], "wide", k) for k in order]
    direct = [swap(far[0], across, n_narrow + j) for j in range(n_narrow)]
    near_line = [near] + [swap(near, "narrow", j) for j in range(1, n_narrow)]
    bundles = after(bundles, *direct)
    if n_wide > 4:
        bundles = [jnp.concatenate(bundles, axis=0)]
    lines = [list(bundles)]
    for j in range(1, n_narrow):
        lines.append([swap(value, "narrow", j) for value in bundles])
    per = len(bundles) + 1
    slots = [value.shape[0] for value in bundles] + [CAP]
    near_line = after(near_line, *bundles)
    near_all = list(near_line)
    for c in range(1, n_pair):
        near_all += [swap(value, "pair", c) for value in near_line]

    near_rows = n_narrow * n_pair * tokens
    near_mid = call(
        near_shared_kernel,
        "near_shared",
        near_all + shared,
        [VSPEC] * (n_narrow * n_pair + 3),
        [
            jax.ShapeDtypeStruct((near_rows, features), BF16),
            jax.ShapeDtypeStruct((near_rows, LANES), F32),
            jax.ShapeDtypeStruct((near_rows, features), F32),
        ],
        [VMEM((near_rows * tall, LANES), F32)],
        flops=6 * near_rows * features * hidden,
        moved=6 * features * hidden,
        limit=limit,
    )
    side = after([value for line in lines[1:] for value in line], near_mid[1])
    far_line = []
    for j in range(n_narrow):
        far_line += lines[0] if j == 0 else side[(j - 1) * (per - 1) : j * (per - 1)]
        far_line.append(direct[j])
    far_all = list(far_line)
    for c in range(1, n_pair):
        far_all += [swap(value, "pair", c) for value in far_line]

    far_rows = n_narrow * n_pair * sum(slots)
    pass_rows = far_rows if far_rows <= MAX_ROWS else sum(slots)
    pass_rows = near_rows + -(-pass_rows // 16) * 16
    outs = call(
        functools.partial(routed_kernel, n_narrow, n_pair, per),
        "routed",
        far_all + list(near_mid) + routed,
        [VSPEC] * (n_narrow * n_pair * per + 6),
        [block(n_narrow, tokens)] * n_pair
        + [block(n_narrow, count) for count in slots] * n_pair,
        [VMEM((pass_rows * tall, LANES), F32), VMEM((pass_rows, features), BF16)],
        flops=6 * (near_rows + far_rows) * features * hidden,
        moved=6 * features * hidden,
        limit=limit,
    )
    near_out, far_out = outs[:n_pair], outs[n_pair:]

    def reduce_pair(parts, *first, cuts=1):
        rows = parts[0].shape[1]
        return call(
            functools.partial(pair_sum_kernel, n_pair, cuts),
            "pair_sum",
            after([parts[0]] + [swap(parts[c], "pair", c) for c in range(1, n_pair)], *first),
            [VSPEC] * n_pair,
            [block(rows // cuts)] * (n_narrow * cuts),
            [],
            limit=limit,
        )

    def send_narrow(parts):
        return [parts[0]] + [swap(parts[j], "narrow", j) for j in range(1, n_narrow)]

    sums = []
    for k in range(per):
        sums += call(
            functools.partial(narrow_sum_kernel, n_narrow),
            "narrow_sum",
            send_narrow(reduce_pair(far_out[k::per])),
            [VSPEC] * n_narrow,
            [block(CAP)] * (slots[k] // CAP),
            [],
            limit=limit,
        )
    order.append(1)
    far_back = [swap(value, "wide", k) for k, value in zip(order, sums)]
    near_parts = reduce_pair(near_out, cuts=HALVES)
    near_back = []
    for cut in range(HALVES):
        near_back += send_narrow(near_parts[cut::HALVES])
    far_sum = call(
        functools.partial(far_combine_kernel, order),
        "far_combine",
        [route, gains] + far_back + in_hbm(*shared, *routed),
        [SSPEC] * 2 + [VSPEC] * len(order) + [ASPEC] * 6,
        jax.ShapeDtypeStruct((tokens, tall, LANES), F32),
        [VMEM((n_wide * CAP, tall, LANES), F32)],
    )
    return call(
        functools.partial(combine_kernel, n_narrow),
        "combine",
        [far_sum] + near_back,
        [VSPEC] * (1 + HALVES * n_narrow),
        jax.ShapeDtypeStruct((tokens, features), BF16),
        [VMEM((tokens * tall, LANES), F32)],
    )


def solution(mesh):
    rows = P(("groups", "wide", "narrow", "pair"), None)
    return jax.shard_map(
        shards,
        mesh=mesh,
        in_specs=(
            rows,
            rows,
            rows,
            rows,
            P(),
            P("wide", None, ("narrow", "pair")),
            P("wide", None, ("narrow", "pair")),
            P("wide", ("narrow", "pair"), None),
            P(None, ("narrow", "pair")),
            P(None, ("narrow", "pair")),
            P(("narrow", "pair"), None),
        ),
        out_specs=rows,
        check_vma=False,
    )
```

```python
import functools

import jax
import jax.numpy as jnp
from jax import lax
from jax.experimental import pallas as pl
from jax.experimental.pallas import tpu as pltpu
from jax.sharding import PartitionSpec as P

CAP = 5
LANES = 128
SPAN = 7
HALVES = 2
MAX_ROWS = 128

VMEM = pltpu.VMEM
VSPEC = pl.BlockSpec(memory_space=pltpu.VMEM)
SSPEC = pl.BlockSpec(memory_space=pltpu.SMEM)
ASPEC = pl.BlockSpec(memory_space=pl.ANY)
F32 = jnp.float32
BF16 = jnp.bfloat16


def put(flat, at, value, tall):
    rows = value.shape[0]
    for b in range(value.shape[1] // LANES):
        flat[pl.ds(at // LANES + b, rows, stride=tall), :] = value[
            :, b * LANES : (b + 1) * LANES
        ]


def dispatch_kernel(ids_in, place_in, weights_in, codes_in, scales_in, *refs):
    refs = refs[6:]
    near, far = refs[0], refs[1:-10]
    route, gains = refs[-10:-8]
    ids, place, weights, codes, scales, tok, stage, sems = refs[-8:]
    copies = [
        pltpu.make_async_copy(src, dst, sems.at[i])
        for i, (src, dst) in enumerate(
            (
                (codes_in, codes),
                (scales_in, scales),
                (ids_in, ids),
                (place_in, place),
                (weights_in, weights),
            )
        )
    ]
    for copy in copies:
        copy.start()
    here = lax.axis_index("wide")
    rows, features = codes.shape
    topk = ids.shape[0]
    tall = features // LANES
    stage[...] = jnp.zeros_like(stage)
    for copy in copies:
        copy.wait()
    for b in range(tall):
        block = codes[:, b * LANES : (b + 1) * LANES].astype(F32)
        tok[pl.ds(b, rows, stride=tall), :] = block * scales[:, b : b + 1].astype(F32)
    near[:rows] = tok[...].reshape(rows, tall, LANES).astype(BF16)
    sub = lax.broadcasted_iota(jnp.int32, (rows, LANES), 0)
    lane = lax.broadcasted_iota(jnp.int32, (rows, LANES), 1)
    weight = jnp.zeros((rows, LANES), F32)
    named = []
    for t in range(rows):
        for k in range(topk):
            e = ids[k, t]
            node = place[e]
            slot = jnp.int32(0)
            for other in named[: t * topk]:
                slot = slot + jnp.where(other == e, 1, 0)
            named.append(e)
            at = (node ^ here) * CAP + slot
            route[k, t] = at
            gains[k, t] = weights[k, t]
            weight = jnp.where((sub == t) & (lane == node), weights[k, t], weight)
            stage[at] = tok[t * tall : (t + 1) * tall, :]
    high = weight.astype(BF16).astype(F32)
    middle = (weight - high).astype(BF16).astype(F32)
    low = weight - high - middle
    near[rows] = jnp.concatenate(
        [high, middle, low, jnp.zeros((tall - 3 * rows, LANES), F32)], axis=0
    ).astype(BF16)
    for k, ref in enumerate(far):
        ref[...] = stage[(k + 1) * CAP : (k + 2) * CAP].astype(BF16)


def unpack(refs, blocks, rows, flat, inputs, first=0):
    tall = inputs.shape[1] // LANES
    at = 0
    for ref, count in zip(refs, blocks):
        flat[at * tall : (at + count) * tall, :] = (
            ref[:count].astype(F32).reshape(count * tall, LANES)
        )
        at += count
    if at < rows:
        flat[at * tall : rows * tall, :] = jnp.zeros(((rows - at) * tall, LANES), F32)
    for b in range(tall):
        inputs[first : first + rows, b * LANES : (b + 1) * LANES] = flat[
            pl.ds(b, rows, stride=tall), :
        ].astype(BF16)


def gather_kernel(count, *refs):
    out = refs[-1]
    for i, ref in enumerate(refs[:count]):
        out[i * CAP : (i + 1) * CAP] = ref[...]


def silu_mul(gate, up):
    return (gate / (1.0 + jnp.exp(-gate)) * up).astype(BF16)


def near_shared_kernel(*refs):
    count = len(refs) - 7
    arrived, (gate_w, up_w, down_w), outs = refs[:count], refs[count : count + 3], refs[-4:]
    inputs, weight, value, flat = outs
    here = lax.axis_index("wide")
    tokens, tall = arrived[0].shape[0] - 1, arrived[0].shape[1]
    rows = count * tokens
    unpack(arrived, [tokens] * count, rows, flat, inputs)
    for i, ref in enumerate(arrived):
        parts = ref[tokens].astype(F32)
        whole = (
            parts[:tokens] + parts[tokens : 2 * tokens] + parts[2 * tokens : 3 * tokens]
        )
        lane = lax.broadcasted_iota(jnp.int32, whole.shape, 1)
        gain = jnp.sum(jnp.where(lane == here, whole, 0.0), axis=1, keepdims=True)
        weight[i * tokens : (i + 1) * tokens, :] = jnp.broadcast_to(gain, whole.shape)
    x = inputs[...]
    gate = jnp.dot(x, gate_w[...], preferred_element_type=F32)
    up = jnp.dot(x, up_w[...], preferred_element_type=F32)
    hidden = silu_mul(gate, up)
    for first in range(0, tall * LANES, SPAN * LANES):
        at = slice(first, first + SPAN * LANES)
        value[:, at] = jnp.dot(hidden, down_w[:, at], preferred_element_type=F32)


def routed_kernel(n_narrow, n_pair, per, n_direct, *refs):
    count = n_narrow * n_pair * per
    n_lines = n_narrow * (per - n_direct)
    arrived = []
    for c in range(n_pair):
        *lines, gathered = refs[c * (n_lines + 1) : (c + 1) * (n_lines + 1)]
        for j in range(n_narrow):
            arrived += lines[j * (per - n_direct) : (j + 1) * (per - n_direct)]
            for i in range(n_direct):
                arrived.append(gathered.at[pl.ds((i * n_narrow + j) * CAP, CAP)])
    rest = refs[n_pair * (n_lines + 1) :]
    near, weight, value, gate_w, up_w, down_w = rest[:6]
    near_outs, outs = rest[6 : 6 + n_pair], rest[6 + n_pair : -2]
    flat, inputs = rest[-2:]
    tall = arrived[0].shape[1]
    near_rows = near.shape[0]
    each = near_rows // n_pair
    blocks = [ref.shape[0] for ref in arrived]
    step = count if sum(blocks) <= MAX_ROWS else per
    for first in range(0, count, step):
        group = blocks[first : first + step]
        head = 0 if first else near_rows
        rows = -(-sum(group) // 16) * 16
        unpack(arrived[first : first + step], group, rows, flat, inputs, head)
        if head:
            inputs[:head] = near[...]
        x = inputs[: head + rows]
        gate = jnp.dot(x, gate_w[...], preferred_element_type=F32)
        up = jnp.dot(x, up_w[...], preferred_element_type=F32)
        hidden = silu_mul(gate, up)
        for at in range(0, tall * LANES, SPAN * LANES):
            part = jnp.dot(
                hidden, down_w[:, at : at + SPAN * LANES], preferred_element_type=F32
            )
            if head:
                part = jnp.concatenate(
                    [
                        value[:, at : at + SPAN * LANES] + weight[:, :1] * part[:head],
                        part[head:],
                    ],
                    axis=0,
                )
            put(flat, at, part, tall)
        if head:
            for c in range(n_pair):
                part = flat[c * each * tall : (c + 1) * each * tall, :]
                near_outs[c][...] = part.reshape(near_outs[c].shape).astype(BF16)
        at = head
        for i, slots in enumerate(group):
            line, k = divmod(first + i, per)
            c, j = divmod(line, n_narrow)
            part = flat[at * tall : (at + slots) * tall, :]
            outs[c * per + k][j] = part.reshape(slots, tall, LANES).astype(BF16)
            at += slots


def pair_sum_kernel(n_pair, cuts, *refs):
    parts, outs = refs[:n_pair], refs[n_pair:]
    for i, out in enumerate(outs):
        j, cut = divmod(i, cuts)
        rows = slice(cut * out.shape[0], (cut + 1) * out.shape[0])
        total = parts[0][j, rows].astype(F32)
        for ref in parts[1:]:
            total = total + ref[j, rows].astype(F32)
        out[...] = total.astype(BF16)


def narrow_sum_kernel(n_narrow, *refs):
    parts, outs = refs[:n_narrow], refs[n_narrow:]
    at = 0
    for out in outs:
        rows = slice(at, at + out.shape[0])
        total = parts[0][rows].astype(F32)
        for ref in parts[1:]:
            total = total + ref[rows].astype(F32)
        out[...] = total.astype(BF16)
        at += out.shape[0]


def weigh(route, gains, stage, t):
    value = gains[0, t] * stage[route[0, t]]
    for k in range(1, route.shape[0]):
        value = value + gains[k, t] * stage[route[k, t]]
    return value


def direct_combine_kernel(n_narrow, order, route, gains, *refs):
    direct, (total, stage) = refs[: n_narrow * len(order)], refs[-2:]
    stage[...] = jnp.zeros_like(stage)
    for i, k in enumerate(order):
        arrived = direct[i * n_narrow][...].astype(F32)
        for ref in direct[i * n_narrow + 1 : (i + 1) * n_narrow]:
            arrived = arrived + ref[...].astype(F32)
        stage[k * CAP : (k + 1) * CAP] = arrived
    for t in range(route.shape[1]):
        total[t] = weigh(route, gains, stage, t)


def combine_kernel(n_narrow, order, route, gains, direct, *refs):
    near, far = refs[: HALVES * n_narrow], refs[HALVES * n_narrow : -3]
    out, total, stage = refs[-3:]
    rows, features = out.shape
    tall = features // LANES
    stage[...] = jnp.zeros_like(stage)
    for k, ref in zip(order, far):
        stage[k * CAP : (k + 1) * CAP] = ref[...].astype(F32)
    for t in range(rows):
        value = direct[t] + weigh(route, gains, stage, t)
        cut, row = divmod(t, rows // HALVES)
        for ref in near[cut * n_narrow : (cut + 1) * n_narrow]:
            value = value + ref[row].astype(F32)
        total[t * tall : (t + 1) * tall, :] = value
    for b in range(tall):
        out[:, b * LANES : (b + 1) * LANES] = total[
            pl.ds(b, rows, stride=tall), :
        ].astype(BF16)


def swap(value, axis, offset):
    size = lax.axis_size(axis)
    return lax.ppermute(value, axis, [(i, i ^ offset) for i in range(size)])


def in_hbm(*values):
    return [pltpu.with_memory_space_constraint(value, pltpu.HBM) for value in values]


def after(values, *others):
    return list(lax.optimization_barrier((tuple(values), others))[0])


def call(kernel, name, ins, specs, outs, scratch, flops=0, moved=0, limit=16):
    return pl.pallas_call(
        kernel,
        out_shape=outs,
        in_specs=specs,
        out_specs=jax.tree.map(
            lambda out: SSPEC if getattr(out, "memory_space", None) == pltpu.SMEM else VSPEC,
            outs,
        ),
        scratch_shapes=scratch,
        compiler_params=pltpu.CompilerParams(vmem_limit_bytes=limit << 20),
        cost_estimate=pl.CostEstimate(flops=flops, bytes_accessed=moved, transcendentals=0),
        name=name,
    )(*ins)


def shards(
    row_codes,
    row_scales,
    expert_ids,
    gate_weights,
    placement,
    w_gate,
    w_up,
    w_down,
    shared_gate,
    shared_up,
    shared_down,
):
    n_wide = lax.axis_size("wide")
    n_narrow = lax.axis_size("narrow")
    n_pair = lax.axis_size("pair")
    tokens, features = row_codes.shape
    hidden = w_gate.shape[2]
    tall = features // LANES
    topk = expert_ids.shape[1]
    limit = 16 if n_wide <= 4 else 48

    def block(*lead):
        return jax.ShapeDtypeStruct(lead + (tall, LANES), BF16)

    shared = [shared_gate, shared_up, shared_down]
    routed = [
        w_gate.reshape(features, hidden),
        w_up.reshape(features, hidden),
        w_down.reshape(hidden, features),
    ]
    near, *far = call(
        dispatch_kernel,
        "dispatch",
        in_hbm(expert_ids.T, placement, gate_weights.T, row_codes, row_scales)
        + in_hbm(*shared, *routed),
        [ASPEC] * 11,
        [block(tokens + 1)]
        + [block(CAP)] * (n_wide - 1)
        + [pltpu.SMEM((topk, tokens), jnp.int32), pltpu.SMEM((topk, tokens), F32)],
        [
            pltpu.SMEM((topk, tokens), jnp.int32),
            pltpu.SMEM(placement.shape, jnp.int32),
            pltpu.SMEM((topk, tokens), F32),
            VMEM((tokens, features), BF16),
            VMEM(row_scales.shape, BF16),
            VMEM((tokens * tall, LANES), F32),
            VMEM((n_wide * CAP, tall, LANES), F32),
            pltpu.SemaphoreType.DMA((5,)),
        ],
    )
    far, (route, gains) = far[:-2], far[-2:]
    directly = [k for k in (3, 1) if k < n_wide]
    order = [k for k in range(n_wide - 1, 0, -1) if k not in directly]
    across = ("wide", "narrow")
    bundles = [swap(far[k - 1], "wide", k) for k in order]
    direct = [
        swap(far[k - 1], across, k * n_narrow + j)
        for k in directly
        for j in range(n_narrow)
    ]
    near_line = [near] + [swap(near, "narrow", j) for j in range(1, n_narrow)]
    if n_wide > 4:
        bundles = [jnp.concatenate(bundles, axis=0)]
    lines = [list(bundles)]
    for j in range(1, n_narrow):
        lines.append([swap(value, "narrow", j) for value in bundles])
    per = len(bundles) + len(directly)
    slots = [value.shape[0] for value in bundles] + [CAP] * len(directly)
    near_line = after(near_line, *bundles)
    near_all = list(near_line)
    for c in range(1, n_pair):
        near_all += [swap(value, "pair", c) for value in near_line]

    near_rows = n_narrow * n_pair * tokens
    near_mid = call(
        near_shared_kernel,
        "near_shared",
        near_all + shared,
        [VSPEC] * (n_narrow * n_pair + 3),
        [
            jax.ShapeDtypeStruct((near_rows, features), BF16),
            jax.ShapeDtypeStruct((near_rows, LANES), F32),
            jax.ShapeDtypeStruct((near_rows, features), F32),
        ],
        [VMEM((near_rows * tall, LANES), F32)],
        flops=6 * near_rows * features * hidden,
        moved=6 * features * hidden,
        limit=limit,
    )
    side = after([value for line in lines[1:] for value in line], near_mid[1])
    direct = after(direct, *side)
    gathered = call(
        functools.partial(gather_kernel, len(direct)),
        "gather",
        direct,
        [VSPEC] * len(direct),
        block(CAP * len(direct)),
        [],
    )
    far_line = lines[0] + side + [gathered]
    far_all = list(far_line)
    for c in range(1, n_pair):
        far_all += [swap(value, "pair", c) for value in far_line]

    far_rows = n_narrow * n_pair * sum(slots)
    pass_rows = far_rows if far_rows <= MAX_ROWS else sum(slots)
    pass_rows = near_rows + -(-pass_rows // 16) * 16
    outs = call(
        functools.partial(routed_kernel, n_narrow, n_pair, per, len(directly)),
        "routed",
        far_all + list(near_mid) + routed,
        [VSPEC] * (len(far_all) + 6),
        [block(n_narrow, tokens)] * n_pair
        + [block(n_narrow, count) for count in slots] * n_pair,
        [VMEM((pass_rows * tall, LANES), F32), VMEM((pass_rows, features), BF16)],
        flops=6 * (near_rows + far_rows) * features * hidden,
        moved=6 * features * hidden,
        limit=limit,
    )
    near_out, far_out = outs[:n_pair], outs[n_pair:]

    def reduce_pair(parts, *first, cuts=1):
        rows = parts[0].shape[1]
        return call(
            functools.partial(pair_sum_kernel, n_pair, cuts),
            "pair_sum",
            after([parts[0]] + [swap(parts[c], "pair", c) for c in range(1, n_pair)], *first),
            [VSPEC] * n_pair,
            [block(rows // cuts)] * (n_narrow * cuts),
            [],
            limit=limit,
        )

    def send_narrow(parts):
        return [parts[0]] + [swap(parts[j], "narrow", j) for j in range(1, n_narrow)]

    sums = []
    for k in range(len(bundles)):
        sums += call(
            functools.partial(narrow_sum_kernel, n_narrow),
            "narrow_sum",
            send_narrow(reduce_pair(far_out[k::per])),
            [VSPEC] * n_narrow,
            [block(CAP)] * (slots[k] // CAP),
            [],
            limit=limit,
        )
    direct_back = []
    for i, k in enumerate(directly):
        parts = reduce_pair(far_out[len(bundles) + i :: per])
        direct_back += [
            swap(value, across, k * n_narrow + j) for j, value in enumerate(parts)
        ]
    far_back = [swap(value, "wide", k) for k, value in zip(order, sums)]
    near_parts = reduce_pair(near_out, cuts=HALVES)
    near_back = []
    for cut in range(HALVES):
        near_back += send_narrow(near_parts[cut::HALVES])
    direct_sum = call(
        functools.partial(direct_combine_kernel, n_narrow, directly),
        "direct_combine",
        [route, gains] + direct_back + in_hbm(*shared, *routed),
        [SSPEC] * 2 + [VSPEC] * len(direct_back) + [ASPEC] * 6,
        jax.ShapeDtypeStruct((tokens, tall, LANES), F32),
        [VMEM((n_wide * CAP, tall, LANES), F32)],
    )
    return call(
        functools.partial(combine_kernel, n_narrow, order),
        "combine",
        [route, gains, direct_sum] + near_back + far_back,
        [SSPEC] * 2 + [VSPEC] * (1 + HALVES * n_narrow + len(far_back)),
        jax.ShapeDtypeStruct((tokens, features), BF16),
        [
            VMEM((tokens * tall, LANES), F32),
            VMEM((n_wide * CAP, tall, LANES), F32),
        ],
    )


def solution(mesh):
    rows = P(("groups", "wide", "narrow", "pair"), None)
    return jax.shard_map(
        shards,
        mesh=mesh,
        in_specs=(
            rows,
            rows,
            rows,
            rows,
            P(),
            P("wide", None, ("narrow", "pair")),
            P("wide", None, ("narrow", "pair")),
            P("wide", ("narrow", "pair"), None),
            P(None, ("narrow", "pair")),
            P(None, ("narrow", "pair")),
            P(("narrow", "pair"), None),
        ),
        out_specs=rows,
        check_vma=False,
    )
```

```python
import functools

import jax
import jax.numpy as jnp
from jax import lax
from jax.experimental import pallas as pl
from jax.experimental.pallas import tpu as pltpu
from jax.sharding import PartitionSpec as P

CAP = 5
LANES = 128
SPAN = 7
HALVES = 1
MAX_ROWS = 128

VMEM = pltpu.VMEM
VSPEC = pl.BlockSpec(memory_space=pltpu.VMEM)
SSPEC = pl.BlockSpec(memory_space=pltpu.SMEM)
ASPEC = pl.BlockSpec(memory_space=pl.ANY)
F32 = jnp.float32
BF16 = jnp.bfloat16


def put(flat, at, value, tall):
    rows = value.shape[0]
    for b in range(value.shape[1] // LANES):
        flat[pl.ds(at // LANES + b, rows, stride=tall), :] = value[
            :, b * LANES : (b + 1) * LANES
        ]


def dispatch_kernel(ids_in, place_in, weights_in, codes_in, scales_in, *refs):
    refs = refs[6:]
    near, far = refs[0], refs[1:-10]
    route, gains = refs[-10:-8]
    ids, place, weights, codes, scales, tok, stage, sems = refs[-8:]
    copies = [
        pltpu.make_async_copy(src, dst, sems.at[i])
        for i, (src, dst) in enumerate(
            (
                (codes_in, codes),
                (scales_in, scales),
                (ids_in, ids),
                (place_in, place),
                (weights_in, weights),
            )
        )
    ]
    for copy in copies:
        copy.start()
    here = lax.axis_index("wide")
    rows, features = codes.shape
    topk = ids.shape[0]
    tall = features // LANES
    stage[...] = jnp.zeros_like(stage)
    for copy in copies:
        copy.wait()
    for b in range(tall):
        block = codes[:, b * LANES : (b + 1) * LANES].astype(F32)
        tok[pl.ds(b, rows, stride=tall), :] = block * scales[:, b : b + 1].astype(F32)
    near[:rows] = tok[...].reshape(rows, tall, LANES).astype(BF16)
    sub = lax.broadcasted_iota(jnp.int32, (rows, LANES), 0)
    lane = lax.broadcasted_iota(jnp.int32, (rows, LANES), 1)
    weight = jnp.zeros((rows, LANES), F32)
    named = []
    for t in range(rows):
        for k in range(topk):
            e = ids[k, t]
            node = place[e]
            slot = jnp.int32(0)
            for other in named[: t * topk]:
                slot = slot + jnp.where(other == e, 1, 0)
            named.append(e)
            at = (node ^ here) * CAP + slot
            route[k, t] = at
            gains[k, t] = weights[k, t]
            weight = jnp.where((sub == t) & (lane == node), weights[k, t], weight)
            stage[at] = tok[t * tall : (t + 1) * tall, :]
    high = weight.astype(BF16).astype(F32)
    middle = (weight - high).astype(BF16).astype(F32)
    low = weight - high - middle
    near[rows] = jnp.concatenate(
        [high, middle, low, jnp.zeros((tall - 3 * rows, LANES), F32)], axis=0
    ).astype(BF16)
    for k, ref in enumerate(far):
        ref[...] = stage[(k + 1) * CAP : (k + 2) * CAP].astype(BF16)


def unpack(refs, blocks, rows, flat, inputs, first=0):
    tall = inputs.shape[1] // LANES
    at = 0
    for ref, count in zip(refs, blocks):
        flat[at * tall : (at + count) * tall, :] = (
            ref[:count].astype(F32).reshape(count * tall, LANES)
        )
        at += count
    if at < rows:
        flat[at * tall : rows * tall, :] = jnp.zeros(((rows - at) * tall, LANES), F32)
    for b in range(tall):
        inputs[first : first + rows, b * LANES : (b + 1) * LANES] = flat[
            pl.ds(b, rows, stride=tall), :
        ].astype(BF16)


def silu_mul(gate, up):
    return (gate / (1.0 + jnp.exp(-gate)) * up).astype(BF16)


def near_shared_kernel(*refs):
    count = len(refs) - 7
    arrived, (gate_w, up_w, down_w), outs = refs[:count], refs[count : count + 3], refs[-4:]
    inputs, weight, value, flat = outs
    here = lax.axis_index("wide")
    tokens, tall = arrived[0].shape[0] - 1, arrived[0].shape[1]
    rows = count * tokens
    unpack(arrived, [tokens] * count, rows, flat, inputs)
    for i, ref in enumerate(arrived):
        parts = ref[tokens].astype(F32)
        whole = (
            parts[:tokens] + parts[tokens : 2 * tokens] + parts[2 * tokens : 3 * tokens]
        )
        lane = lax.broadcasted_iota(jnp.int32, whole.shape, 1)
        gain = jnp.sum(jnp.where(lane == here, whole, 0.0), axis=1, keepdims=True)
        weight[i * tokens : (i + 1) * tokens, :] = jnp.broadcast_to(gain, whole.shape)
    x = inputs[...]
    gate = jnp.dot(x, gate_w[...], preferred_element_type=F32)
    up = jnp.dot(x, up_w[...], preferred_element_type=F32)
    hidden = silu_mul(gate, up)
    for first in range(0, tall * LANES, SPAN * LANES):
        at = slice(first, first + SPAN * LANES)
        value[:, at] = jnp.dot(hidden, down_w[:, at], preferred_element_type=F32)


def routed_kernel(n_narrow, n_pair, per, *refs):
    count = n_narrow * n_pair * per
    arrived, rest = refs[:count], refs[count:]
    near, weight, value, gate_w, up_w, down_w = rest[:6]
    near_outs, outs = rest[6 : 6 + n_pair], rest[6 + n_pair : -2]
    flat, inputs = rest[-2:]
    tall = arrived[0].shape[1]
    near_rows = near.shape[0]
    each = near_rows // n_pair
    blocks = [ref.shape[0] for ref in arrived]
    step = count if sum(blocks) <= MAX_ROWS else per
    for first in range(0, count, step):
        group = blocks[first : first + step]
        head = 0 if first else near_rows
        rows = -(-sum(group) // 16) * 16
        unpack(arrived[first : first + step], group, rows, flat, inputs, head)
        if head:
            inputs[:head] = near[...]
        x = inputs[: head + rows]
        gate = jnp.dot(x, gate_w[...], preferred_element_type=F32)
        up = jnp.dot(x, up_w[...], preferred_element_type=F32)
        hidden = silu_mul(gate, up)
        for at in range(0, tall * LANES, SPAN * LANES):
            part = jnp.dot(
                hidden, down_w[:, at : at + SPAN * LANES], preferred_element_type=F32
            )
            if head:
                part = jnp.concatenate(
                    [
                        value[:, at : at + SPAN * LANES] + weight[:, :1] * part[:head],
                        part[head:],
                    ],
                    axis=0,
                )
            put(flat, at, part, tall)
        if head:
            for c in range(n_pair):
                part = flat[c * each * tall : (c + 1) * each * tall, :]
                near_outs[c][...] = part.reshape(near_outs[c].shape).astype(BF16)
        at = head
        for i, slots in enumerate(group):
            line, k = divmod(first + i, per)
            c, j = divmod(line, n_narrow)
            part = flat[at * tall : (at + slots) * tall, :]
            outs[c * per + k][j] = part.reshape(slots, tall, LANES).astype(BF16)
            at += slots


def pair_sum_kernel(n_pair, cuts, *refs):
    parts, outs = refs[:n_pair], refs[n_pair:]
    for i, out in enumerate(outs):
        j, cut = divmod(i, cuts)
        rows = slice(cut * out.shape[0], (cut + 1) * out.shape[0])
        total = parts[0][j, rows].astype(F32)
        for ref in parts[1:]:
            total = total + ref[j, rows].astype(F32)
        out[...] = total.astype(BF16)


def narrow_sum_kernel(n_narrow, *refs):
    parts, outs = refs[:n_narrow], refs[n_narrow:]
    at = 0
    for out in outs:
        rows = slice(at, at + out.shape[0])
        total = parts[0][rows].astype(F32)
        for ref in parts[1:]:
            total = total + ref[rows].astype(F32)
        out[...] = total.astype(BF16)
        at += out.shape[0]


def far_combine_kernel(order, route, gains, *refs):
    far, (total, stage) = refs[: len(order)], refs[-2:]
    topk, rows = route.shape
    tall = stage.shape[1]
    stage[:CAP] = jnp.zeros((CAP, tall, LANES), F32)
    for k, ref in zip(order, far):
        stage[k * CAP : (k + 1) * CAP] = ref[...].astype(F32)
    for t in range(rows):
        value = gains[0, t] * stage[route[0, t]]
        for k in range(1, topk):
            value = value + gains[k, t] * stage[route[k, t]]
        total[t] = value


def combine_kernel(n_narrow, far, *refs):
    near, (out, total) = refs[:-2], refs[-2:]
    rows, features = out.shape
    tall = features // LANES
    for t in range(rows):
        value = far[t]
        cut, row = divmod(t, rows // HALVES)
        for ref in near[cut * n_narrow : (cut + 1) * n_narrow]:
            value = value + ref[row].astype(F32)
        total[t * tall : (t + 1) * tall, :] = value
    for b in range(tall):
        out[:, b * LANES : (b + 1) * LANES] = total[
            pl.ds(b, rows, stride=tall), :
        ].astype(BF16)


def swap(value, axis, offset):
    size = lax.axis_size(axis)
    return lax.ppermute(value, axis, [(i, i ^ offset) for i in range(size)])


def in_hbm(*values):
    return [pltpu.with_memory_space_constraint(value, pltpu.HBM) for value in values]


def after(values, *others):
    return list(lax.optimization_barrier((tuple(values), others))[0])


def call(kernel, name, ins, specs, outs, scratch, flops=0, moved=0, limit=16):
    return pl.pallas_call(
        kernel,
        out_shape=outs,
        in_specs=specs,
        out_specs=jax.tree.map(
            lambda out: SSPEC if getattr(out, "memory_space", None) == pltpu.SMEM else VSPEC,
            outs,
        ),
        scratch_shapes=scratch,
        compiler_params=pltpu.CompilerParams(vmem_limit_bytes=limit << 20),
        cost_estimate=pl.CostEstimate(flops=flops, bytes_accessed=moved, transcendentals=0),
        name=name,
    )(*ins)


def shards(
    row_codes,
    row_scales,
    expert_ids,
    gate_weights,
    placement,
    w_gate,
    w_up,
    w_down,
    shared_gate,
    shared_up,
    shared_down,
):
    n_wide = lax.axis_size("wide")
    n_narrow = lax.axis_size("narrow")
    n_pair = lax.axis_size("pair")
    tokens, features = row_codes.shape
    hidden = w_gate.shape[2]
    tall = features // LANES
    topk = expert_ids.shape[1]
    limit = 16 if n_wide <= 4 else 48

    def block(*lead):
        return jax.ShapeDtypeStruct(lead + (tall, LANES), BF16)

    shared = [shared_gate, shared_up, shared_down]
    routed = [
        w_gate.reshape(features, hidden),
        w_up.reshape(features, hidden),
        w_down.reshape(hidden, features),
    ]
    near, *far = call(
        dispatch_kernel,
        "dispatch",
        in_hbm(expert_ids.T, placement, gate_weights.T, row_codes, row_scales)
        + in_hbm(*shared, *routed),
        [ASPEC] * 11,
        [block(tokens + 1)]
        + [block(CAP)] * (n_wide - 1)
        + [pltpu.SMEM((topk, tokens), jnp.int32), pltpu.SMEM((topk, tokens), F32)],
        [
            pltpu.SMEM((topk, tokens), jnp.int32),
            pltpu.SMEM(placement.shape, jnp.int32),
            pltpu.SMEM((topk, tokens), F32),
            VMEM((tokens, features), BF16),
            VMEM(row_scales.shape, BF16),
            VMEM((tokens * tall, LANES), F32),
            VMEM((n_wide * CAP, tall, LANES), F32),
            pltpu.SemaphoreType.DMA((5,)),
        ],
    )
    far, (route, gains) = far[:-2], far[-2:]
    order = list(range(n_wide - 1, 1, -1))
    across = ("wide", "narrow")
    bundles = [swap(far[k - 1], "wide", k) for k in order]
    direct = [swap(far[0], across, n_narrow + j) for j in range(n_narrow)]
    near_line = [near] + [swap(near, "narrow", j) for j in range(1, n_narrow)]
    bundles = after(bundles, *direct)
    if n_wide > 4:
        bundles = [jnp.concatenate(bundles, axis=0)]
    lines = [list(bundles)]
    for j in range(1, n_narrow):
        lines.append([swap(value, "narrow", j) for value in bundles])
    per = len(bundles) + 1
    slots = [value.shape[0] for value in bundles] + [CAP]
    near_line = after(near_line, *bundles)
    near_all = list(near_line)
    for c in range(1, n_pair):
        near_all += [swap(value, "pair", c) for value in near_line]

    near_rows = n_narrow * n_pair * tokens
    near_mid = call(
        near_shared_kernel,
        "near_shared",
        near_all + shared,
        [VSPEC] * (n_narrow * n_pair + 3),
        [
            jax.ShapeDtypeStruct((near_rows, features), BF16),
            jax.ShapeDtypeStruct((near_rows, LANES), F32),
            jax.ShapeDtypeStruct((near_rows, features), F32),
        ],
        [VMEM((near_rows * tall, LANES), F32)],
        flops=6 * near_rows * features * hidden,
        moved=6 * features * hidden,
        limit=limit,
    )
    side = after([value for line in lines[1:] for value in line], near_mid[1])
    far_line = []
    for j in range(n_narrow):
        far_line += lines[0] if j == 0 else side[(j - 1) * (per - 1) : j * (per - 1)]
        far_line.append(direct[j])
    far_all = list(far_line)
    for c in range(1, n_pair):
        far_all += [swap(value, "pair", c) for value in far_line]

    far_rows = n_narrow * n_pair * sum(slots)
    pass_rows = far_rows if far_rows <= MAX_ROWS else sum(slots)
    pass_rows = near_rows + -(-pass_rows // 16) * 16
    outs = call(
        functools.partial(routed_kernel, n_narrow, n_pair, per),
        "routed",
        far_all + list(near_mid) + routed,
        [VSPEC] * (n_narrow * n_pair * per + 6),
        [block(n_narrow, tokens)] * n_pair
        + [block(n_narrow, count) for count in slots] * n_pair,
        [VMEM((pass_rows * tall, LANES), F32), VMEM((pass_rows, features), BF16)],
        flops=6 * (near_rows + far_rows) * features * hidden,
        moved=6 * features * hidden,
        limit=limit,
    )
    near_out, far_out = outs[:n_pair], outs[n_pair:]

    def reduce_pair(parts, *first, cuts=1):
        rows = parts[0].shape[1]
        return call(
            functools.partial(pair_sum_kernel, n_pair, cuts),
            "pair_sum",
            after([parts[0]] + [swap(parts[c], "pair", c) for c in range(1, n_pair)], *first),
            [VSPEC] * n_pair,
            [block(rows // cuts)] * (n_narrow * cuts),
            [],
            limit=limit,
        )

    def send_narrow(parts):
        return [parts[0]] + [swap(parts[j], "narrow", j) for j in range(1, n_narrow)]

    sums = []
    for k in range(per):
        sums += call(
            functools.partial(narrow_sum_kernel, n_narrow),
            "narrow_sum",
            send_narrow(reduce_pair(far_out[k::per])),
            [VSPEC] * n_narrow,
            [block(CAP)] * (slots[k] // CAP),
            [],
            limit=limit,
        )
    order.append(1)
    far_back = [swap(value, "wide", k) for k, value in zip(order, sums)]
    near_parts = reduce_pair(near_out, cuts=HALVES)
    near_back = []
    for cut in range(HALVES):
        near_back += send_narrow(near_parts[cut::HALVES])
    far_sum = call(
        functools.partial(far_combine_kernel, order),
        "far_combine",
        [route, gains] + far_back,
        [SSPEC] * 2 + [VSPEC] * len(order),
        jax.ShapeDtypeStruct((tokens, tall, LANES), F32),
        [VMEM((n_wide * CAP, tall, LANES), F32)],
    )
    return call(
        functools.partial(combine_kernel, n_narrow),
        "combine",
        [far_sum] + near_back,
        [VSPEC] * (1 + HALVES * n_narrow),
        jax.ShapeDtypeStruct((tokens, features), BF16),
        [VMEM((tokens * tall, LANES), F32)],
    )


def solution(mesh):
    rows = P(("groups", "wide", "narrow", "pair"), None)
    return jax.shard_map(
        shards,
        mesh=mesh,
        in_specs=(
            rows,
            rows,
            rows,
            rows,
            P(),
            P("wide", None, ("narrow", "pair")),
            P("wide", None, ("narrow", "pair")),
            P("wide", ("narrow", "pair"), None),
            P(None, ("narrow", "pair")),
            P(None, ("narrow", "pair")),
            P(("narrow", "pair"), None),
        ),
        out_specs=rows,
        check_vma=False,
    )
```

```python
import functools

import jax
import jax.numpy as jnp
from jax import lax
from jax.experimental import pallas as pl
from jax.experimental.pallas import tpu as pltpu
from jax.sharding import PartitionSpec as P

CAP = 5
LANES = 128
SPAN = 7
HALVES = 1
MAX_ROWS = 128

VMEM = pltpu.VMEM
VSPEC = pl.BlockSpec(memory_space=pltpu.VMEM)
SSPEC = pl.BlockSpec(memory_space=pltpu.SMEM)
ASPEC = pl.BlockSpec(memory_space=pl.ANY)
F32 = jnp.float32
BF16 = jnp.bfloat16


def put(flat, at, value, tall):
    rows = value.shape[0]
    for b in range(value.shape[1] // LANES):
        flat[pl.ds(at // LANES + b, rows, stride=tall), :] = value[
            :, b * LANES : (b + 1) * LANES
        ]


def dispatch_kernel(ids_in, place_in, weights_in, codes_in, scales_in, *refs):
    refs = refs[6:]
    near, far = refs[0], refs[1:-10]
    route, gains = refs[-10:-8]
    ids, place, weights, codes, scales, tok, stage, sems = refs[-8:]
    copies = [
        pltpu.make_async_copy(src, dst, sems.at[i])
        for i, (src, dst) in enumerate(
            (
                (codes_in, codes),
                (scales_in, scales),
                (ids_in, ids),
                (place_in, place),
                (weights_in, weights),
            )
        )
    ]
    for copy in copies:
        copy.start()
    here = lax.axis_index("wide")
    rows, features = codes.shape
    topk = ids.shape[0]
    tall = features // LANES
    stage[...] = jnp.zeros_like(stage)
    for copy in copies:
        copy.wait()
    for b in range(tall):
        block = codes[:, b * LANES : (b + 1) * LANES].astype(F32)
        tok[pl.ds(b, rows, stride=tall), :] = block * scales[:, b : b + 1].astype(F32)
    near[:rows] = tok[...].reshape(rows, tall, LANES).astype(BF16)
    sub = lax.broadcasted_iota(jnp.int32, (rows, LANES), 0)
    lane = lax.broadcasted_iota(jnp.int32, (rows, LANES), 1)
    weight = jnp.zeros((rows, LANES), F32)
    named = []
    for t in range(rows):
        for k in range(topk):
            e = ids[k, t]
            node = place[e]
            slot = jnp.int32(0)
            for other in named[: t * topk]:
                slot = slot + jnp.where(other == e, 1, 0)
            named.append(e)
            at = (node ^ here) * CAP + slot
            route[k, t] = at
            gains[k, t] = weights[k, t]
            weight = jnp.where((sub == t) & (lane == node), weights[k, t], weight)
            stage[at] = tok[t * tall : (t + 1) * tall, :]
    high = weight.astype(BF16).astype(F32)
    middle = (weight - high).astype(BF16).astype(F32)
    low = weight - high - middle
    near[rows] = jnp.concatenate(
        [high, middle, low, jnp.zeros((tall - 3 * rows, LANES), F32)], axis=0
    ).astype(BF16)
    for k, ref in enumerate(far):
        ref[...] = stage[(k + 1) * CAP : (k + 2) * CAP].astype(BF16)


def unpack(refs, blocks, rows, flat, inputs, first=0):
    tall = inputs.shape[1] // LANES
    at = 0
    for ref, count in zip(refs, blocks):
        flat[at * tall : (at + count) * tall, :] = (
            ref[:count].astype(F32).reshape(count * tall, LANES)
        )
        at += count
    if at < rows:
        flat[at * tall : rows * tall, :] = jnp.zeros(((rows - at) * tall, LANES), F32)
    for b in range(tall):
        inputs[first : first + rows, b * LANES : (b + 1) * LANES] = flat[
            pl.ds(b, rows, stride=tall), :
        ].astype(BF16)


def silu_mul(gate, up):
    return (gate / (1.0 + jnp.exp(-gate)) * up).astype(BF16)


def near_shared_kernel(*refs):
    count = len(refs) - 7
    arrived, (gate_w, up_w, down_w), outs = refs[:count], refs[count : count + 3], refs[-4:]
    inputs, weight, value, flat = outs
    here = lax.axis_index("wide")
    tokens, tall = arrived[0].shape[0] - 1, arrived[0].shape[1]
    rows = count * tokens
    unpack(arrived, [tokens] * count, rows, flat, inputs)
    for i, ref in enumerate(arrived):
        parts = ref[tokens].astype(F32)
        whole = (
            parts[:tokens] + parts[tokens : 2 * tokens] + parts[2 * tokens : 3 * tokens]
        )
        lane = lax.broadcasted_iota(jnp.int32, whole.shape, 1)
        gain = jnp.sum(jnp.where(lane == here, whole, 0.0), axis=1, keepdims=True)
        weight[i * tokens : (i + 1) * tokens, :] = jnp.broadcast_to(gain, whole.shape)
    x = inputs[...]
    gate = jnp.dot(x, gate_w[...], preferred_element_type=F32)
    up = jnp.dot(x, up_w[...], preferred_element_type=F32)
    hidden = silu_mul(gate, up)
    for first in range(0, tall * LANES, SPAN * LANES):
        at = slice(first, first + SPAN * LANES)
        value[:, at] = jnp.dot(hidden, down_w[:, at], preferred_element_type=F32)


def routed_kernel(n_narrow, n_pair, per, *refs):
    count = n_narrow * n_pair * per
    arrived, rest = refs[:count], refs[count:]
    near, weight, value, gate_w, up_w, down_w = rest[:6]
    near_outs, outs = rest[6 : 6 + n_pair], rest[6 + n_pair : -2]
    flat, inputs = rest[-2:]
    tall = arrived[0].shape[1]
    near_rows = near.shape[0]
    each = near_rows // n_pair
    blocks = [ref.shape[0] for ref in arrived]
    step = count if sum(blocks) <= MAX_ROWS else per
    for first in range(0, count, step):
        group = blocks[first : first + step]
        head = 0 if first else near_rows
        rows = -(-sum(group) // 16) * 16
        unpack(arrived[first : first + step], group, rows, flat, inputs, head)
        if head:
            inputs[:head] = near[...]
        x = inputs[: head + rows]
        gate = jnp.dot(x, gate_w[...], preferred_element_type=F32)
        up = jnp.dot(x, up_w[...], preferred_element_type=F32)
        hidden = silu_mul(gate, up)
        for at in range(0, tall * LANES, SPAN * LANES):
            part = jnp.dot(
                hidden, down_w[:, at : at + SPAN * LANES], preferred_element_type=F32
            )
            if head:
                part = jnp.concatenate(
                    [
                        value[:, at : at + SPAN * LANES] + weight[:, :1] * part[:head],
                        part[head:],
                    ],
                    axis=0,
                )
            put(flat, at, part, tall)
        if head:
            for c in range(n_pair):
                part = flat[c * each * tall : (c + 1) * each * tall, :]
                near_outs[c][...] = part.reshape(near_outs[c].shape).astype(BF16)
        at = head
        for i, slots in enumerate(group):
            line, k = divmod(first + i, per)
            c, j = divmod(line, n_narrow)
            part = flat[at * tall : (at + slots) * tall, :]
            outs[c * per + k][j] = part.reshape(slots, tall, LANES).astype(BF16)
            at += slots


def pair_sum_kernel(n_pair, cuts, *refs):
    parts, outs = refs[:n_pair], refs[n_pair:]
    for i, out in enumerate(outs):
        j, cut = divmod(i, cuts)
        rows = slice(cut * out.shape[0], (cut + 1) * out.shape[0])
        total = parts[0][j, rows].astype(F32)
        for ref in parts[1:]:
            total = total + ref[j, rows].astype(F32)
        out[...] = total.astype(BF16)


def narrow_sum_kernel(n_narrow, *refs):
    parts, outs = refs[:n_narrow], refs[n_narrow:]
    at = 0
    for out in outs:
        rows = slice(at, at + out.shape[0])
        total = parts[0][rows].astype(F32)
        for ref in parts[1:]:
            total = total + ref[rows].astype(F32)
        out[...] = total.astype(BF16)
        at += out.shape[0]


def far_combine_kernel(order, route, gains, *refs):
    far, (total, stage) = refs[: len(order)], refs[-2:]
    topk, rows = route.shape
    tall = stage.shape[1]
    stage[:CAP] = jnp.zeros((CAP, tall, LANES), F32)
    for k, ref in zip(order, far):
        stage[k * CAP : (k + 1) * CAP] = ref[...].astype(F32)
    for t in range(rows):
        value = gains[0, t] * stage[route[0, t]]
        for k in range(1, topk):
            value = value + gains[k, t] * stage[route[k, t]]
        total[t] = value


def combine_kernel(n_narrow, far, *refs):
    near, (out, total) = refs[:-2], refs[-2:]
    rows, features = out.shape
    tall = features // LANES
    for t in range(rows):
        value = far[t]
        cut, row = divmod(t, rows // HALVES)
        for ref in near[cut * n_narrow : (cut + 1) * n_narrow]:
            value = value + ref[row].astype(F32)
        total[t * tall : (t + 1) * tall, :] = value
    for b in range(tall):
        out[:, b * LANES : (b + 1) * LANES] = total[
            pl.ds(b, rows, stride=tall), :
        ].astype(BF16)


def swap(value, axis, offset):
    size = lax.axis_size(axis)
    return lax.ppermute(value, axis, [(i, i ^ offset) for i in range(size)])


def in_hbm(*values):
    return [pltpu.with_memory_space_constraint(value, pltpu.HBM) for value in values]


def after(values, *others):
    return list(lax.optimization_barrier((tuple(values), others))[0])


def call(kernel, name, ins, specs, outs, scratch, flops=0, moved=0, limit=16):
    return pl.pallas_call(
        kernel,
        out_shape=outs,
        in_specs=specs,
        out_specs=jax.tree.map(
            lambda out: SSPEC if getattr(out, "memory_space", None) == pltpu.SMEM else VSPEC,
            outs,
        ),
        scratch_shapes=scratch,
        compiler_params=pltpu.CompilerParams(vmem_limit_bytes=limit << 20),
        cost_estimate=pl.CostEstimate(flops=flops, bytes_accessed=moved, transcendentals=0),
        name=name,
    )(*ins)


def shards(
    row_codes,
    row_scales,
    expert_ids,
    gate_weights,
    placement,
    w_gate,
    w_up,
    w_down,
    shared_gate,
    shared_up,
    shared_down,
):
    n_wide = lax.axis_size("wide")
    n_narrow = lax.axis_size("narrow")
    n_pair = lax.axis_size("pair")
    tokens, features = row_codes.shape
    hidden = w_gate.shape[2]
    tall = features // LANES
    topk = expert_ids.shape[1]
    limit = 16 if n_wide <= 4 else 48

    def block(*lead):
        return jax.ShapeDtypeStruct(lead + (tall, LANES), BF16)

    shared = [shared_gate, shared_up, shared_down]
    routed = [
        w_gate.reshape(features, hidden),
        w_up.reshape(features, hidden),
        w_down.reshape(hidden, features),
    ]
    near, *far = call(
        dispatch_kernel,
        "dispatch",
        in_hbm(expert_ids.T, placement, gate_weights.T, row_codes, row_scales)
        + in_hbm(*shared, *routed),
        [ASPEC] * 11,
        [block(tokens + 1)]
        + [block(CAP)] * (n_wide - 1)
        + [pltpu.SMEM((topk, tokens), jnp.int32), pltpu.SMEM((topk, tokens), F32)],
        [
            pltpu.SMEM((topk, tokens), jnp.int32),
            pltpu.SMEM(placement.shape, jnp.int32),
            pltpu.SMEM((topk, tokens), F32),
            VMEM((tokens, features), BF16),
            VMEM(row_scales.shape, BF16),
            VMEM((tokens * tall, LANES), F32),
            VMEM((n_wide * CAP, tall, LANES), F32),
            pltpu.SemaphoreType.DMA((5,)),
        ],
    )
    far, (route, gains) = far[:-2], far[-2:]
    order = list(range(n_wide - 1, 0, -1))
    bundles = [swap(far[k - 1], "wide", k) for k in order]
    near_line = [near] + [swap(near, "narrow", j) for j in range(1, n_narrow)]
    if n_wide > 4:
        bundles = [jnp.concatenate(bundles, axis=0)]
    lines = [list(bundles)]
    for j in range(1, n_narrow):
        lines.append([swap(value, "narrow", j) for value in bundles])
    per = len(bundles)
    slots = [value.shape[0] for value in bundles]
    near_line = after(near_line, *bundles)
    near_all = list(near_line)
    for c in range(1, n_pair):
        near_all += [swap(value, "pair", c) for value in near_line]

    near_rows = n_narrow * n_pair * tokens
    near_mid = call(
        near_shared_kernel,
        "near_shared",
        near_all + shared,
        [VSPEC] * (n_narrow * n_pair + 3),
        [
            jax.ShapeDtypeStruct((near_rows, features), BF16),
            jax.ShapeDtypeStruct((near_rows, LANES), F32),
            jax.ShapeDtypeStruct((near_rows, features), F32),
        ],
        [VMEM((near_rows * tall, LANES), F32)],
        flops=6 * near_rows * features * hidden,
        moved=6 * features * hidden,
        limit=limit,
    )
    side = after([value for line in lines[1:] for value in line], near_mid[1])
    far_line = []
    for j in range(n_narrow):
        far_line += lines[0] if j == 0 else side[(j - 1) * per : j * per]
    far_all = list(far_line)
    for c in range(1, n_pair):
        far_all += [swap(value, "pair", c) for value in far_line]

    far_rows = n_narrow * n_pair * sum(slots)
    pass_rows = far_rows if far_rows <= MAX_ROWS else sum(slots)
    pass_rows = near_rows + -(-pass_rows // 16) * 16
    outs = call(
        functools.partial(routed_kernel, n_narrow, n_pair, per),
        "routed",
        far_all + list(near_mid) + routed,
        [VSPEC] * (n_narrow * n_pair * per + 6),
        [block(n_narrow, tokens)] * n_pair
        + [block(n_narrow, count) for count in slots] * n_pair,
        [VMEM((pass_rows * tall, LANES), F32), VMEM((pass_rows, features), BF16)],
        flops=6 * (near_rows + far_rows) * features * hidden,
        moved=6 * features * hidden,
        limit=limit,
    )
    near_out, far_out = outs[:n_pair], outs[n_pair:]

    def reduce_pair(parts, *first, cuts=1):
        rows = parts[0].shape[1]
        return call(
            functools.partial(pair_sum_kernel, n_pair, cuts),
            "pair_sum",
            after([parts[0]] + [swap(parts[c], "pair", c) for c in range(1, n_pair)], *first),
            [VSPEC] * n_pair,
            [block(rows // cuts)] * (n_narrow * cuts),
            [],
            limit=limit,
        )

    def send_narrow(parts):
        return [parts[0]] + [swap(parts[j], "narrow", j) for j in range(1, n_narrow)]

    sums = []
    for k in range(per):
        sums += call(
            functools.partial(narrow_sum_kernel, n_narrow),
            "narrow_sum",
            send_narrow(reduce_pair(far_out[k::per])),
            [VSPEC] * n_narrow,
            [block(CAP)] * (slots[k] // CAP),
            [],
            limit=limit,
        )
    far_back = [swap(value, "wide", k) for k, value in zip(order, sums)]
    near_parts = reduce_pair(near_out, cuts=HALVES)
    near_back = []
    for cut in range(HALVES):
        near_back += send_narrow(near_parts[cut::HALVES])
    far_sum = call(
        functools.partial(far_combine_kernel, order),
        "far_combine",
        [route, gains] + far_back,
        [SSPEC] * 2 + [VSPEC] * len(order),
        jax.ShapeDtypeStruct((tokens, tall, LANES), F32),
        [VMEM((n_wide * CAP, tall, LANES), F32)],
    )
    return call(
        functools.partial(combine_kernel, n_narrow),
        "combine",
        [far_sum] + near_back,
        [VSPEC] * (1 + HALVES * n_narrow),
        jax.ShapeDtypeStruct((tokens, features), BF16),
        [VMEM((tokens * tall, LANES), F32)],
    )


def solution(mesh):
    rows = P(("groups", "wide", "narrow", "pair"), None)
    return jax.shard_map(
        shards,
        mesh=mesh,
        in_specs=(
            rows,
            rows,
            rows,
            rows,
            P(),
            P("wide", None, ("narrow", "pair")),
            P("wide", None, ("narrow", "pair")),
            P("wide", ("narrow", "pair"), None),
            P(None, ("narrow", "pair")),
            P(None, ("narrow", "pair")),
            P(("narrow", "pair"), None),
        ),
        out_specs=rows,
        check_vma=False,
    )
```

```python
import functools

import jax
import jax.numpy as jnp
from jax import lax
from jax.experimental import pallas as pl
from jax.experimental.pallas import tpu as pltpu
from jax.sharding import PartitionSpec as P

CAP = 5
LANES = 128
SPAN = 7
MAX_ROWS = 128

VMEM = pltpu.VMEM
VSPEC = pl.BlockSpec(memory_space=pltpu.VMEM)
SSPEC = pl.BlockSpec(memory_space=pltpu.SMEM)
ASPEC = pl.BlockSpec(memory_space=pl.ANY)
F32 = jnp.float32
BF16 = jnp.bfloat16


def put(flat, at, value, tall):
    rows = value.shape[0]
    for b in range(value.shape[1] // LANES):
        flat[pl.ds(at // LANES + b, rows, stride=tall), :] = value[
            :, b * LANES : (b + 1) * LANES
        ]


def dispatch_kernel(ids_in, place_in, weights_in, codes_in, scales_in, *refs):
    refs = refs[6:]
    near, far = refs[0], refs[1:-10]
    route, gains = refs[-10:-8]
    ids, place, weights, codes, scales, tok, stage, sems = refs[-8:]
    copies = [
        pltpu.make_async_copy(src, dst, sems.at[i])
        for i, (src, dst) in enumerate(
            (
                (codes_in, codes),
                (scales_in, scales),
                (ids_in, ids),
                (place_in, place),
                (weights_in, weights),
            )
        )
    ]
    for copy in copies:
        copy.start()
    here = lax.axis_index("wide")
    rows, features = codes.shape
    topk = ids.shape[0]
    tall = features // LANES
    stage[...] = jnp.zeros_like(stage)
    for copy in copies:
        copy.wait()
    for b in range(tall):
        block = codes[:, b * LANES : (b + 1) * LANES].astype(F32)
        tok[pl.ds(b, rows, stride=tall), :] = block * scales[:, b : b + 1].astype(F32)
    near[:rows] = tok[...].reshape(rows, tall, LANES).astype(BF16)
    sub = lax.broadcasted_iota(jnp.int32, (rows, LANES), 0)
    lane = lax.broadcasted_iota(jnp.int32, (rows, LANES), 1)
    weight = jnp.zeros((rows, LANES), F32)
    named = []
    for t in range(rows):
        for k in range(topk):
            e = ids[k, t]
            node = place[e]
            slot = jnp.int32(0)
            for other in named[: t * topk]:
                slot = slot + jnp.where(other == e, 1, 0)
            named.append(e)
            at = (node ^ here) * CAP + slot
            route[k, t] = at
            gains[k, t] = weights[k, t]
            weight = jnp.where((sub == t) & (lane == node), weights[k, t], weight)
            stage[at] = tok[t * tall : (t + 1) * tall, :]
    high = weight.astype(BF16).astype(F32)
    middle = (weight - high).astype(BF16).astype(F32)
    low = weight - high - middle
    near[rows] = jnp.concatenate(
        [high, middle, low, jnp.zeros((tall - 3 * rows, LANES), F32)], axis=0
    ).astype(BF16)
    for k, ref in enumerate(far):
        ref[...] = stage[(k + 1) * CAP : (k + 2) * CAP].astype(BF16)


def unpack(refs, blocks, rows, flat, inputs, first=0):
    tall = inputs.shape[1] // LANES
    at = 0
    for ref, count in zip(refs, blocks):
        flat[at * tall : (at + count) * tall, :] = (
            ref[:count].astype(F32).reshape(count * tall, LANES)
        )
        at += count
    if at < rows:
        flat[at * tall : rows * tall, :] = jnp.zeros(((rows - at) * tall, LANES), F32)
    for b in range(tall):
        inputs[first : first + rows, b * LANES : (b + 1) * LANES] = flat[
            pl.ds(b, rows, stride=tall), :
        ].astype(BF16)


def silu_mul(gate, up):
    return (gate / (1.0 + jnp.exp(-gate)) * up).astype(BF16)


def near_shared_kernel(*refs):
    count = len(refs) - 7
    arrived, (gate_w, up_w, down_w), outs = refs[:count], refs[count : count + 3], refs[-4:]
    inputs, weight, value, flat = outs
    here = lax.axis_index("wide")
    tokens, tall = arrived[0].shape[0] - 1, arrived[0].shape[1]
    rows = count * tokens
    unpack(arrived, [tokens] * count, rows, flat, inputs)
    for i, ref in enumerate(arrived):
        parts = ref[tokens].astype(F32)
        whole = (
            parts[:tokens] + parts[tokens : 2 * tokens] + parts[2 * tokens : 3 * tokens]
        )
        lane = lax.broadcasted_iota(jnp.int32, whole.shape, 1)
        gain = jnp.sum(jnp.where(lane == here, whole, 0.0), axis=1, keepdims=True)
        weight[i * tokens : (i + 1) * tokens, :] = jnp.broadcast_to(gain, whole.shape)
    x = inputs[...]
    gate = jnp.dot(x, gate_w[...], preferred_element_type=F32)
    up = jnp.dot(x, up_w[...], preferred_element_type=F32)
    hidden = silu_mul(gate, up)
    for first in range(0, tall * LANES, SPAN * LANES):
        at = slice(first, first + SPAN * LANES)
        value[:, at] = jnp.dot(hidden, down_w[:, at], preferred_element_type=F32)


def routed_kernel(n_narrow, n_pair, per, *refs):
    count = n_narrow * n_pair * per
    arrived, rest = refs[:count], refs[count:]
    near, weight, value, gate_w, up_w, down_w = rest[:6]
    first_outs, outs = rest[6 : 6 + n_pair], rest[6 + n_pair : -2]
    flat, inputs = rest[-2:]
    tall = arrived[0].shape[1]
    near_rows = near.shape[0]
    each = near_rows // n_pair
    blocks = [ref.shape[0] for ref in arrived]
    step = count if sum(blocks) <= MAX_ROWS else per
    for first in range(0, count, step):
        group = blocks[first : first + step]
        head = 0 if first else near_rows
        rows = -(-sum(group) // 16) * 16
        unpack(arrived[first : first + step], group, rows, flat, inputs, head)
        if head:
            inputs[:head] = near[...]
        x = inputs[: head + rows]
        gate = jnp.dot(x, gate_w[...], preferred_element_type=F32)
        up = jnp.dot(x, up_w[...], preferred_element_type=F32)
        hidden = silu_mul(gate, up)
        for at in range(0, tall * LANES, SPAN * LANES):
            part = jnp.dot(
                hidden, down_w[:, at : at + SPAN * LANES], preferred_element_type=F32
            )
            if head:
                part = jnp.concatenate(
                    [
                        value[:, at : at + SPAN * LANES] + weight[:, :1] * part[:head],
                        part[head:],
                    ],
                    axis=0,
                )
            put(flat, at, part, tall)
        if head:
            for c in range(n_pair):
                part = flat[c * each * tall : (c + 1) * each * tall, :]
                part = part.reshape(n_narrow, each // n_narrow, tall, LANES)
                outs[c][:, outs[c].shape[1] - part.shape[1] :] = part.astype(BF16)
        at = head
        for i, slots in enumerate(group):
            line, k = divmod(first + i, per)
            c, j = divmod(line, n_narrow)
            part = flat[at * tall : (at + slots) * tall, :]
            part = part.reshape(slots, tall, LANES).astype(BF16)
            if k == 0:
                first_outs[c][j] = part
            else:
                start = sum(blocks[1:k])
                outs[c][j, start : start + slots] = part
            at += slots


def pair_sum_kernel(n_pair, n_narrow, *refs):
    parts, outs = refs[:n_pair], refs[n_pair:]
    at = 0
    for first in range(0, len(outs), n_narrow):
        rows = slice(at, at + outs[first].shape[0])
        for j in range(n_narrow):
            total = parts[0][j, rows].astype(F32)
            for ref in parts[1:]:
                total = total + ref[j, rows].astype(F32)
            outs[first + j][...] = total.astype(BF16)
        at = rows.stop


def narrow_sum_kernel(n_narrow, *refs):
    parts, outs = refs[:n_narrow], refs[n_narrow:]
    at = 0
    for out in outs:
        rows = slice(at, at + out.shape[0])
        total = parts[0][rows].astype(F32)
        for ref in parts[1:]:
            total = total + ref[rows].astype(F32)
        out[...] = total.astype(BF16)
        at += out.shape[0]


def far_combine_kernel(order, route, gains, *refs):
    far, (total, stage) = refs[: len(order)], refs[-2:]
    topk, rows = route.shape
    tall = stage.shape[1]
    stage[:CAP] = jnp.zeros((CAP, tall, LANES), F32)
    for k, ref in zip(order, far):
        stage[k * CAP : (k + 1) * CAP] = ref[...].astype(F32)
    for t in range(rows):
        value = gains[0, t] * stage[route[0, t]]
        for k in range(1, topk):
            value = value + gains[k, t] * stage[route[k, t]]
        total[t] = value


def combine_kernel(far, *refs):
    near, (out, total) = refs[:-2], refs[-2:]
    rows, features = out.shape
    tall = features // LANES
    for t in range(rows):
        value = far[t]
        for ref in near:
            value = value + ref[t].astype(F32)
        total[t * tall : (t + 1) * tall, :] = value
    for b in range(tall):
        out[:, b * LANES : (b + 1) * LANES] = total[
            pl.ds(b, rows, stride=tall), :
        ].astype(BF16)


def swap(value, axis, offset):
    size = lax.axis_size(axis)
    return lax.ppermute(value, axis, [(i, i ^ offset) for i in range(size)])


def in_hbm(*values):
    return [pltpu.with_memory_space_constraint(value, pltpu.HBM) for value in values]


def after(values, *others):
    return list(lax.optimization_barrier((tuple(values), others))[0])


def call(kernel, name, ins, specs, outs, scratch, flops=0, moved=0, limit=16):
    return pl.pallas_call(
        kernel,
        out_shape=outs,
        in_specs=specs,
        out_specs=jax.tree.map(
            lambda out: SSPEC if getattr(out, "memory_space", None) == pltpu.SMEM else VSPEC,
            outs,
        ),
        scratch_shapes=scratch,
        compiler_params=pltpu.CompilerParams(vmem_limit_bytes=limit << 20),
        cost_estimate=pl.CostEstimate(flops=flops, bytes_accessed=moved, transcendentals=0),
        name=name,
    )(*ins)


def shards(
    row_codes,
    row_scales,
    expert_ids,
    gate_weights,
    placement,
    w_gate,
    w_up,
    w_down,
    shared_gate,
    shared_up,
    shared_down,
):
    n_wide = lax.axis_size("wide")
    n_narrow = lax.axis_size("narrow")
    n_pair = lax.axis_size("pair")
    tokens, features = row_codes.shape
    hidden = w_gate.shape[2]
    tall = features // LANES
    topk = expert_ids.shape[1]
    limit = 16 if n_wide <= 4 else 48

    def block(*lead):
        return jax.ShapeDtypeStruct(lead + (tall, LANES), BF16)

    shared = [shared_gate, shared_up, shared_down]
    routed = [
        w_gate.reshape(features, hidden),
        w_up.reshape(features, hidden),
        w_down.reshape(hidden, features),
    ]
    near, *far = call(
        dispatch_kernel,
        "dispatch",
        in_hbm(expert_ids.T, placement, gate_weights.T, row_codes, row_scales)
        + in_hbm(*shared, *routed),
        [ASPEC] * 11,
        [block(tokens + 1)]
        + [block(CAP)] * (n_wide - 1)
        + [pltpu.SMEM((topk, tokens), jnp.int32), pltpu.SMEM((topk, tokens), F32)],
        [
            pltpu.SMEM((topk, tokens), jnp.int32),
            pltpu.SMEM(placement.shape, jnp.int32),
            pltpu.SMEM((topk, tokens), F32),
            VMEM((tokens, features), BF16),
            VMEM(row_scales.shape, BF16),
            VMEM((tokens * tall, LANES), F32),
            VMEM((n_wide * CAP, tall, LANES), F32),
            pltpu.SemaphoreType.DMA((5,)),
        ],
    )
    far, (route, gains) = far[:-2], far[-2:]
    order = list(range(n_wide - 1, 1, -1))
    across = ("wide", "narrow")
    bundles = [swap(far[k - 1], "wide", k) for k in order]
    direct = [swap(far[0], across, n_narrow + j) for j in range(n_narrow)]
    near_line = [near] + [swap(near, "narrow", j) for j in range(1, n_narrow)]
    bundles = after(bundles, *direct)
    if n_wide > 4:
        bundles = [jnp.concatenate(bundles, axis=0)]
    lines = [list(bundles)]
    for j in range(1, n_narrow):
        lines.append([swap(value, "narrow", j) for value in bundles])
    per = len(bundles) + 1
    slots = [value.shape[0] for value in bundles] + [CAP]
    near_line = after(near_line, *bundles)
    near_all = list(near_line)
    for c in range(1, n_pair):
        near_all += [swap(value, "pair", c) for value in near_line]

    near_rows = n_narrow * n_pair * tokens
    near_mid = call(
        near_shared_kernel,
        "near_shared",
        near_all + shared,
        [VSPEC] * (n_narrow * n_pair + 3),
        [
            jax.ShapeDtypeStruct((near_rows, features), BF16),
            jax.ShapeDtypeStruct((near_rows, LANES), F32),
            jax.ShapeDtypeStruct((near_rows, features), F32),
        ],
        [VMEM((near_rows * tall, LANES), F32)],
        flops=6 * near_rows * features * hidden,
        moved=6 * features * hidden,
        limit=limit,
    )
    side = after([value for line in lines[1:] for value in line], near_mid[1])
    far_line = []
    for j in range(n_narrow):
        far_line += lines[0] if j == 0 else side[(j - 1) * (per - 1) : j * (per - 1)]
        far_line.append(direct[j])
    far_all = list(far_line)
    for c in range(1, n_pair):
        far_all += [swap(value, "pair", c) for value in far_line]

    far_rows = n_narrow * n_pair * sum(slots)
    pass_rows = far_rows if far_rows <= MAX_ROWS else sum(slots)
    pass_rows = near_rows + -(-pass_rows // 16) * 16
    outs = call(
        functools.partial(routed_kernel, n_narrow, n_pair, per),
        "routed",
        far_all + list(near_mid) + routed,
        [VSPEC] * (n_narrow * n_pair * per + 6),
        [block(n_narrow, slots[0])] * n_pair
        + [block(n_narrow, sum(slots[1:]) + tokens)] * n_pair,
        [VMEM((pass_rows * tall, LANES), F32), VMEM((pass_rows, features), BF16)],
        flops=6 * (near_rows + far_rows) * features * hidden,
        moved=6 * features * hidden,
        limit=limit,
    )
    def reduce_pair(parts, pieces):
        outs = call(
            functools.partial(pair_sum_kernel, n_pair, n_narrow),
            "pair_sum",
            [parts[0]] + [swap(parts[c], "pair", c) for c in range(1, n_pair)],
            [VSPEC] * n_pair,
            [block(rows) for rows in pieces for _ in range(n_narrow)],
            [],
            limit=limit,
        )
        return [outs[i : i + n_narrow] for i in range(0, len(outs), n_narrow)]

    def send_narrow(parts):
        return [parts[0]] + [swap(parts[j], "narrow", j) for j in range(1, n_narrow)]

    reduced = reduce_pair(outs[:n_pair], slots[:1])
    reduced += reduce_pair(outs[n_pair:], slots[1:] + [tokens])
    sums = []
    for k in range(per):
        sums += call(
            functools.partial(narrow_sum_kernel, n_narrow),
            "narrow_sum",
            send_narrow(reduced[k]),
            [VSPEC] * n_narrow,
            [block(CAP)] * (slots[k] // CAP),
            [],
            limit=limit,
        )
    order.append(1)
    far_back = [swap(value, "wide", k) for k, value in zip(order, sums)]
    near_back = send_narrow(reduced[per])
    far_sum = call(
        functools.partial(far_combine_kernel, order),
        "far_combine",
        [route, gains] + far_back,
        [SSPEC] * 2 + [VSPEC] * len(order),
        jax.ShapeDtypeStruct((tokens, tall, LANES), F32),
        [VMEM((n_wide * CAP, tall, LANES), F32)],
    )
    return call(
        combine_kernel,
        "combine",
        [far_sum] + near_back,
        [VSPEC] * (1 + n_narrow),
        jax.ShapeDtypeStruct((tokens, features), BF16),
        [VMEM((tokens * tall, LANES), F32)],
    )


def solution(mesh):
    rows = P(("groups", "wide", "narrow", "pair"), None)
    return jax.shard_map(
        shards,
        mesh=mesh,
        in_specs=(
            rows,
            rows,
            rows,
            rows,
            P(),
            P("wide", None, ("narrow", "pair")),
            P("wide", None, ("narrow", "pair")),
            P("wide", ("narrow", "pair"), None),
            P(None, ("narrow", "pair")),
            P(None, ("narrow", "pair")),
            P(("narrow", "pair"), None),
        ),
        out_specs=rows,
        check_vma=False,
    )
```

```python
import functools

import jax
import jax.numpy as jnp
from jax import lax
from jax.experimental import pallas as pl
from jax.experimental.pallas import tpu as pltpu
from jax.sharding import PartitionSpec as P

CAP = 5
LANES = 128
SPAN = 7
MAX_ROWS = 128

VMEM = pltpu.VMEM
VSPEC = pl.BlockSpec(memory_space=pltpu.VMEM)
SSPEC = pl.BlockSpec(memory_space=pltpu.SMEM)
ASPEC = pl.BlockSpec(memory_space=pl.ANY)
F32 = jnp.float32
BF16 = jnp.bfloat16


def put(flat, at, value, tall):
    rows = value.shape[0]
    for b in range(value.shape[1] // LANES):
        flat[pl.ds(at // LANES + b, rows, stride=tall), :] = value[
            :, b * LANES : (b + 1) * LANES
        ]


def dispatch_kernel(ids_in, place_in, weights_in, codes_in, scales_in, *refs):
    refs = refs[6:]
    near, far = refs[0], refs[1:-10]
    route, gains = refs[-10:-8]
    ids, place, weights, codes, scales, tok, stage, sems = refs[-8:]
    copies = [
        pltpu.make_async_copy(src, dst, sems.at[i])
        for i, (src, dst) in enumerate(
            (
                (codes_in, codes),
                (scales_in, scales),
                (ids_in, ids),
                (place_in, place),
                (weights_in, weights),
            )
        )
    ]
    for copy in copies:
        copy.start()
    here = lax.axis_index("wide")
    rows, features = codes.shape
    topk = ids.shape[0]
    tall = features // LANES
    stage[...] = jnp.zeros_like(stage)
    for copy in copies:
        copy.wait()
    for b in range(tall):
        block = codes[:, b * LANES : (b + 1) * LANES].astype(F32)
        tok[pl.ds(b, rows, stride=tall), :] = block * scales[:, b : b + 1].astype(F32)
    near[:rows] = tok[...].reshape(rows, tall, LANES).astype(BF16)
    sub = lax.broadcasted_iota(jnp.int32, (rows, LANES), 0)
    lane = lax.broadcasted_iota(jnp.int32, (rows, LANES), 1)
    weight = jnp.zeros((rows, LANES), F32)
    named = []
    for t in range(rows):
        for k in range(topk):
            e = ids[k, t]
            node = place[e]
            slot = jnp.int32(0)
            for other in named[: t * topk]:
                slot = slot + jnp.where(other == e, 1, 0)
            named.append(e)
            at = (node ^ here) * CAP + slot
            route[k, t] = at
            gains[k, t] = weights[k, t]
            weight = jnp.where((sub == t) & (lane == node), weights[k, t], weight)
            stage[at] = tok[t * tall : (t + 1) * tall, :]
    high = weight.astype(BF16).astype(F32)
    middle = (weight - high).astype(BF16).astype(F32)
    low = weight - high - middle
    near[rows] = jnp.concatenate(
        [high, middle, low, jnp.zeros((tall - 3 * rows, LANES), F32)], axis=0
    ).astype(BF16)
    for k, ref in enumerate(far):
        ref[...] = stage[(k + 1) * CAP : (k + 2) * CAP].astype(BF16)


def unpack(refs, blocks, rows, flat, inputs, first=0):
    tall = inputs.shape[1] // LANES
    at = 0
    for ref, count in zip(refs, blocks):
        flat[at * tall : (at + count) * tall, :] = (
            ref[:count].astype(F32).reshape(count * tall, LANES)
        )
        at += count
    if at < rows:
        flat[at * tall : rows * tall, :] = jnp.zeros(((rows - at) * tall, LANES), F32)
    for b in range(tall):
        inputs[first : first + rows, b * LANES : (b + 1) * LANES] = flat[
            pl.ds(b, rows, stride=tall), :
        ].astype(BF16)


def silu_mul(gate, up):
    return (gate / (1.0 + jnp.exp(-gate)) * up).astype(BF16)


def near_shared_kernel(*refs):
    count = len(refs) - 7
    arrived, (gate_w, up_w, down_w), outs = refs[:count], refs[count : count + 3], refs[-4:]
    inputs, weight, value, flat = outs
    here = lax.axis_index("wide")
    tokens, tall = arrived[0].shape[0] - 1, arrived[0].shape[1]
    rows = count * tokens
    unpack(arrived, [tokens] * count, rows, flat, inputs)
    for i, ref in enumerate(arrived):
        parts = ref[tokens].astype(F32)
        whole = (
            parts[:tokens] + parts[tokens : 2 * tokens] + parts[2 * tokens : 3 * tokens]
        )
        lane = lax.broadcasted_iota(jnp.int32, whole.shape, 1)
        gain = jnp.sum(jnp.where(lane == here, whole, 0.0), axis=1, keepdims=True)
        weight[i * tokens : (i + 1) * tokens, :] = jnp.broadcast_to(gain, whole.shape)
    x = inputs[...]
    gate = jnp.dot(x, gate_w[...], preferred_element_type=F32)
    up = jnp.dot(x, up_w[...], preferred_element_type=F32)
    hidden = silu_mul(gate, up)
    for first in range(0, tall * LANES, SPAN * LANES):
        at = slice(first, first + SPAN * LANES)
        value[:, at] = jnp.dot(hidden, down_w[:, at], preferred_element_type=F32)


def routed_kernel(n_narrow, n_pair, per, *refs):
    count = n_narrow * n_pair * per
    arrived, rest = refs[:count], refs[count:]
    near, weight, value, gate_w, up_w, down_w = rest[:6]
    first_outs, outs = rest[6 : 6 + n_pair], rest[6 + n_pair : -2]
    flat, inputs = rest[-2:]
    tall = arrived[0].shape[1]
    near_rows = near.shape[0]
    each = near_rows // n_pair
    blocks = [ref.shape[0] for ref in arrived]
    step = count if sum(blocks) <= MAX_ROWS else per
    for first in range(0, count, step):
        group = blocks[first : first + step]
        head = 0 if first else near_rows
        rows = -(-sum(group) // 16) * 16
        unpack(arrived[first : first + step], group, rows, flat, inputs, head)
        if head:
            inputs[:head] = near[...]
        x = inputs[: head + rows]
        gate = jnp.dot(x, gate_w[...], preferred_element_type=F32)
        up = jnp.dot(x, up_w[...], preferred_element_type=F32)
        hidden = silu_mul(gate, up)
        for at in range(0, tall * LANES, SPAN * LANES):
            part = jnp.dot(
                hidden, down_w[:, at : at + SPAN * LANES], preferred_element_type=F32
            )
            if head:
                part = jnp.concatenate(
                    [
                        value[:, at : at + SPAN * LANES] + weight[:, :1] * part[:head],
                        part[head:],
                    ],
                    axis=0,
                )
            put(flat, at, part, tall)
        if head:
            for c in range(n_pair):
                part = flat[c * each * tall : (c + 1) * each * tall, :]
                part = part.reshape(n_narrow, each // n_narrow, tall, LANES)
                outs[c][:, outs[c].shape[1] - part.shape[1] :] = part.astype(BF16)
        at = head
        for i, slots in enumerate(group):
            line, k = divmod(first + i, per)
            c, j = divmod(line, n_narrow)
            part = flat[at * tall : (at + slots) * tall, :]
            part = part.reshape(slots, tall, LANES).astype(BF16)
            if k == 0:
                first_outs[c][j] = part
            else:
                start = sum(blocks[1:k])
                outs[c][j, start : start + slots] = part
            at += slots


def pair_sum_kernel(n_pair, n_narrow, *refs):
    parts, outs = refs[:n_pair], refs[n_pair:]
    at = 0
    for first in range(0, len(outs), n_narrow):
        rows = slice(at, at + outs[first].shape[0])
        for j in range(n_narrow):
            total = parts[0][j, rows].astype(F32)
            for ref in parts[1:]:
                total = total + ref[j, rows].astype(F32)
            outs[first + j][...] = total.astype(BF16)
        at = rows.stop


def narrow_sum_kernel(n_narrow, *refs):
    parts, outs = refs[:n_narrow], refs[n_narrow:]
    at = 0
    for out in outs:
        rows = slice(at, at + out.shape[0])
        total = parts[0][rows].astype(F32)
        for ref in parts[1:]:
            total = total + ref[rows].astype(F32)
        out[...] = total.astype(BF16)
        at += out.shape[0]


def far_combine_kernel(order, route, gains, *refs):
    far, (total, stage) = refs[: len(order)], refs[-2:]
    topk, rows = route.shape
    tall = stage.shape[1]
    stage[:CAP] = jnp.zeros((CAP, tall, LANES), F32)
    for k, ref in zip(order, far):
        stage[k * CAP : (k + 1) * CAP] = ref[...].astype(F32)
    for t in range(rows):
        value = gains[0, t] * stage[route[0, t]]
        for k in range(1, topk):
            value = value + gains[k, t] * stage[route[k, t]]
        total[t] = value


def combine_kernel(far, *refs):
    near, (out, total) = refs[:-2], refs[-2:]
    rows, features = out.shape
    tall = features // LANES
    for t in range(rows):
        value = far[t]
        for ref in near:
            value = value + ref[t].astype(F32)
        total[t * tall : (t + 1) * tall, :] = value
    for b in range(tall):
        out[:, b * LANES : (b + 1) * LANES] = total[
            pl.ds(b, rows, stride=tall), :
        ].astype(BF16)


def swap(value, axis, offset):
    size = lax.axis_size(axis)
    return lax.ppermute(value, axis, [(i, i ^ offset) for i in range(size)])


def in_hbm(*values):
    return [pltpu.with_memory_space_constraint(value, pltpu.HBM) for value in values]


def after(values, *others):
    return list(lax.optimization_barrier((tuple(values), others))[0])


def call(kernel, name, ins, specs, outs, scratch, flops=0, moved=0, limit=16):
    return pl.pallas_call(
        kernel,
        out_shape=outs,
        in_specs=specs,
        out_specs=jax.tree.map(
            lambda out: SSPEC if getattr(out, "memory_space", None) == pltpu.SMEM else VSPEC,
            outs,
        ),
        scratch_shapes=scratch,
        compiler_params=pltpu.CompilerParams(vmem_limit_bytes=limit << 20),
        cost_estimate=pl.CostEstimate(flops=flops, bytes_accessed=moved, transcendentals=0),
        name=name,
    )(*ins)


def shards(
    row_codes,
    row_scales,
    expert_ids,
    gate_weights,
    placement,
    w_gate,
    w_up,
    w_down,
    shared_gate,
    shared_up,
    shared_down,
):
    n_wide = lax.axis_size("wide")
    n_narrow = lax.axis_size("narrow")
    n_pair = lax.axis_size("pair")
    tokens, features = row_codes.shape
    hidden = w_gate.shape[2]
    tall = features // LANES
    topk = expert_ids.shape[1]
    limit = 16 if n_wide <= 4 else 48

    def block(*lead):
        return jax.ShapeDtypeStruct(lead + (tall, LANES), BF16)

    shared = [shared_gate, shared_up, shared_down]
    routed = [
        w_gate.reshape(features, hidden),
        w_up.reshape(features, hidden),
        w_down.reshape(hidden, features),
    ]
    near, *far = call(
        dispatch_kernel,
        "dispatch",
        in_hbm(expert_ids.T, placement, gate_weights.T, row_codes, row_scales)
        + in_hbm(*shared, *routed),
        [ASPEC] * 11,
        [block(tokens + 1)]
        + [block(CAP)] * (n_wide - 1)
        + [pltpu.SMEM((topk, tokens), jnp.int32), pltpu.SMEM((topk, tokens), F32)],
        [
            pltpu.SMEM((topk, tokens), jnp.int32),
            pltpu.SMEM(placement.shape, jnp.int32),
            pltpu.SMEM((topk, tokens), F32),
            VMEM((tokens, features), BF16),
            VMEM(row_scales.shape, BF16),
            VMEM((tokens * tall, LANES), F32),
            VMEM((n_wide * CAP, tall, LANES), F32),
            pltpu.SemaphoreType.DMA((5,)),
        ],
    )
    far, (route, gains) = far[:-2], far[-2:]
    order = list(range(n_wide - 1, 1, -1))
    across = ("wide", "narrow")
    bundles = [swap(far[k - 1], "wide", k) for k in order]
    direct = [swap(far[0], across, n_narrow + j) for j in range(n_narrow)]
    near_line = [near] + [swap(near, "narrow", j) for j in range(1, n_narrow)]
    bundles = after(bundles, *direct)
    if n_wide > 4:
        bundles = [jnp.concatenate(bundles, axis=0)]
    lines = [list(bundles)]
    for j in range(1, n_narrow):
        lines.append([swap(value, "narrow", j) for value in bundles])
    per = len(bundles) + 1
    slots = [value.shape[0] for value in bundles] + [CAP]
    near_line = after(near_line, *bundles)
    near_all = list(near_line)
    for c in range(1, n_pair):
        near_all += [swap(value, "pair", c) for value in near_line]

    near_rows = n_narrow * n_pair * tokens
    near_mid = call(
        near_shared_kernel,
        "near_shared",
        near_all + shared,
        [VSPEC] * (n_narrow * n_pair + 3),
        [
            jax.ShapeDtypeStruct((near_rows, features), BF16),
            jax.ShapeDtypeStruct((near_rows, LANES), F32),
            jax.ShapeDtypeStruct((near_rows, features), F32),
        ],
        [VMEM((near_rows * tall, LANES), F32)],
        flops=6 * near_rows * features * hidden,
        moved=6 * features * hidden,
        limit=limit,
    )
    side = after([value for line in lines[1:] for value in line], near_mid[1])
    far_line = []
    for j in range(n_narrow):
        far_line += lines[0] if j == 0 else side[(j - 1) * (per - 1) : j * (per - 1)]
        far_line.append(direct[j])
    far_all = list(far_line)
    for c in range(1, n_pair):
        far_all += [swap(value, "pair", c) for value in far_line]

    far_rows = n_narrow * n_pair * sum(slots)
    pass_rows = far_rows if far_rows <= MAX_ROWS else sum(slots)
    pass_rows = near_rows + -(-pass_rows // 16) * 16
    outs = call(
        functools.partial(routed_kernel, n_narrow, n_pair, per),
        "routed",
        far_all + list(near_mid) + routed,
        [VSPEC] * (n_narrow * n_pair * per + 6),
        [block(n_narrow, slots[0])] * n_pair
        + [block(n_narrow, sum(slots[1:]) + tokens)] * n_pair,
        [VMEM((pass_rows * tall, LANES), F32), VMEM((pass_rows, features), BF16)],
        flops=6 * (near_rows + far_rows) * features * hidden,
        moved=6 * features * hidden,
        limit=limit,
    )
    def reduce_pair(parts, pieces):
        outs = call(
            functools.partial(pair_sum_kernel, n_pair, n_narrow),
            "pair_sum",
            [parts[0]] + [swap(parts[c], "pair", c) for c in range(1, n_pair)],
            [VSPEC] * n_pair,
            [block(rows) for rows in pieces for _ in range(n_narrow)],
            [],
            limit=limit,
        )
        return [outs[i : i + n_narrow] for i in range(0, len(outs), n_narrow)]

    def send_narrow(parts):
        return [parts[0]] + [swap(parts[j], "narrow", j) for j in range(1, n_narrow)]

    reduced = reduce_pair(outs[:n_pair], slots[:1])
    later = list(outs[n_pair : n_pair + 1]) + after(outs[n_pair + 1 :], reduced[0][0])
    reduced += reduce_pair(later, slots[1:] + [tokens])
    sums = []
    for k in range(per):
        sums += call(
            functools.partial(narrow_sum_kernel, n_narrow),
            "narrow_sum",
            send_narrow(reduced[k]),
            [VSPEC] * n_narrow,
            [block(CAP)] * (slots[k] // CAP),
            [],
            limit=limit,
        )
    order.append(1)
    far_back = [swap(value, "wide", k) for k, value in zip(order, sums)]
    near_back = send_narrow(reduced[per])
    far_sum = call(
        functools.partial(far_combine_kernel, order),
        "far_combine",
        [route, gains] + far_back,
        [SSPEC] * 2 + [VSPEC] * len(order),
        jax.ShapeDtypeStruct((tokens, tall, LANES), F32),
        [VMEM((n_wide * CAP, tall, LANES), F32)],
    )
    return call(
        combine_kernel,
        "combine",
        [far_sum] + near_back,
        [VSPEC] * (1 + n_narrow),
        jax.ShapeDtypeStruct((tokens, features), BF16),
        [VMEM((tokens * tall, LANES), F32)],
    )


def solution(mesh):
    rows = P(("groups", "wide", "narrow", "pair"), None)
    return jax.shard_map(
        shards,
        mesh=mesh,
        in_specs=(
            rows,
            rows,
            rows,
            rows,
            P(),
            P("wide", None, ("narrow", "pair")),
            P("wide", None, ("narrow", "pair")),
            P("wide", ("narrow", "pair"), None),
            P(None, ("narrow", "pair")),
            P(None, ("narrow", "pair")),
            P(("narrow", "pair"), None),
        ),
        out_specs=rows,
        check_vma=False,
    )
```
